32 devices in a mesh: star: 8 (over y, x, core), gas: 4 (over z).
Axes of the slice: x: 2, y: 2, z: 4, core: 2. Of those that a mesh axis runs over, the one named last changes fastest.
Arguments:
- star_pos: float32 [3, 16384], P(None, ('star', 'gas')), may hold values from 0 to 32
- star_vel: float32 [3, 16384], P(None, ('star', 'gas')), may hold values from -6 to 6
- star_accel: float32 [6, 16384], P(None, ('star', 'gas')), may hold values from -6 to 6
- star_mass: float32 [16384], P(('star', 'gas')), may hold values from 0.1 to 2
- active: int32 [256], replicated, may hold values from 0 to 16383, as said below
- density: float32 [32, 32, 64], P('star', 'gas'), may hold values from 0.5 to 4
- flow_in: float32 [3, 32, 32, 64], P(None, 'star', 'gas'), may hold values from -2 to 2
- field_in: float32 [3, 32, 32, 64], P(None, 'star', 'gas'), may hold values from -4 to 4
Outputs:
- star_new: float32 [12, 16384], P(None, ('star', 'gas'))
- flow: float32 [3, 32, 32, 64], P(None, 'star', 'gas')
- field_out: float32 [3, 32, 32, 64], P(None, 'star', 'gas')
The draws below stay inside these ranges and needn't reach their ends.
Inputs may be any that keep to these rules, and one draw needn't show every extreme that they name: Distinct and increasing; among the 512 consecutive indices of one device at most 24 are active, and in every draw some device holds exactly 24.
All inputs are finite; a program needn't handle non-finite values.
Results may differ from the reference program's by a relative error of at most 0.0001.
Values sent between devices are 32-bit elements; how exact they have to be, the bound alone decides.
No kernel may reach another device: no remote copies, remote signals or barrier semaphores. Data moves between devices by JAX's collectives and lax.ppermute only.
A program may use at most 64 MiB of HBM per device.

```python
import math
import jax
import jax.numpy as jnp
from jax import lax

STAR_DEV = 512
ACT_DEV = 8
STARS = 16384
ACTIVE = 256
NX = 32
NY = 32
NZ = 64


def draw_active(key, part):
    owners = STARS // STAR_DEV
    groups = owners // 4
    key_a, key_b, key_c, key_d = jax.random.split(jax.random.fold_in(key, 17), 4)
    shift_one = jax.random.randint(key_a, (groups,), 0, ACT_DEV + 1)
    shift_two = jax.random.randint(key_b, (groups,), 0, ACT_DEV // 2 + 1)
    shift_two = jnp.where(jnp.arange(groups) == 0, 0, shift_two)
    pattern = jnp.stack([3 * ACT_DEV - shift_two, shift_one, ACT_DEV - shift_one, shift_two], 1).reshape(-1)
    order = jax.random.permutation(key_c, owners)
    counts_at = pattern[order].astype(jnp.int32)
    owner_keys = jax.random.split(key_d, owners)
    ranks = jax.vmap(lambda one_key: jax.random.permutation(one_key, STAR_DEV))(owner_keys)
    chosen = (ranks < counts_at[:, None]).reshape(-1)
    return jnp.nonzero(chosen, size=ACTIVE, fill_value=0)[0].astype(jnp.int32)


def steps_of(stream_key, dims, cuts, low, top_value):
    factor_of = 1.0
    for axis_at, parts in cuts:
        heights = jax.random.uniform(jax.random.fold_in(jax.random.fold_in(stream_key, 6), axis_at), (parts,), jnp.float32, low / len(cuts), top_value / len(cuts))
        factor_of = factor_of * jnp.repeat(jnp.exp(heights), dims[axis_at] // parts).reshape((-1,) + (1,) * (len(dims) - 1 - axis_at))
    return factor_of


def gaussian(own_key, shape, width, limit, shards=(), held_as=jnp.bfloat16):
    gain = steps_of(own_key, shape, shards, -0.22, 0.18) if shards else 1.0
    entries = jax.random.normal(own_key, shape, jnp.float32) * width * gain
    return jnp.minimum(jnp.maximum(entries, -limit), limit).astype(held_as)


def setup_inputs(seed: int = 0) -> dict:
    key_of = jax.random.split(jax.random.key(seed), 9)
    star_pos = jnp.clip(32.0 * jax.random.uniform(key_of[0], (3, STARS), jnp.float32) ** steps_of(key_of[0], (3, STARS), ((1, 32),), -0.2, 0.2), 0.0, 32.0)
    star_vel = gaussian(key_of[1], (3, STARS), 1.0, 6.0, ((1, 32),), jnp.float32)
    star_accel = gaussian(key_of[2], (6, STARS), 1.0, 6.0, ((1, 32),), jnp.float32)
    star_mass = jnp.clip(jnp.exp(math.log(2.0) - 2.9957323 * jax.random.uniform(key_of[3], (STARS,), jnp.float32) ** steps_of(key_of[3], (STARS,), ((0, 32),), -0.2, 0.2)), 0.1, 2.0)
    active = draw_active(jax.random.fold_in(key_of[8], 71), 0)
    density = jnp.clip(jnp.exp(math.log(4.0) - 2.0794415 * jax.random.uniform(key_of[5], (NX, NY, NZ), jnp.float32) ** steps_of(key_of[5], (NX, NY, NZ), ((0, 8), (1, 4)), -0.2, 0.2)), 0.5, 4.0)
    flow_in = gaussian(key_of[6], (3, NX, NY, NZ), 0.3, 2.0, ((1, 8), (2, 4)), jnp.float32)
    field_in = gaussian(key_of[7], (3, NX, NY, NZ), 0.7, 4.0, ((1, 8), (2, 4)), jnp.float32)
    return {"star_pos": star_pos, "star_vel": star_vel, "star_accel": star_accel, "star_mass": star_mass, "active": active, "density": density, "flow_in": flow_in, "field_in": field_in}


gravity = 0.02
soften = 4.0
time_step = 1.5
field_step = 0.1

def grad_x(values):
    return 0.5 * (values[2:, 1:-1] - values[:-2, 1:-1])

def grad_y(values):
    return 0.5 * (values[1:-1, 2:] - values[1:-1, :-2])

def grad_z(values):
    return 0.5 * (jnp.roll(values, -1, 2) - jnp.roll(values, 1, 2))[1:-1, 1:-1]

def trim_rim(values):
    return values[1:-1, 1:-1]

def curl_of(comp_a, comp_b, comp_c):
    return (grad_y(comp_c) - grad_z(comp_b), grad_z(comp_a) - grad_x(comp_c), grad_x(comp_b) - grad_y(comp_a))

def cross_of(lhs_vec, rhs_vec):
    return (lhs_vec[1] * rhs_vec[2] - lhs_vec[2] * rhs_vec[1], lhs_vec[2] * rhs_vec[0] - lhs_vec[0] * rhs_vec[2], lhs_vec[0] * rhs_vec[1] - lhs_vec[1] * rhs_vec[0])

def field_rate(padded_field, padded_flow, padded_density):
    current = curl_of(padded_field[0], padded_field[1], padded_field[2])
    inner_field = (trim_rim(padded_field[0]), trim_rim(padded_field[1]), trim_rim(padded_field[2]))
    inner_flow = (trim_rim(padded_flow[0]), trim_rim(padded_flow[1]), trim_rim(padded_flow[2]))
    resist = trim_rim(padded_density) ** (-1.5)
    lorentz = cross_of(current, inner_field)
    drift = cross_of(lorentz, inner_field)
    motion = cross_of(inner_flow, inner_field)
    emf_a = motion[0] + resist * drift[0]
    emf_b = motion[1] + resist * drift[1]
    emf_c = motion[2] + resist * drift[2]
    return jnp.stack(curl_of(emf_a, emf_b, emf_c))

def wrap_pad(values):
    widths = ((0, 0),) * (values.ndim - 3) + ((2, 2), (2, 2), (0, 0))
    return jnp.pad(values, widths, mode='wrap')

def star_terms(target, resident):
    star_gap = resident[0:3, None, :] - target[0:3, :, None]
    rel_vel = resident[3:6, None, :] - target[3:6, :, None]
    inv_r = lax.rsqrt(lax.optimization_barrier(jnp.sum(star_gap * star_gap, 0)) + soften)
    weight = gravity * resident[6][None, :] * inv_r * inv_r * inv_r
    star_acc = lax.optimization_barrier(jnp.sum(weight[None] * star_gap, 2))
    approach = lax.optimization_barrier(jnp.sum(star_gap * rel_vel, 0))
    star_jerk = lax.optimization_barrier(jnp.sum(weight[None] * (rel_vel - 3.0 * (approach * inv_r * inv_r)[None] * star_gap), 2))
    return jnp.concatenate([star_acc, star_jerk], 0)

def gas_terms(target, cell_place, cell_mass):
    cell_gap = cell_place[:, None, :] - target[0:3, :, None]
    inv_g = lax.rsqrt(lax.optimization_barrier(jnp.sum(cell_gap * cell_gap, 0)) + soften)
    inv_cube = gravity * inv_g * inv_g * inv_g
    gas_acc = lax.optimization_barrier(jnp.sum((inv_cube * cell_mass[None, :])[None] * cell_gap, 2))
    cell_kick = -lax.optimization_barrier(jnp.sum((inv_cube * target[6][:, None])[None] * cell_gap, 1))
    return (gas_acc, cell_kick)

def reference(star_pos, star_vel, star_accel, star_mass, active, density, flow_in, field_in):
    old_acc = star_accel[0:3]
    old_jerk = star_accel[3:6]
    pred_pos = star_pos + time_step * star_vel + time_step ** 2 / 2.0 * old_acc + time_step ** 3 / 6.0 * old_jerk
    pred_vel = star_vel + time_step * old_acc + time_step ** 2 / 2.0 * old_jerk
    resident = jnp.concatenate([pred_pos, pred_vel, star_mass[None]], 0)
    targets = jnp.take(resident, active, axis=1)
    star_blocks = targets.reshape(7, ACTIVE // 64, 64).transpose(1, 0, 2)
    star_part = lax.map(lambda target_block: star_terms(target_block, resident), star_blocks)
    star_part = star_part.transpose(1, 0, 2).reshape(6, ACTIVE)
    grid_shape = (NX, NY, NZ)
    coord_x = jnp.arange(NX).astype(jnp.float32) + 0.5
    coord_y = jnp.arange(NY).astype(jnp.float32) + 0.5
    coord_z = jnp.arange(NZ).astype(jnp.float32) + 0.5
    cell_place = jnp.stack([jnp.broadcast_to(coord_x[:, None, None], grid_shape), jnp.broadcast_to(coord_y[None, :, None], grid_shape), jnp.broadcast_to(coord_z[None, None, :], grid_shape)]).reshape(3, -1)
    cell_mass = density.reshape(-1)
    gas_blocks = targets.reshape(7, ACTIVE // 16, 16).transpose(1, 0, 2)

    def one_block(running, target_block):
        gas_acc, cell_kick = gas_terms(target_block, cell_place, cell_mass)
        return (running + cell_kick, gas_acc)
    kick_sum, gas_part = lax.scan(one_block, jnp.zeros(cell_place.shape, jnp.float32), gas_blocks)
    gas_part = gas_part.transpose(1, 0, 2).reshape(3, ACTIVE)
    new_acc = star_part[0:3] + gas_part
    new_jerk = star_part[3:6]
    acc_zero = jnp.take(old_acc, active, axis=1)
    jerk_zero = jnp.take(old_jerk, active, axis=1)
    vel_zero = jnp.take(star_vel, active, axis=1)
    pos_zero = jnp.take(star_pos, active, axis=1)
    vel_one = vel_zero + time_step * (acc_zero + new_acc) / 2.0 + time_step ** 2 * (jerk_zero - new_jerk) / 12.0
    pos_one = pos_zero + time_step * (vel_zero + vel_one) / 2.0 + time_step ** 2 * (acc_zero - new_acc) / 12.0
    updated = jnp.concatenate([pos_one, vel_one, new_acc, new_jerk], 0)
    base = jnp.concatenate([star_pos, star_vel, star_accel], 0)
    star_new = base.at[:, active].set(updated)
    flow = flow_in + time_step * kick_sum.reshape(3, NX, NY, NZ)
    padded_flow = wrap_pad(flow)
    padded_density = wrap_pad(density)
    first_section = field_in + field_step * field_rate(wrap_pad(field_in), padded_flow, padded_density)
    field_out = 0.5 * (field_in + first_section + field_step * field_rate(wrap_pad(first_section), padded_flow, padded_density))
    return (star_new, flow, field_out)
```

```python
import jax
import jax.numpy as jnp
from jax import lax
from jax.sharding import PartitionSpec as P

gravity = 0.02
soften = 4.0
time_step = 1.5
field_step = 0.1
highest = lax.Precision.HIGHEST
both = ("star", "gas")
reach = 4


def grad_x(values):
    return 0.5 * (values[2:, 1:-1] - values[:-2, 1:-1])


def grad_y(values):
    return 0.5 * (values[1:-1, 2:] - values[1:-1, :-2])


def grad_z(values):
    return 0.5 * (jnp.roll(values, -1, 2) - jnp.roll(values, 1, 2))[1:-1, 1:-1]


def trim_rim(values, width=1):
    return values[..., width:-width, width:-width, :]


def curl_of(comp_a, comp_b, comp_c):
    return (
        grad_y(comp_c) - grad_z(comp_b),
        grad_z(comp_a) - grad_x(comp_c),
        grad_x(comp_b) - grad_y(comp_a),
    )


def cross_of(lhs_vec, rhs_vec):
    return (
        lhs_vec[1] * rhs_vec[2] - lhs_vec[2] * rhs_vec[1],
        lhs_vec[2] * rhs_vec[0] - lhs_vec[0] * rhs_vec[2],
        lhs_vec[0] * rhs_vec[1] - lhs_vec[1] * rhs_vec[0],
    )


def field_rate(padded_field, inner_flow, inner_resist):
    current = curl_of(padded_field[0], padded_field[1], padded_field[2])
    inner_field = trim_rim(padded_field)
    drift = cross_of(cross_of(current, inner_field), inner_field)
    motion = cross_of(inner_flow, inner_field)
    emf = [motion[k] + inner_resist * drift[k] for k in range(3)]
    return jnp.stack(curl_of(*emf))


def pair_halo(block, axis, dim):
    count = lax.axis_size(axis)
    even = lax.axis_index(axis) % 2 == 0
    low = lax.slice_in_dim(block, 0, reach, axis=dim)
    high = lax.slice_in_dim(block, block.shape[dim] - reach, None, axis=dim)
    near = [(i, i ^ 1) for i in range(count)]
    far = [(i, (i + (1 if i % 2 else -1)) % count) for i in range(count)]
    from_far = lax.ppermute(jnp.where(even, low, high), axis, far)
    from_near = lax.ppermute(jnp.where(even, high, low), axis, near)
    below = jnp.where(even, from_far, from_near)
    above = jnp.where(even, from_near, from_far)
    return jnp.concatenate([below, block, above], axis=dim)


def pair_terms(target, resident, cell_place, cell_mass):
    star_gap = resident[0:3, None, :] - target[0:3, :, None]
    rel_vel = resident[3:6, None, :] - target[3:6, :, None]
    inv_r = lax.rsqrt(jnp.sum(star_gap * star_gap, 0) + soften)
    weight = gravity * resident[6][None, :] * inv_r * inv_r * inv_r
    star_acc = jnp.sum(weight[None] * star_gap, 2)
    approach = jnp.sum(star_gap * rel_vel, 0)
    star_jerk = jnp.sum(
        weight[None] * (rel_vel - 3.0 * (approach * inv_r * inv_r)[None] * star_gap), 2
    )
    cell_gap = cell_place[:, None, :] - target[0:3, :, None]
    inv_g = lax.rsqrt(jnp.sum(cell_gap * cell_gap, 0) + soften)
    inv_cube = gravity * inv_g * inv_g * inv_g
    gas_acc = jnp.sum((inv_cube * cell_mass[None, :])[None] * cell_gap, 2)
    return jnp.concatenate([star_acc + gas_acc, star_jerk], 0)


def kick_terms(target, cell_place):
    cell_gap = target[0:3, :, None] - cell_place[:, None, :]
    inv_g = lax.rsqrt(jnp.sum(cell_gap * cell_gap, 0) + soften)
    weight = gravity * inv_g * inv_g * inv_g * target[6][:, None]
    return jnp.sum(weight[None] * cell_gap, 1)


def in_blocks(targets, width):
    count = targets.shape[1] // width
    return targets.reshape(targets.shape[0], count, width).transpose(1, 0, 2)


def cells_at(first_x, count_x, total_x, first_y, count_y, total_y, count_z):
    shape = (count_x, count_y, count_z)
    place_x = ((first_x + jnp.arange(count_x)) % total_x).astype(jnp.float32) + 0.5
    place_y = ((first_y + jnp.arange(count_y)) % total_y).astype(jnp.float32) + 0.5
    place_z = jnp.arange(count_z).astype(jnp.float32) + 0.5
    return jnp.stack(
        [
            jnp.broadcast_to(place_x[:, None, None], shape),
            jnp.broadcast_to(place_y[None, :, None], shape),
            jnp.broadcast_to(place_z[None, None, :], shape),
        ]
    ).reshape(3, -1)


def body(star_pos, star_vel, star_accel, star_mass, active, density, flow_in, field_in):
    resident_total = star_pos.shape[1]
    listed = active.shape[0]
    star_count, gas_count = lax.axis_size("star"), lax.axis_size("gas")
    devices = star_count * gas_count
    slots = 4 * (listed // devices)
    ext_x, ext_y, ext_z = density.shape
    my_star, my_gas = lax.axis_index("star"), lax.axis_index("gas")
    base_row = (my_star * gas_count + my_gas) * resident_total
    old_acc = star_accel[0:3]
    old_jerk = star_accel[3:6]
    pred_pos = (
        star_pos
        + time_step * star_vel
        + time_step**2 / 2.0 * old_acc
        + time_step**3 / 6.0 * old_jerk
    )
    pred_vel = star_vel + time_step * old_acc + time_step**2 / 2.0 * old_jerk
    resident = jnp.concatenate([pred_pos, pred_vel, star_mass[None]], 0)

    owner_of = active // resident_total
    device_ids = jnp.arange(devices, dtype=jnp.int32)
    owned_by = (owner_of[None, :] == device_ids[:, None]).astype(jnp.float32)
    first_of = jnp.sum((owner_of[None, :] < device_ids[:, None]).astype(jnp.float32), 1)
    place_of = jnp.arange(listed) - jnp.sum(owned_by * first_of[:, None], 0).astype(jnp.int32)
    slot_hit = (place_of[None, :] == jnp.arange(slots)[:, None]).astype(jnp.float32)
    my_slot = jnp.where(
        owner_of[None, :] * resident_total == base_row, slot_hit, 0.0
    )
    local_row = (active - base_row)[:, None] == jnp.arange(resident_total)[None, :]
    slot_row = jnp.dot(my_slot, local_row.astype(jnp.float32))
    is_active = jnp.sum(slot_row, 0) > 0.5

    own = lax.dot_general(slot_row, resident, (((1,), (1,)), ((), ())), precision=highest)
    own = jnp.pad(own.T, ((0, 1), (0, 0))).reshape(8, slots)
    send = jnp.stack(
        [jnp.concatenate([own[0:3], own[6:7]]).reshape(-1), jnp.concatenate([own[3:6], own[7:8]]).reshape(-1)]
    )
    got = lax.all_to_all(
        jnp.broadcast_to(send[None], (devices,) + send.shape), both, 0, 0, tiled=True
    )
    spread = jnp.einsum("dl,dt->lt", got.reshape(devices, -1), owned_by, precision=highest)
    spread = jnp.sum(spread.reshape(8, slots, listed) * slot_hit[None], 1)
    targets = jnp.concatenate([spread[0:3], spread[4:7], spread[3:4]], 0)

    gas_block = jnp.concatenate([field_in, flow_in, density[None]], 0)
    padded = pair_halo(gas_block, "gas", 2)
    padded = pair_halo(padded, "star", 1)

    grid_x, grid_y = ext_x * star_count, ext_y * gas_count
    cell_place = cells_at(my_star * ext_x, ext_x, grid_x, my_gas * ext_y, ext_y, grid_y, ext_z)
    blocks = in_blocks(targets, min(listed, 128))
    partial = lax.map(
        lambda block: pair_terms(block, resident, cell_place, density.reshape(-1)), blocks
    )
    partial = partial.transpose(1, 0, 2).reshape(6, listed)
    partial = jnp.pad(partial.reshape(2, 3, listed), ((0, 0), (0, 1), (0, 0)))
    to_owner = jnp.einsum(
        "dt,pcst->dpcs", owned_by, partial[:, :, None, :] * slot_hit[None, None], precision=highest
    )
    back = lax.all_to_all(to_owner.reshape(devices, 2, 4 * slots), both, 0, 0, tiled=True)
    own_sum = jnp.sum(back, 0).reshape(2, 4, slots)[:, 0:3].reshape(6, slots)
    own_terms = jnp.dot(own_sum, slot_row, precision=highest)
    new_acc = own_terms[0:3]
    new_jerk = own_terms[3:6]
    vel_one = (
        star_vel
        + time_step * (old_acc + new_acc) / 2.0
        + time_step**2 * (old_jerk - new_jerk) / 12.0
    )
    pos_one = (
        star_pos
        + time_step * (star_vel + vel_one) / 2.0
        + time_step**2 * (old_acc - new_acc) / 12.0
    )
    updated = jnp.concatenate([pos_one, vel_one, new_acc, new_jerk], 0)
    base = jnp.concatenate([star_pos, star_vel, star_accel], 0)
    star_new = jnp.where(is_active[None, :], updated, base)

    rim = reach - 1
    rim_place = cells_at(
        my_star * ext_x - rim + grid_x, ext_x + 2 * rim, grid_x,
        my_gas * ext_y - rim + grid_y, ext_y + 2 * rim, grid_y, ext_z,
    )
    kick, _ = lax.scan(
        lambda total, block: (total + kick_terms(block, rim_place), None),
        jnp.zeros(rim_place.shape, jnp.float32), blocks,
    )
    rim_flow = trim_rim(padded[3:6])
    rim_flow = rim_flow + time_step * kick.reshape(rim_flow.shape)
    rim_resist = trim_rim(padded[6]) ** (-1.5)
    flow = trim_rim(rim_flow, rim)

    wide = padded[0:3]
    section = trim_rim(wide, 2) + field_step * field_rate(wide, rim_flow, rim_resist)
    rate = field_rate(section, trim_rim(rim_flow, 2), trim_rim(rim_resist, 2))
    field_out = 0.5 * (field_in + trim_rim(section, 2) + field_step * rate)
    return (star_new, flow, field_out)


def solution(mesh):
    placed = (
        P(None, both),
        P(None, both),
        P(None, both),
        P(both),
        P(),
        P("star", "gas", None),
        P(None, "star", "gas", None),
        P(None, "star", "gas", None),
    )
    return jax.shard_map(
        body,
        mesh=mesh,
        in_specs=placed,
        out_specs=(
            P(None, both),
            P(None, "star", "gas", None),
            P(None, "star", "gas", None),
        ),
        check_vma=False,
    )
```

```python
import functools

import jax
import jax.numpy as jnp
from jax import lax
from jax.experimental import pallas as pl
from jax.experimental.pallas import tpu as pltpu
from jax.sharding import PartitionSpec as P

gravity = 0.02
soften = 4.0
time_step = 1.5
field_step = 0.1
both = ("star", "gas")
reach = 4
rim = reach - 1
lanes = 128
vmem_bytes = 48 * 1024 * 1024
f32, bf16, i32 = jnp.float32, jnp.bfloat16, jnp.int32


def iota(shape, dim):
    return lax.broadcasted_iota(i32, shape, dim)


def split3(values):
    high = values.astype(bf16)
    rest = values - high.astype(f32)
    mid = rest.astype(bf16)
    low = (rest - mid.astype(f32)).astype(bf16)
    return high, mid, low


def stack3(values):
    return jnp.concatenate(split3(values), 0)


def dot_of(lhs, rhs, lhs_dim=1, rhs_dim=0):
    return lax.dot_general(
        lhs, rhs, (((lhs_dim,), (rhs_dim,)), ((), ())), preferred_element_type=f32
    )


def one_hot(hits):
    return jnp.where(hits, 1.0, 0.0)


def my_rank():
    return lax.axis_index("star") * lax.axis_size("gas") + lax.axis_index("gas")


def call(kernel, outs, *args, grid=None, in_specs=None, out_specs=None, scratch=(), after=0, where=pl.ANY):
    spec = {}
    if grid is not None:
        spec = dict(grid=grid, in_specs=in_specs, out_specs=out_specs)
    elif in_specs is not None:
        spec = dict(in_specs=in_specs)
    elif after:
        held = [pl.BlockSpec(memory_space=pltpu.VMEM)] * (len(args) - after)
        spec = dict(in_specs=held + [pl.BlockSpec(memory_space=where)] * after)
    return pl.pallas_call(
        kernel,
        out_shape=outs,
        scratch_shapes=list(scratch),
        compiler_params=pltpu.CompilerParams(vmem_limit_bytes=vmem_bytes),
        **spec,
    )(*args)


def predict_kernel(*refs):
    sources, held = refs[0:8], refs[8:16]
    send_ref, state_ref, sems = refs[16:]
    copies = [
        pltpu.make_async_copy(source, target, sems.at[k])
        for k, (source, target) in enumerate(zip(sources, held))
    ]
    for copy in copies:
        copy.start()
    for copy in copies:
        copy.wait()
    pos_ref, vel_ref, acc_ref, mass_ref, active_ref = held[0:5]
    total = pos_ref.shape[1]
    listed = active_ref.shape[1]
    slots = lanes // 4
    pos, vel = pos_ref[...], vel_ref[...]
    old_acc, old_jerk = acc_ref[0:3], acc_ref[3:6]
    pred_pos = (
        pos + time_step * vel + time_step**2 / 2.0 * old_acc + time_step**3 / 6.0 * old_jerk
    )
    pred_vel = vel + time_step * old_acc + time_step**2 / 2.0 * old_jerk
    state = jnp.concatenate([pred_pos, mass_ref[...], pred_vel, jnp.zeros((1, total), f32)], 0)
    state_ref[...] = state
    local = active_ref[...] - my_rank() * total
    first = jnp.sum(one_hot(local < 0)).astype(i32)
    hit = one_hot(iota((total, listed), 0) == local).astype(bf16)
    pieces = dot_of(stack3(state), hit)
    placed = pieces[0:8] + pieces[8:16] + pieces[16:24]
    placed = pltpu.roll(placed, lax.rem(listed - first, listed), 1)[:, 0:lanes]
    lane = iota((8, lanes), 1)
    row = iota((8, lanes), 0)
    part = jnp.where(lane < slots, placed, 0.0)
    spread = part
    for k in range(1, 4):
        spread = jnp.where(lane // slots == k, pltpu.roll(part, k * slots, 1), spread)
    spread = jnp.where(row % 4 == lane // slots, spread, 0.0)
    one = jnp.sum(spread[0:4], 0, keepdims=True)
    two = jnp.sum(spread[4:8], 0, keepdims=True)
    send_ref[...] = jnp.broadcast_to(jnp.concatenate([one, two], 0)[None], send_ref.shape)


def pack_kernel(field_ref, flow_ref, density_ref, order_ref, own_ref, near_ref, far_ref, rows_ref):
    comps = [field_ref[0], field_ref[1], field_ref[2], flow_ref[0], flow_ref[1], flow_ref[2]]
    comps = comps + [density_ref[...], density_ref[...]]
    even = lax.axis_index("gas") % 2 == 0
    for k in range(4):
        pair = jnp.concatenate([comps[2 * k], comps[2 * k + 1]], -1)
        own_ref[k] = pair
        low, high = pair[:, :reach], pair[:, -reach:]
        near_ref[k] = jnp.where(even, high, low)
        far_ref[k] = jnp.where(even, low, high)
    half = density_ref.shape[1] // 2
    for k in range(density_ref.shape[0]):
        first = density_ref[k, pl.ds(0, half, stride=2), :]
        second = density_ref[k, pl.ds(1, half, stride=2), :]
        rows_ref[k * half : (k + 1) * half] = jnp.concatenate([first, second], -1)


def join_kernel(own_ref, near_ref, far_ref, order_ref, out_ref):
    even = lax.axis_index("gas") % 2 == 0
    near, far = near_ref[...], far_ref[...]
    below = jnp.where(even, far, near)
    above = jnp.where(even, near, far)
    out_ref[...] = jnp.concatenate([below, own_ref[...], above], 2)


def index_kernel(active_ref, state_ref, density_ref, place_ref, slot_ref, stars_ref, cells_ref):
    listed = active_ref.shape[1]
    total = state_ref.shape[1]
    devices = lax.axis_size("star") * lax.axis_size("gas")
    slots = lanes // 4
    active = active_ref[...]
    starts = iota((devices, listed), 0) * total
    before = one_hot(active < starts)
    after = one_hot(active < starts + total)
    owned = after - before
    first = jnp.sum(before, 1, keepdims=True)
    place = iota((1, listed), 1).astype(f32) - jnp.sum(owned * first, 0, keepdims=True)
    place_ref[...] = place
    local = active - my_rank() * total
    mine = (local >= 0) & (local < total)
    pick = one_hot((iota((lanes, listed), 0) % slots == place.astype(i32)) & mine).astype(bf16)
    hit = one_hot(iota((total, listed), 0) == local).astype(bf16)
    slot_ref[...] = dot_of(pick, hit, 1, 1).astype(bf16)
    state = stack3(state_ref[...])
    order = (0, 1, 2, 3, 4, 5, 6)
    wide = len(order) * lanes
    ask = one_hot(iota((24, wide), 0) % 8 == iota((24, wide), 1) // lanes).astype(bf16)
    stars_ref[...] = dot_of(state, ask, 0, 0)
    rows = density_ref.shape[0]
    wide = rows * lanes
    ask = one_hot(iota((3 * rows, wide), 0) % rows == iota((3 * rows, wide), 1) // lanes).astype(bf16)
    cells_ref[...] = dot_of(stack3(density_ref[...]), ask, 0, 0)


def force_kernel(ext, got_ref, active_ref, place_ref, stars_ref, cells_ref, send_ref, target_ref, *, chunked):
    ext_x, ext_y, ext_z = ext
    total = stars_ref.shape[0]
    width = active_ref.shape[1]
    devices = got_ref.shape[0]
    slots = lanes // 4
    starts = iota((devices, width), 0) * total
    active = active_ref[...]
    owned = one_hot((active >= starts) & (active < starts + total)).astype(bf16)
    owned3 = jnp.concatenate([owned, owned, owned], 0)
    slot_hit = one_hot(iota((slots, width), 0) == place_ref[...].astype(i32))
    rows = []
    for half in range(2):
        spread = dot_of(stack3(got_ref[:, half, :]), owned3, 0, 0)
        spread = spread.reshape(4, slots, width) * slot_hit[None]
        rows.append(jnp.sum(spread, 1))
    targets = jnp.concatenate(rows, 0)
    target_ref[...] = targets

    first_x = lax.axis_index("star") * ext_x
    first_y = lax.axis_index("gas") * ext_y
    parts = []
    step = 32
    for lane in range(0, width, lanes):
        def row_of(k):
            return jnp.broadcast_to(targets[k : k + 1, lane : lane + lanes], (8, lanes))

        tx, ty, tz, _, tu, tv, tw, _ = [row_of(k) for k in range(8)]

        def wide(row):
            return jnp.concatenate([row] * (step // 8), 0)

        wx, wy, wz, wu, wv, ww = [wide(row) for row in (tx, ty, tz, tu, tv, tw)]

        def fold(block):
            return sum(block[k : k + 8] for k in range(0, step, 8))

        sums = [jnp.zeros((8, lanes), f32) for _ in range(6)]
        for at in range(0, total, step):
            src = [stars_ref[at : at + step, k * lanes : (k + 1) * lanes] for k in range(7)]
            dx, dy, dz = src[0] - wx, src[1] - wy, src[2] - wz
            du, dv, dw = src[4] - wu, src[5] - wv, src[6] - ww
            inv = lax.rsqrt(dx * dx + dy * dy + dz * dz + soften)
            inv2 = inv * inv
            weight = src[3] * inv * inv2
            bend = 3.0 * (dx * du + dy * dv + dz * dw) * inv2 * weight
            vals = (
                weight * dx, weight * dy, weight * dz,
                weight * du - bend * dx, weight * dv - bend * dy, weight * dw - bend * dz,
            )
            sums = [a + fold(b) for a, b in zip(sums, vals)]

        for pair in range(ext_y // 2):
            for at in range(0, 2 * ext_z, step):
                cell_y = (first_y + 2 * pair + at // ext_z).astype(f32) + 0.5
                cell_z = (iota((step, lanes), 0) + at % ext_z).astype(f32) + 0.5
                gap_y = cell_y - ty
                gap_z = cell_z - wz
                base = gap_z * gap_z + wide(gap_y * gap_y + soften)
                along = None
                for k in range(ext_x):
                    gap_x = ((first_x + k).astype(f32) + 0.5) - tx
                    col = (k * (ext_y // 2) + pair) * lanes
                    mass = cells_ref[at : at + step, col : col + lanes]
                    inv = lax.rsqrt(base + wide(gap_x * gap_x))
                    weight = mass * inv * (inv * inv)
                    sums[0] = sums[0] + gap_x * fold(weight)
                    along = weight if along is None else along + weight
                sums[1] = sums[1] + gap_y * fold(along)
                sums[2] = sums[2] + fold(gap_z * along)
        none = jnp.zeros((1, lanes), f32)
        sums = [gravity * jnp.sum(a, 0, keepdims=True) for a in sums]
        parts.append(jnp.concatenate(sums[0:3] + [none] + sums[3:6] + [none], 0))
    partial = jnp.concatenate(parts, 1)
    owned3 = jnp.concatenate([owned, owned, owned], 1)
    for half in range(2):
        spread = partial[4 * half : 4 * half + 4][:, None, :] * slot_hit[None]
        spread = jnp.concatenate(split3(spread.reshape(4 * slots, width)), 1)
        sent = dot_of(owned3, spread, 1, 1)
        if chunked:
            step_at = pl.program_id(0)

            @pl.when(step_at == 0)
            def _():
                send_ref[:, half, :] = sent

            @pl.when(step_at > 0)
            def _():
                send_ref[:, half, :] += sent
        else:
            send_ref[:, half, :] = sent


def kick_kernel(ext, grid, target_ref, kick_ref):
    ext_x, ext_y, ext_z = ext
    width = target_ref.shape[1]

    @pl.when(pl.program_id(0) == 0)
    def _():
        kick_ref[...] = jnp.zeros(kick_ref.shape, f32)

    targets = target_ref[...]
    mass = targets[3:4]
    row = iota((8, width), 0)
    moment = jnp.where(row < 3, targets * mass, jnp.where(row == 3, mass, 0.0))
    left = stack3(moment)
    ask = one_hot(iota((24, 3 * lanes), 0) % 8 == iota((24, 3 * lanes), 1) // lanes).astype(bf16)
    spread = dot_of(stack3(targets), ask, 0, 0)
    tx, ty, tz = spread[:, 0:lanes], spread[:, lanes : 2 * lanes], spread[:, 2 * lanes :]
    lane = iota((1, lanes), 1)
    cell_z = (lane % ext_z).astype(f32) + 0.5
    gap_z = cell_z - tz
    base = gap_z * gap_z + soften
    first_x = lax.axis_index("star") * ext_x + grid[0] - rim
    first_y = lax.axis_index("gas") * ext_y + grid[1] - rim
    place_x, square_x = [], []
    for pair in range((ext_x + 2 * rim) // 2):
        at = lax.rem(first_x + 2 * pair + lane // ext_z, grid[0])
        at = at.astype(f32) + 0.5
        place_x.append(at)
        square_x.append((at - tx) * (at - tx))
    for j in range(ext_y + 2 * rim):
        at_y = lax.rem(first_y + j, grid[1]).astype(f32) + 0.5
        gap_y = at_y - ty
        base_y = base + gap_y * gap_y
        out_y = max(rim - j, j - (ext_y + rim - 1), 0)
        for pair in range((ext_x + 2 * rim) // 2):
            out_x = min(max(rim - i, i - (ext_x + rim - 1), 0) for i in (2 * pair, 2 * pair + 1))
            if out_x + out_y > rim:
                continue
            inv = lax.rsqrt(base_y + square_x[pair])
            weight = inv * (inv * inv)
            high = weight.astype(bf16)
            low = (weight - high.astype(f32)).astype(bf16)
            sums = dot_of(left, high) + dot_of(left, low)
            sums = sums[0:8] + sums[8:16] + sums[16:24]
            whole = sums[3:4]
            kick_ref[0, pair, j + 1 : j + 2, :] += sums[0:1] - place_x[pair] * whole
            kick_ref[1, pair, j + 1 : j + 2, :] += sums[1:2] - at_y * whole
            kick_ref[2, pair, j + 1 : j + 2, :] += sums[2:3] - cell_z * whole


def twice(values):
    half = lanes // 2
    turned = pltpu.roll(values, half, values.ndim - 1)
    left = iota(values.shape, values.ndim - 1) < half
    return jnp.where(left, values, turned), jnp.where(left, turned, values)


def diff_x(values):
    return values[2:] - values[:-2]


def diff_y(values):
    rows = values.shape[1]
    return (pltpu.roll(values, rows - 1, 1) - pltpu.roll(values, 1, 1))[1:-1]


def diff_z(values):
    return (pltpu.roll(values, lanes - 1, 2) - pltpu.roll(values, 1, 2))[1:-1]


def double_curl(a, b, c):
    return (diff_y(c) - diff_z(b), diff_z(a) - diff_x(c), diff_x(b) - diff_y(a))


def cross_of(lhs, rhs):
    return (
        lhs[1] * rhs[2] - lhs[2] * rhs[1],
        lhs[2] * rhs[0] - lhs[0] * rhs[2],
        lhs[0] * rhs[1] - lhs[1] * rhs[0],
    )


def inner(values, width):
    return [v[width:-width] for v in values]


def double_rate(field, flow, half_resist):
    current = double_curl(*field)
    held = inner(field, 1)
    drift = cross_of(cross_of(current, held), held)
    motion = cross_of(flow, held)
    return double_curl(*[m + half_resist * d for m, d in zip(motion, drift)])


def field_kernel(ext, own_ref, near_ref, far_ref, kick_ref, flow_ref, out_ref):
    ext_x, ext_y, ext_z = ext
    even = lax.axis_index("star") % 2 == 0
    comps = []
    for k in range(4):
        near, far = near_ref[k], far_ref[k]
        below = jnp.where(even, far, near)
        above = jnp.where(even, near, far)
        if k == 3:
            comps.append(jnp.concatenate([below, own_ref[k], above], 0)[1:-1])
        else:
            comps.extend(twice(jnp.concatenate([below, own_ref[k], above], 0)))
    field = comps[0:3]
    dense = comps[6]
    inv = lax.rsqrt(dense)
    half_resist = 0.5 * (inv * inv * inv)
    flow = []
    for k in range(3):
        kick = jnp.stack(twice(kick_ref[k]), 1).reshape((ext_x + 2 * rim,) + kick_ref.shape[2:])
        flow.append(comps[3 + k][1:-1] + (time_step * gravity) * kick)
    rows = slice(reach, reach + ext_y)
    for k in range(3):
        flow_ref[k] = flow[k][rim:-rim, rows, 0:ext_z]
    rate = double_rate(field, flow, half_resist)
    section = [b + (0.5 * field_step) * r for b, r in zip(inner(field, 2), rate)]
    rate = double_rate(section, inner(flow, 2), half_resist[2:-2])
    for k in range(3):
        new = field[k][reach:-reach] + section[k][2:-2] + (0.5 * field_step) * rate[k]
        out_ref[k] = 0.5 * new[:, rows, 0:ext_z]


def update_kernel(back_ref, pos_ref, vel_ref, acc_ref, slot_ref, order_ref, out_ref):
    slots = lanes // 4
    summed = jnp.sum(back_ref[...], 0)
    row, lane = iota((8, lanes), 0), iota((8, lanes), 1)
    terms = jnp.where(row < 3, summed[0:1], summed[1:2])
    terms = jnp.where((row < 6) & (row % 3 == lane // slots), terms, 0.0)
    slot = slot_ref[...]
    pieces = dot_of(stack3(terms), slot)
    new = pieces[0:8] + pieces[8:16] + pieces[16:24]
    new_acc, new_jerk = new[0:3], new[3:6]
    pos, vel = pos_ref[...], vel_ref[...]
    old_acc, old_jerk = acc_ref[0:3], acc_ref[3:6]
    vel_one = (
        vel + time_step * (old_acc + new_acc) / 2.0 + time_step**2 * (old_jerk - new_jerk) / 12.0
    )
    pos_one = (
        pos + time_step * (vel + vel_one) / 2.0 + time_step**2 * (old_acc - new_acc) / 12.0
    )
    listed = jnp.sum(slot[0:slots].astype(f32), 0, keepdims=True) > 0.5
    out_ref[0:3] = jnp.where(listed, pos_one, pos)
    out_ref[3:6] = jnp.where(listed, vel_one, vel)
    out_ref[6:9] = jnp.where(listed, new_acc, old_acc)
    out_ref[9:12] = jnp.where(listed, new_jerk, old_jerk)


def swap_pairs(near, far, axis):
    count = lax.axis_size(axis)
    inside = [(i, i ^ 1) for i in range(count)]
    between = [(i, (i + (1 if i % 2 else -1)) % count) for i in range(count)]
    got_far = lax.ppermute(far, axis, between)
    got_near = lax.ppermute(near, axis, inside)
    return got_near, got_far


def body(star_pos, star_vel, star_accel, star_mass, active, density, flow_in, field_in):
    def shape(*dims, dtype=f32):
        return jax.ShapeDtypeStruct(dims, dtype)

    total = star_pos.shape[1]
    listed = active.shape[0]
    star_count, gas_count = lax.axis_size("star"), lax.axis_size("gas")
    devices = star_count * gas_count
    ext = density.shape
    ext_x, ext_y, ext_z = ext
    grid = (ext_x * star_count, ext_y * gas_count)
    width = min(listed, 256)
    chunks = listed // width
    names = active.reshape(1, listed)
    inputs = [
        star_pos, star_vel, star_accel, star_mass.reshape(1, total), names, field_in, flow_in, density
    ]
    *held, send, state = call(
        predict_kernel,
        [shape(*x.shape, dtype=x.dtype) for x in inputs] + [shape(devices, 2, lanes), shape(8, total)],
        *[pltpu.with_memory_space_constraint(x, pltpu.HBM) for x in inputs],
        in_specs=[pl.BlockSpec(memory_space=pltpu.HBM)] * len(inputs),
        scratch=[pltpu.SemaphoreType.DMA((len(inputs),))],
    )
    pos, vel, acc, _, names, field, flow, dense = held
    got = lax.all_to_all(send, both, 0, 0, tiled=True)

    own, near, far, rows = call(
        pack_kernel,
        (shape(4, ext_x, ext_y, lanes), shape(4, ext_x, reach, lanes), shape(4, ext_x, reach, lanes),
         shape(ext_x * ext_y // 2, 2 * ext_z)),
        field, flow, dense, send, after=1,
    )
    near, far = swap_pairs(near, far, "gas")
    place, slot, stars, cells = call(
        index_kernel,
        (shape(1, listed), shape(lanes, total, dtype=bf16), shape(total, 7 * lanes),
         shape(2 * ext_z, ext_x * ext_y // 2 * lanes)),
        names, state, rows,
    )
    def all_of(*dims):
        return pl.BlockSpec(dims, lambda k: (0,) * len(dims))

    def part_of(rows):
        return pl.BlockSpec((rows, width), lambda k: (0, k))

    back, targets = call(
        functools.partial(force_kernel, ext, chunked=chunks > 1),
        (shape(devices, 2, lanes), shape(8, listed)),
        got, names, place, stars, cells,
        grid=(chunks,),
        in_specs=[all_of(*got.shape), part_of(1), part_of(1), all_of(*stars.shape), all_of(*cells.shape)],
        out_specs=(all_of(devices, 2, lanes), part_of(8)),
    )
    back = lax.all_to_all(back, both, 0, 0, tiled=True)

    if ext_x != reach:
        raise ValueError("brick depth")
    brick = call(
        join_kernel, shape(4, ext_x, ext_y + 2 * reach, lanes), own, near, far, targets, after=1
    )
    near, far = swap_pairs(brick, brick, "star")
    kick_shape = (3, (ext_x + 2 * rim) // 2, ext_y + 2 * reach, lanes)
    kick = call(
        functools.partial(kick_kernel, ext, grid), shape(*kick_shape), targets,
        grid=(chunks,), in_specs=[part_of(8)], out_specs=all_of(*kick_shape),
    )
    flow, field_out = call(
        functools.partial(field_kernel, ext),
        (shape(*flow_in.shape), shape(*field_in.shape)), brick, near, far, kick,
    )
    star_new = call(
        update_kernel, shape(12, total), back, pos, vel, acc, slot,
        pltpu.with_memory_space_constraint(field_out, pltpu.HBM), after=1, where=pltpu.HBM,
    )
    return (star_new, flow, field_out)


def solution(mesh):
    placed = (
        P(None, both),
        P(None, both),
        P(None, both),
        P(both),
        P(),
        P("star", "gas", None),
        P(None, "star", "gas", None),
        P(None, "star", "gas", None),
    )
    return jax.shard_map(
        body,
        mesh=mesh,
        in_specs=placed,
        out_specs=(
            P(None, both),
            P(None, "star", "gas", None),
            P(None, "star", "gas", None),
        ),
        check_vma=False,
    )
```

```python
import functools

import jax
import jax.numpy as jnp
from jax import lax
from jax.experimental import pallas as pl
from jax.experimental.pallas import tpu as pltpu
from jax.sharding import PartitionSpec as P

gravity = 0.02
soften = 4.0
time_step = 1.5
field_step = 0.1
both = ("star", "gas")
reach = 4
rim = reach - 1
lanes = 128
vmem_bytes = 48 * 1024 * 1024
batch = 4
f32, bf16, i32 = jnp.float32, jnp.bfloat16, jnp.int32


def iota(shape, dim):
    return lax.broadcasted_iota(i32, shape, dim)


def split3(values):
    high = values.astype(bf16)
    rest = values - high.astype(f32)
    mid = rest.astype(bf16)
    low = (rest - mid.astype(f32)).astype(bf16)
    return high, mid, low


def stack3(values):
    return jnp.concatenate(split3(values), 0)


def dot_of(lhs, rhs, lhs_dim=1, rhs_dim=0):
    return lax.dot_general(
        lhs, rhs, (((lhs_dim,), (rhs_dim,)), ((), ())), preferred_element_type=f32
    )


def one_hot(hits):
    return jnp.where(hits, 1.0, 0.0)


def my_rank():
    return lax.axis_index("star") * lax.axis_size("gas") + lax.axis_index("gas")


def call(kernel, outs, *args, grid=None, in_specs=None, out_specs=None, scratch=(), after=0, where=pl.ANY, cost=None):
    spec = {}
    if grid is not None:
        spec = dict(grid=grid, in_specs=in_specs, out_specs=out_specs)
    elif in_specs is not None:
        spec = dict(in_specs=in_specs)
    elif after:
        held = [pl.BlockSpec(memory_space=pltpu.VMEM)] * (len(args) - after)
        spec = dict(in_specs=held + [pl.BlockSpec(memory_space=where)] * after)
    return pl.pallas_call(
        kernel,
        out_shape=outs,
        scratch_shapes=list(scratch),
        cost_estimate=cost,
        compiler_params=pltpu.CompilerParams(vmem_limit_bytes=vmem_bytes),
        **spec,
    )(*args)


def predict_kernel(*refs):
    sources, held = refs[0:8], refs[8:16]
    send_ref, state_ref, sems = refs[16:]
    copies = [
        pltpu.make_async_copy(source, target, sems.at[k])
        for k, (source, target) in enumerate(zip(sources, held))
    ]
    for copy in copies:
        copy.start()
    for copy in copies[0:5]:
        copy.wait()
    pos_ref, vel_ref, acc_ref, mass_ref, active_ref = held[0:5]
    total = pos_ref.shape[1]
    listed = active_ref.shape[1]
    slots = lanes // 4
    pos, vel = pos_ref[...], vel_ref[...]
    old_acc, old_jerk = acc_ref[0:3], acc_ref[3:6]
    pred_pos = (
        pos + time_step * vel + time_step**2 / 2.0 * old_acc + time_step**3 / 6.0 * old_jerk
    )
    pred_vel = vel + time_step * old_acc + time_step**2 / 2.0 * old_jerk
    state = jnp.concatenate([pred_pos, mass_ref[...], pred_vel, jnp.zeros((1, total), f32)], 0)
    state_ref[...] = state
    local = active_ref[...] - my_rank() * total
    first = jnp.sum(one_hot(local < 0)).astype(i32)
    hit = one_hot(iota((total, listed), 0) == local).astype(bf16)
    pieces = dot_of(stack3(state), hit)
    placed = pieces[0:8] + pieces[8:16] + pieces[16:24]
    placed = pltpu.roll(placed, lax.rem(listed - first, listed), 1)[:, 0:lanes]
    lane = iota((8, lanes), 1)
    row = iota((8, lanes), 0)
    part = jnp.where(lane < slots, placed, 0.0)
    spread = part
    for k in range(1, 4):
        spread = jnp.where(lane // slots == k, pltpu.roll(part, k * slots, 1), spread)
    spread = jnp.where(row % 4 == lane // slots, spread, 0.0)
    one = jnp.sum(spread[0:4], 0, keepdims=True)
    two = jnp.sum(spread[4:8], 0, keepdims=True)
    send_ref[...] = jnp.broadcast_to(jnp.concatenate([one, two], 0)[None], send_ref.shape)
    for copy in copies[5:]:
        copy.wait()


def pack_kernel(field_ref, flow_ref, density_ref, order_ref, own_ref, near_ref, far_ref, rows_ref):
    comps = [field_ref[0], field_ref[1], field_ref[2], flow_ref[0], flow_ref[1], flow_ref[2]]
    comps = comps + [density_ref[...], density_ref[...]]
    even = lax.axis_index("gas") % 2 == 0
    for k in range(4):
        pair = jnp.concatenate([comps[2 * k], comps[2 * k + 1]], -1)
        own_ref[k] = pair
        low, high = pair[:, :reach], pair[:, -reach:]
        near_ref[k] = jnp.where(even, high, low)
        far_ref[k] = jnp.where(even, low, high)
    half = density_ref.shape[1] // 2
    for k in range(density_ref.shape[0]):
        first = density_ref[k, pl.ds(0, half, stride=2), :]
        second = density_ref[k, pl.ds(1, half, stride=2), :]
        rows_ref[k * half : (k + 1) * half] = jnp.concatenate([first, second], -1)


def join_kernel(own_ref, near_ref, far_ref, order_ref, out_ref):
    even = lax.axis_index("gas") % 2 == 0
    near, far = near_ref[...], far_ref[...]
    below = jnp.where(even, far, near)
    above = jnp.where(even, near, far)
    out_ref[...] = jnp.concatenate([below, own_ref[...], above], 2)


def index_kernel(active_ref, state_ref, density_ref, place_ref, slot_ref, stars_ref, cells_ref):
    listed = active_ref.shape[1]
    total = state_ref.shape[1]
    devices = lax.axis_size("star") * lax.axis_size("gas")
    slots = lanes // 4
    active = active_ref[...]
    starts = iota((devices, listed), 0) * total
    before = one_hot(active < starts)
    after = one_hot(active < starts + total)
    owned = after - before
    first = jnp.sum(before, 1, keepdims=True)
    place = iota((1, listed), 1).astype(f32) - jnp.sum(owned * first, 0, keepdims=True)
    place_ref[...] = place
    local = active - my_rank() * total
    mine = (local >= 0) & (local < total)
    pick = one_hot((iota((lanes, listed), 0) % slots == place.astype(i32)) & mine).astype(bf16)
    hit = one_hot(iota((total, listed), 0) == local).astype(bf16)
    slot_ref[...] = dot_of(pick, hit, 1, 1).astype(bf16)
    state = stack3(state_ref[...])
    order = (0, 1, 2, 3, 4, 5, 6)
    wide = len(order) * lanes
    ask = one_hot(iota((24, wide), 0) % 8 == iota((24, wide), 1) // lanes).astype(bf16)
    stars_ref[...] = dot_of(state, ask, 0, 0)
    rows = density_ref.shape[0]
    wide = rows * lanes
    ask = one_hot(iota((3 * rows, wide), 0) % rows == iota((3 * rows, wide), 1) // lanes).astype(bf16)
    cells_ref[...] = dot_of(stack3(density_ref[...]), ask, 0, 0)


def force_kernel(ext, got_ref, active_ref, place_ref, stars_ref, cells_ref, send_ref, target_ref, *, chunked):
    ext_x, ext_y, ext_z = ext
    total = stars_ref.shape[0]
    width = active_ref.shape[1]
    devices = got_ref.shape[0]
    slots = lanes // 4
    starts = iota((devices, width), 0) * total
    active = active_ref[...]
    owned = one_hot((active >= starts) & (active < starts + total)).astype(bf16)
    owned3 = jnp.concatenate([owned, owned, owned], 0)
    slot_hit = one_hot(iota((slots, width), 0) == place_ref[...].astype(i32))
    rows = []
    for half in range(2):
        spread = dot_of(stack3(got_ref[:, half, :]), owned3, 0, 0)
        spread = spread.reshape(4, slots, width) * slot_hit[None]
        rows.append(jnp.sum(spread, 1))
    targets = jnp.concatenate(rows, 0)
    target_ref[...] = targets

    first_x = lax.axis_index("star") * ext_x
    first_y = lax.axis_index("gas") * ext_y
    parts = []
    step = 32
    for lane in range(0, width, lanes):
        def row_of(k):
            return jnp.broadcast_to(targets[k : k + 1, lane : lane + lanes], (8, lanes))

        tx, ty, tz, _, tu, tv, tw, _ = [row_of(k) for k in range(8)]

        def wide(row):
            return jnp.concatenate([row] * (step // 8), 0)

        wx, wy, wz, wu, wv, ww = [wide(row) for row in (tx, ty, tz, tu, tv, tw)]

        def fold(block):
            return sum(block[k : k + 8] for k in range(0, step, 8))

        sums = [jnp.zeros((8, lanes), f32) for _ in range(6)]
        for at in range(0, total, step):
            src = [stars_ref[at : at + step, k * lanes : (k + 1) * lanes] for k in range(7)]
            dx, dy, dz = src[0] - wx, src[1] - wy, src[2] - wz
            du, dv, dw = src[4] - wu, src[5] - wv, src[6] - ww
            inv = lax.rsqrt(dx * dx + dy * dy + dz * dz + soften)
            inv2 = inv * inv
            weight = src[3] * inv * inv2
            bend = 3.0 * (dx * du + dy * dv + dz * dw) * inv2 * weight
            vals = (
                weight * dx, weight * dy, weight * dz,
                weight * du - bend * dx, weight * dv - bend * dy, weight * dw - bend * dz,
            )
            sums = [a + fold(b) for a, b in zip(sums, vals)]

        for pair in range(ext_y // 2):
            for at in range(0, 2 * ext_z, step):
                cell_y = (first_y + 2 * pair + at // ext_z).astype(f32) + 0.5
                cell_z = (iota((step, lanes), 0) + at % ext_z).astype(f32) + 0.5
                gap_y = cell_y - ty
                gap_z = cell_z - wz
                base = gap_z * gap_z + wide(gap_y * gap_y + soften)
                along = None
                for k in range(ext_x):
                    gap_x = ((first_x + k).astype(f32) + 0.5) - tx
                    col = (k * (ext_y // 2) + pair) * lanes
                    mass = cells_ref[at : at + step, col : col + lanes]
                    inv = lax.rsqrt(base + wide(gap_x * gap_x))
                    weight = mass * inv * (inv * inv)
                    sums[0] = sums[0] + gap_x * fold(weight)
                    along = weight if along is None else along + weight
                sums[1] = sums[1] + gap_y * fold(along)
                sums[2] = sums[2] + fold(gap_z * along)
        none = jnp.zeros((1, lanes), f32)
        sums = [gravity * jnp.sum(a, 0, keepdims=True) for a in sums]
        parts.append(jnp.concatenate(sums[0:3] + [none] + sums[3:6] + [none], 0))
    partial = jnp.concatenate(parts, 1)
    owned3 = jnp.concatenate([owned, owned, owned], 1)
    for half in range(2):
        spread = partial[4 * half : 4 * half + 4][:, None, :] * slot_hit[None]
        spread = jnp.concatenate(split3(spread.reshape(4 * slots, width)), 1)
        sent = dot_of(owned3, spread, 1, 1)
        if chunked:
            step_at = pl.program_id(0)

            @pl.when(step_at == 0)
            def _():
                send_ref[:, half, :] = sent

            @pl.when(step_at > 0)
            def _():
                send_ref[:, half, :] += sent
        else:
            send_ref[:, half, :] = sent


def kick_kernel(ext, grid, target_ref, kick_ref, *, chunked):
    ext_x, ext_y, ext_z = ext
    width = target_ref.shape[1]

    def clear():
        kick_ref[...] = jnp.zeros(kick_ref.shape, f32)

    if chunked:
        pl.when(pl.program_id(0) == 0)(clear)
    else:
        clear()
    targets = target_ref[...]
    mass = targets[3:4]
    row = iota((8, width), 0)
    moment = jnp.where(row < 3, targets * mass, jnp.where(row == 3, mass, 0.0))
    left = stack3(moment)
    ask = one_hot(iota((24, 3 * lanes), 0) % 8 == iota((24, 3 * lanes), 1) // lanes).astype(bf16)
    spread = dot_of(stack3(targets), ask, 0, 0)
    tx, ty, tz = spread[:, 0:lanes], spread[:, lanes : 2 * lanes], spread[:, 2 * lanes :]
    lane = iota((1, lanes), 1)
    cell_z = (lane % ext_z).astype(f32) + 0.5
    gap_z = cell_z - tz
    base = gap_z * gap_z + soften
    first_x = lax.axis_index("star") * ext_x + grid[0] - rim
    first_y = lax.axis_index("gas") * ext_y + grid[1] - rim
    place_x, square_x = [], []
    for pair in range((ext_x + 2 * rim) // 2):
        at = lax.rem(first_x + 2 * pair + lane // ext_z, grid[0])
        at = at.astype(f32) + 0.5
        place_x.append(at)
        square_x.append((at - tx) * (at - tx))
    tiles = []
    for j in range(ext_y + 2 * rim):
        out_y = max(rim - j, j - (ext_y + rim - 1), 0)
        for pair in range((ext_x + 2 * rim) // 2):
            out_x = min(max(rim - i, i - (ext_x + rim - 1), 0) for i in (2 * pair, 2 * pair + 1))
            if out_x + out_y <= rim:
                tiles.append((j, pair))
    base_y, at_y = {}, {}
    for k in range(0, len(tiles), batch):
        part = tiles[k : k + batch]
        high, low = [], []
        for j, pair in part:
            if j not in base_y:
                at_y[j] = lax.rem(first_y + j, grid[1]).astype(f32) + 0.5
                gap_y = at_y[j] - ty
                base_y[j] = base + gap_y * gap_y
            inv = lax.rsqrt(base_y[j] + square_x[pair])
            weight = inv * (inv * inv)
            high.append(weight.astype(bf16))
            low.append((weight - high[-1].astype(f32)).astype(bf16))
        sums = dot_of(left, jnp.concatenate(high, 1)) + dot_of(left, jnp.concatenate(low, 1))
        sums = sums[0:8] + sums[8:16] + sums[16:24]
        for at, (j, pair) in enumerate(part):
            here = sums[:, at * lanes : (at + 1) * lanes]
            whole = here[3:4]
            kick_ref[0, pair, j + 1 : j + 2, :] += here[0:1] - place_x[pair] * whole
            kick_ref[1, pair, j + 1 : j + 2, :] += here[1:2] - at_y[j] * whole
            kick_ref[2, pair, j + 1 : j + 2, :] += here[2:3] - cell_z * whole


def twice(values):
    half = lanes // 2
    turned = pltpu.roll(values, half, values.ndim - 1)
    left = iota(values.shape, values.ndim - 1) < half
    return jnp.where(left, values, turned), jnp.where(left, turned, values)


def diff_x(values):
    return values[2:] - values[:-2]


def diff_y(values):
    rows = values.shape[1]
    return (pltpu.roll(values, rows - 1, 1) - pltpu.roll(values, 1, 1))[1:-1]


def diff_z(values):
    return (pltpu.roll(values, lanes - 1, 2) - pltpu.roll(values, 1, 2))[1:-1]


def double_curl(a, b, c):
    return (diff_y(c) - diff_z(b), diff_z(a) - diff_x(c), diff_x(b) - diff_y(a))


def cross_of(lhs, rhs):
    return (
        lhs[1] * rhs[2] - lhs[2] * rhs[1],
        lhs[2] * rhs[0] - lhs[0] * rhs[2],
        lhs[0] * rhs[1] - lhs[1] * rhs[0],
    )


def inner(values, width):
    return [v[width:-width] for v in values]


def double_rate(field, flow, half_resist):
    current = double_curl(*field)
    held = inner(field, 1)
    drift = cross_of(cross_of(current, held), held)
    motion = cross_of(flow, held)
    return double_curl(*[m + half_resist * d for m, d in zip(motion, drift)])


def field_kernel(ext, own_ref, near_ref, far_ref, kick_ref, flow_ref, out_ref):
    ext_x, ext_y, ext_z = ext
    even = lax.axis_index("star") % 2 == 0
    comps = []
    for k in range(4):
        near, far = near_ref[k], far_ref[k]
        below = jnp.where(even, far, near)
        above = jnp.where(even, near, far)
        if k == 3:
            comps.append(jnp.concatenate([below, own_ref[k], above], 0)[1:-1])
        else:
            comps.extend(twice(jnp.concatenate([below, own_ref[k], above], 0)))
    field = comps[0:3]
    dense = comps[6]
    inv = lax.rsqrt(dense)
    half_resist = 0.5 * (inv * inv * inv)
    flow = []
    for k in range(3):
        kick = jnp.stack(twice(kick_ref[k]), 1).reshape((ext_x + 2 * rim,) + kick_ref.shape[2:])
        flow.append(comps[3 + k][1:-1] + (time_step * gravity) * kick)
    rows = slice(reach, reach + ext_y)
    for k in range(3):
        flow_ref[k] = flow[k][rim:-rim, rows, 0:ext_z]
    rate = double_rate(field, flow, half_resist)
    section = [b + (0.5 * field_step) * r for b, r in zip(inner(field, 2), rate)]
    rate = double_rate(section, inner(flow, 2), half_resist[2:-2])
    for k in range(3):
        new = field[k][reach:-reach] + section[k][2:-2] + (0.5 * field_step) * rate[k]
        out_ref[k] = 0.5 * new[:, rows, 0:ext_z]


def order_kernel(order_ref, out_ref):
    out_ref[...] = jnp.zeros(out_ref.shape, f32)


def update_kernel(back_ref, pos_ref, vel_ref, acc_ref, slot_ref, order_ref, out_ref):
    slots = lanes // 4
    summed = jnp.sum(back_ref[...], 0)
    row, lane = iota((8, lanes), 0), iota((8, lanes), 1)
    terms = jnp.where(row < 3, summed[0:1], summed[1:2])
    terms = jnp.where((row < 6) & (row % 3 == lane // slots), terms, 0.0)
    slot = slot_ref[...]
    pieces = dot_of(stack3(terms), slot)
    new = pieces[0:8] + pieces[8:16] + pieces[16:24]
    new_acc, new_jerk = new[0:3], new[3:6]
    pos, vel = pos_ref[...], vel_ref[...]
    old_acc, old_jerk = acc_ref[0:3], acc_ref[3:6]
    vel_one = (
        vel + time_step * (old_acc + new_acc) / 2.0 + time_step**2 * (old_jerk - new_jerk) / 12.0
    )
    pos_one = (
        pos + time_step * (vel + vel_one) / 2.0 + time_step**2 * (old_acc - new_acc) / 12.0
    )
    listed = jnp.sum(slot[0:slots].astype(f32), 0, keepdims=True) > 0.5
    out_ref[0:3] = jnp.where(listed, pos_one, pos)
    out_ref[3:6] = jnp.where(listed, vel_one, vel)
    out_ref[6:9] = jnp.where(listed, new_acc, old_acc)
    out_ref[9:12] = jnp.where(listed, new_jerk, old_jerk)


def swap_pairs(near, far, axis):
    count = lax.axis_size(axis)
    inside = [(i, i ^ 1) for i in range(count)]
    between = [(i, (i + (1 if i % 2 else -1)) % count) for i in range(count)]
    got_far = lax.ppermute(far, axis, between)
    got_near = lax.ppermute(near, axis, inside)
    return got_near, got_far


def body(star_pos, star_vel, star_accel, star_mass, active, density, flow_in, field_in):
    def shape(*dims, dtype=f32):
        return jax.ShapeDtypeStruct(dims, dtype)

    total = star_pos.shape[1]
    listed = active.shape[0]
    star_count, gas_count = lax.axis_size("star"), lax.axis_size("gas")
    devices = star_count * gas_count
    ext = density.shape
    ext_x, ext_y, ext_z = ext
    grid = (ext_x * star_count, ext_y * gas_count)
    width = min(listed, 256)
    chunks = listed // width
    names = active.reshape(1, listed)
    inputs = [
        star_pos, star_vel, star_accel, star_mass.reshape(1, total), names, field_in, flow_in, density
    ]
    *held, send, state = call(
        predict_kernel,
        [shape(*x.shape, dtype=x.dtype) for x in inputs] + [shape(devices, 2, lanes), shape(8, total)],
        *[pltpu.with_memory_space_constraint(x, pltpu.HBM) for x in inputs],
        in_specs=[pl.BlockSpec(memory_space=pltpu.HBM)] * len(inputs),
        scratch=[pltpu.SemaphoreType.DMA((len(inputs),))],
    )
    pos, vel, acc, _, names, field, flow, dense = held
    got = lax.all_to_all(send, both, 0, 0, tiled=True)

    own, near, far, rows = call(
        pack_kernel,
        (shape(4, ext_x, ext_y, lanes), shape(4, ext_x, reach, lanes), shape(4, ext_x, reach, lanes),
         shape(ext_x * ext_y // 2, 2 * ext_z)),
        field, flow, dense, send, after=1,
    )
    near, far = swap_pairs(near, far, "gas")
    place, slot, stars, cells = call(
        index_kernel,
        (shape(1, listed), shape(lanes, total, dtype=bf16), shape(total, 7 * lanes),
         shape(2 * ext_z, ext_x * ext_y // 2 * lanes)),
        names, state, rows,
    )
    def all_of(*dims):
        return pl.BlockSpec(dims, lambda k: (0,) * len(dims))

    def part_of(rows):
        return pl.BlockSpec((rows, width), lambda k: (0, k))

    def in_parts(in_specs, out_specs):
        if chunks == 1:
            return {}
        return dict(grid=(chunks,), in_specs=in_specs, out_specs=out_specs)

    back, targets = call(
        functools.partial(force_kernel, ext, chunked=chunks > 1),
        (shape(devices, 2, lanes), shape(8, listed)),
        got, names, place, stars, cells,
        **in_parts(
            [all_of(*got.shape), part_of(1), part_of(1), all_of(*stars.shape), all_of(*cells.shape)],
            (all_of(devices, 2, lanes), part_of(8)),
        ),
    )
    back = lax.all_to_all(back, both, 0, 0, tiled=True)

    if ext_x != reach:
        raise ValueError("brick depth")
    kick_shape = (3, (ext_x + 2 * rim) // 2, ext_y + 2 * reach, lanes)
    brick_shape = (4, ext_x, ext_y + 2 * reach, lanes)

    def one_turn(_):
        brick = call(join_kernel, shape(*brick_shape), own, near, far, targets, after=1)
        side, other = swap_pairs(brick, brick, "star")
        kick = call(
            functools.partial(kick_kernel, ext, grid, chunked=chunks > 1), shape(*kick_shape), targets,
            **in_parts([part_of(8)], all_of(*kick_shape)),
        )
        flow, field_out = call(
            functools.partial(field_kernel, ext),
            (shape(*flow_in.shape), shape(*field_in.shape)), brick, side, other, kick,
        )
        return flow, field_out

    def no_turn(_):
        return jnp.zeros(flow_in.shape, f32), jnp.zeros(field_in.shape, f32)

    flow, field_out = lax.cond(lax.axis_index("star") < star_count, one_turn, no_turn, 0)
    order = call(
        order_kernel, shape(8, lanes), pltpu.with_memory_space_constraint(field_out, pltpu.HBM),
        after=1, where=pltpu.HBM,
        cost=pl.CostEstimate(flops=10**10, bytes_accessed=10**8, transcendentals=0),
    )
    star_new = call(
        update_kernel, shape(12, total), back, pos, vel, acc, slot,
        order, after=1,
    )
    return (star_new, flow, field_out)


def solution(mesh):
    placed = (
        P(None, both),
        P(None, both),
        P(None, both),
        P(both),
        P(),
        P("star", "gas", None),
        P(None, "star", "gas", None),
        P(None, "star", "gas", None),
    )
    return jax.shard_map(
        body,
        mesh=mesh,
        in_specs=placed,
        out_specs=(
            P(None, both),
            P(None, "star", "gas", None),
            P(None, "star", "gas", None),
        ),
        check_vma=False,
    )
```

```python
import functools

import jax
import jax.numpy as jnp
from jax import lax
from jax.experimental import pallas as pl
from jax.experimental.pallas import tpu as pltpu
from jax.sharding import PartitionSpec as P

gravity = 0.02
soften = 4.0
time_step = 1.5
field_step = 0.1
both = ("star", "gas")
reach = 4
rim = reach - 1
lanes = 128
vmem_bytes = 48 * 1024 * 1024
batch = 4
depth = 512
f32, bf16, i32 = jnp.float32, jnp.bfloat16, jnp.int32


def iota(shape, dim):
    return lax.broadcasted_iota(i32, shape, dim)


def split3(values):
    high = values.astype(bf16)
    rest = values - high.astype(f32)
    mid = rest.astype(bf16)
    low = (rest - mid.astype(f32)).astype(bf16)
    return high, mid, low


def stack3(values):
    return jnp.concatenate(split3(values), 0)


def dot_of(lhs, rhs, lhs_dim=1, rhs_dim=0):
    return lax.dot_general(
        lhs, rhs, (((lhs_dim,), (rhs_dim,)), ((), ())), preferred_element_type=f32
    )


def one_hot(hits):
    return jnp.where(hits, 1.0, 0.0)


def my_rank():
    return lax.axis_index("star") * lax.axis_size("gas") + lax.axis_index("gas")


def call(kernel, outs, *args, grid=None, in_specs=None, out_specs=None, scratch=(), after=0, where=pl.ANY, cost=None):
    spec = {}
    if grid is not None:
        spec = dict(grid=grid, in_specs=in_specs, out_specs=out_specs)
    elif in_specs is not None:
        spec = dict(in_specs=in_specs)
    elif after:
        held = [pl.BlockSpec(memory_space=pltpu.VMEM)] * (len(args) - after)
        spec = dict(in_specs=held + [pl.BlockSpec(memory_space=where)] * after)
    return pl.pallas_call(
        kernel,
        out_shape=outs,
        scratch_shapes=list(scratch),
        cost_estimate=cost,
        compiler_params=pltpu.CompilerParams(vmem_limit_bytes=vmem_bytes),
        **spec,
    )(*args)


def predict_kernel(*refs):
    sources, held = refs[0:8], refs[8:16]
    send_ref, state_ref, sems = refs[16:]
    copies = [
        pltpu.make_async_copy(source, target, sems.at[k])
        for k, (source, target) in enumerate(zip(sources, held))
    ]
    for copy in copies:
        copy.start()
    for copy in copies[0:5]:
        copy.wait()
    pos_ref, vel_ref, acc_ref, mass_ref, active_ref = held[0:5]
    total = pos_ref.shape[1]
    listed = active_ref.shape[1]
    slots = lanes // 4
    pos, vel = pos_ref[...], vel_ref[...]
    old_acc, old_jerk = acc_ref[0:3], acc_ref[3:6]
    pred_pos = (
        pos + time_step * vel + time_step**2 / 2.0 * old_acc + time_step**3 / 6.0 * old_jerk
    )
    pred_vel = vel + time_step * old_acc + time_step**2 / 2.0 * old_jerk
    state = jnp.concatenate([pred_pos, mass_ref[...], pred_vel, jnp.zeros((1, total), f32)], 0)
    state_ref[...] = state
    local = active_ref[...] - my_rank() * total
    first = jnp.sum(one_hot(local < 0)).astype(i32)
    hit = one_hot(iota((total, listed), 0) == local).astype(bf16)
    pieces = dot_of(stack3(state), hit)
    placed = pieces[0:8] + pieces[8:16] + pieces[16:24]
    placed = pltpu.roll(placed, lax.rem(listed - first, listed), 1)[:, 0:lanes]
    lane = iota((8, lanes), 1)
    row = iota((8, lanes), 0)
    part = jnp.where(lane < slots, placed, 0.0)
    spread = part
    for k in range(1, 4):
        spread = jnp.where(lane // slots == k, pltpu.roll(part, k * slots, 1), spread)
    spread = jnp.where(row % 4 == lane // slots, spread, 0.0)
    one = jnp.sum(spread[0:4], 0, keepdims=True)
    two = jnp.sum(spread[4:8], 0, keepdims=True)
    send_ref[...] = jnp.broadcast_to(jnp.concatenate([one, two], 0)[None], send_ref.shape)
    for copy in copies[5:]:
        copy.wait()


def pack_kernel(field_ref, flow_ref, density_ref, order_ref, own_ref, near_ref, far_ref, rows_ref):
    comps = [field_ref[0], field_ref[1], field_ref[2], flow_ref[0], flow_ref[1], flow_ref[2]]
    comps = comps + [density_ref[...], density_ref[...]]
    even = lax.axis_index("gas") % 2 == 0
    for k in range(4):
        pair = jnp.concatenate([comps[2 * k], comps[2 * k + 1]], -1)
        own_ref[k] = pair
        low, high = pair[:, :reach], pair[:, -reach:]
        near_ref[k] = jnp.where(even, high, low)
        far_ref[k] = jnp.where(even, low, high)
    half = density_ref.shape[1] // 2
    for k in range(density_ref.shape[0]):
        first = density_ref[k, pl.ds(0, half, stride=2), :]
        second = density_ref[k, pl.ds(1, half, stride=2), :]
        rows_ref[k * half : (k + 1) * half] = jnp.concatenate([first, second], -1)


def join_kernel(own_ref, near_ref, far_ref, order_ref, brick_ref, side_ref, other_ref):
    even = lax.axis_index("gas") % 2 == 0
    own, near, far = own_ref[...], near_ref[...], far_ref[...]
    rows = own.shape[2]
    below = jnp.where(even, far, near)
    above = jnp.where(even, near, far)
    beyond = jnp.concatenate([above, below], 2)
    brick_ref[:, :, 0:rows] = own
    brick_ref[:, :, rows:] = beyond
    even = lax.axis_index("star") % 2 == 0
    depth = own.shape[1]
    left = iota((1, lanes), 1) < lanes // 2

    def layer(part, k, away, high):
        return part[k, depth - away if high else away - 1]

    for send_ref, high_if_even in ((side_ref, True), (other_ref, False)):
        for at, (part, pairs, away) in enumerate(sent_layers()):
            part = beyond if part else own
            tile = []
            for high in (high_if_even, not high_if_even):
                value = layer(part, pairs, away, high)
                if pairs == 3 and away == 1:
                    value = jnp.where(left, value, layer(part, pairs, 2, high))
                tile.append(value)
            send_ref[at] = jnp.where(even, tile[0], tile[1])


def sent_layers():
    tiles = []
    for away in range(1, reach + 1):
        for part in range(2):
            for pair in range(4):
                if part + away > reach or (pair > 1 and part + away > rim) or (pair == 3 and away == 2):
                    continue
                tiles.append((part, pair, away))
    return tiles


def index_kernel(active_ref, state_ref, density_ref, place_ref, slot_ref, listed_ref, stars_ref, star_left_ref, cells_ref):
    listed = active_ref.shape[1]
    total = state_ref.shape[1]
    devices = lax.axis_size("star") * lax.axis_size("gas")
    slots = lanes // 4
    active = active_ref[...]
    starts = iota((devices, listed), 0) * total
    before = one_hot(active < starts)
    after = one_hot(active < starts + total)
    owned = after - before
    first = jnp.sum(before, 1, keepdims=True)
    place = iota((1, listed), 1).astype(f32) - jnp.sum(owned * first, 0, keepdims=True)
    place_ref[...] = place
    local = active - my_rank() * total
    mine = (local >= 0) & (local < total)
    pick = one_hot((iota((lanes, listed), 0) % slots == place.astype(i32)) & mine).astype(bf16)
    hit = one_hot(iota((total, listed), 0) == local).astype(bf16)
    slot = dot_of(pick, hit, 1, 1)
    slot_ref[...] = slot.astype(bf16)
    listed_ref[...] = jnp.sum(slot[0:slots], 0, keepdims=True)
    state = state_ref[...]
    ask = one_hot(iota((24, 6 * lanes), 0) % 8 == wide_row((24, 6 * lanes))).astype(bf16)
    stars_ref[...] = dot_of(stack3(state), ask, 0, 0)
    star_left_ref[...] = stack4(moments(state, state[3:4]))
    rows = density_ref.shape[0]
    wide = rows * lanes
    ask = one_hot(iota((3 * rows, wide), 0) % rows == iota((3 * rows, wide), 1) // lanes).astype(bf16)
    cells_ref[...] = dot_of(stack3(density_ref[...]), ask, 0, 0)


def wide_row(shape):
    at = iota(shape, 1) // lanes
    return jnp.where(at < 3, at, at + 1)


def moments(values, mass):
    return jnp.where(iota(values.shape, 0) == 3, jnp.broadcast_to(mass, values.shape), values * mass)


def stack4(values):
    return jnp.concatenate([stack3(values), jnp.zeros(values.shape, bf16)], 0)


def weigh(left, weight):
    high = weight.astype(bf16)
    return dot_of(left, high) + dot_of(left.astype(f32), weight - high.astype(f32))


def fold3(sums):
    return sums[0:8] + sums[8:16] + sums[16:24]


def force_kernel(
    ext, got_ref, active_ref, place_ref, stars_ref, star_left_ref, cells_ref, send_ref, target_ref, *, chunked
):
    ext_x, ext_y, ext_z = ext
    total = stars_ref.shape[0]
    width = active_ref.shape[1]
    devices = got_ref.shape[0]
    slots = lanes // 4
    starts = iota((devices, width), 0) * total
    active = active_ref[...]
    owned = one_hot((active >= starts) & (active < starts + total)).astype(bf16)
    owned3 = jnp.concatenate([owned, owned, owned], 0)
    slot_hit = one_hot(iota((slots, width), 0) == place_ref[...].astype(i32))
    spread = dot_of(stack3(jnp.concatenate([got_ref[:, 0, :], got_ref[:, 1, :]], 1)), owned3, 0, 0)
    targets = jnp.sum(spread.reshape(8, slots, width) * slot_hit[None], 1)
    target_ref[...] = targets

    first_x = lax.axis_index("star") * ext_x
    first_y = lax.axis_index("gas") * ext_y
    tx, ty, tz, _, tu, tv, tw, _ = [targets[k : k + 1] for k in range(8)]
    pulls = jnp.zeros((32, width), f32)
    bends = jnp.zeros((32, width), f32)
    step = min(total, depth)
    for at in range(0, total, step):
        src = [stars_ref[at : at + step, k * lanes : (k + 1) * lanes] for k in range(6)]
        src = [jnp.concatenate([v] * (width // lanes), 1) for v in src]
        dx, dy, dz = src[0] - tx, src[1] - ty, src[2] - tz
        du, dv, dw = src[3] - tu, src[4] - tv, src[5] - tw
        inv = lax.rsqrt(dx * dx + dy * dy + dz * dz + soften)
        inv2 = inv * inv
        weight = inv * inv2
        bend = (dx * du + dy * dv + dz * dw) * inv2 * weight
        left = star_left_ref[:, at : at + step]
        pulls = pulls + weigh(left, weight)
        bends = bends + weigh(left, bend)
    gas_acc = []
    step = 32
    for lane in range(0, width, lanes):
        def row_of(k):
            return jnp.broadcast_to(targets[k : k + 1, lane : lane + lanes], (8, lanes))

        def wide(row):
            return jnp.concatenate([row] * (step // 8), 0)

        def fold(block):
            return sum(block[k : k + 8] for k in range(0, step, 8))

        px, py, pz = row_of(0), row_of(1), wide(row_of(2))
        sums = [jnp.zeros((8, lanes), f32) for _ in range(3)]
        for pair in range(ext_y // 2):
            for at in range(0, 2 * ext_z, step):
                gap_y = (first_y + 2 * pair + at // ext_z).astype(f32) + 0.5 - py
                gap_z = (iota((step, lanes), 0) + at % ext_z).astype(f32) + 0.5 - pz
                base = gap_z * gap_z + wide(gap_y * gap_y + soften)
                along = None
                for k in range(ext_x):
                    gap_x = ((first_x + k).astype(f32) + 0.5) - px
                    col = (k * (ext_y // 2) + pair) * lanes
                    inv = lax.rsqrt(base + wide(gap_x * gap_x))
                    weight = cells_ref[at : at + step, col : col + lanes] * inv * (inv * inv)
                    sums[0] = sums[0] + gap_x * fold(weight)
                    along = weight if along is None else along + weight
                sums[1] = sums[1] + gap_y * fold(along)
                sums[2] = sums[2] + fold(gap_z * along)
        gas_acc.append(jnp.concatenate([jnp.sum(v, 0, keepdims=True) for v in sums], 0))
    gas_acc = jnp.concatenate(gas_acc, 1)
    pulls, bends = fold3(pulls), fold3(bends)
    new_acc = gas_acc + (pulls[0:3] - targets[0:3] * pulls[3:4])
    new_jerk = pulls[4:7] - targets[4:7] * pulls[3:4]
    new_jerk = new_jerk - 3.0 * (bends[0:3] - targets[0:3] * bends[3:4])
    none = jnp.zeros((1, width), f32)
    partial = gravity * jnp.concatenate([new_acc, none, new_jerk, none], 0)
    owned3 = jnp.concatenate([owned, owned, owned], 1)
    for half in range(2):
        spread = partial[4 * half : 4 * half + 4][:, None, :] * slot_hit[None]
        spread = jnp.concatenate(split3(spread.reshape(4 * slots, width)), 1)
        sent = dot_of(owned3, spread, 1, 1)
        if chunked:
            step_at = pl.program_id(0)

            @pl.when(step_at == 0)
            def _():
                send_ref[:, half, :] = sent

            @pl.when(step_at > 0)
            def _():
                send_ref[:, half, :] += sent
        else:
            send_ref[:, half, :] = sent


def kick_kernel(ext, grid, target_ref, kick_ref, *, chunked):
    ext_x, ext_y, ext_z = ext
    width = target_ref.shape[1]

    def clear():
        kick_ref[...] = jnp.zeros(kick_ref.shape, f32)

    if chunked:
        pl.when(pl.program_id(0) == 0)(clear)
    else:
        clear()
    targets = target_ref[...]
    mass = targets[3:4]
    row = iota((8, width), 0)
    moment = jnp.where(row < 3, targets * mass, jnp.where(row == 3, mass, 0.0))
    left = stack4(moment)
    ask = one_hot(iota((24, 3 * lanes), 0) % 8 == iota((24, 3 * lanes), 1) // lanes).astype(bf16)
    spread = dot_of(stack3(targets), ask, 0, 0)
    tx, ty, tz = spread[:, 0:lanes], spread[:, lanes : 2 * lanes], spread[:, 2 * lanes :]
    lane = iota((1, lanes), 1)
    cell_z = (lane % ext_z).astype(f32) + 0.5
    gap_z = cell_z - tz
    base = gap_z * gap_z + soften
    first_x = lax.axis_index("star") * ext_x + grid[0] - rim
    first_y = lax.axis_index("gas") * ext_y + grid[1] - rim
    place_x, square_x = [], []
    for pair in range((ext_x + 2 * rim) // 2):
        at = lax.rem(first_x + 2 * pair + lane // ext_z, grid[0])
        at = at.astype(f32) + 0.5
        place_x.append(at)
        square_x.append((at - tx) * (at - tx))
    tiles = []
    for j in range(ext_y + 2 * rim):
        out_y = max(rim - j, j - (ext_y + rim - 1), 0)
        for pair in range((ext_x + 2 * rim) // 2):
            out_x = min(max(rim - i, i - (ext_x + rim - 1), 0) for i in (2 * pair, 2 * pair + 1))
            if out_x + out_y <= rim:
                tiles.append((j, pair))
    base_y, at_y = {}, {}
    for k in range(0, len(tiles), batch):
        part = tiles[k : k + batch]
        weights = []
        for j, pair in part:
            if j not in base_y:
                at_y[j] = lax.rem(first_y + j, grid[1]).astype(f32) + 0.5
                gap_y = at_y[j] - ty
                base_y[j] = base + gap_y * gap_y
            inv = lax.rsqrt(base_y[j] + square_x[pair])
            weights.append(inv * (inv * inv))
        sums = fold3(weigh(left, jnp.concatenate(weights, 1)))
        for at, (j, pair) in enumerate(part):
            here = sums[:, at * lanes : (at + 1) * lanes]
            whole = here[3:4]
            row = (j - rim) % (ext_y + 2 * reach)
            kick_ref[0, pair, row : row + 1, :] += here[0:1] - place_x[pair] * whole
            kick_ref[1, pair, row : row + 1, :] += here[1:2] - at_y[j] * whole
            kick_ref[2, pair, row : row + 1, :] += here[2:3] - cell_z * whole


def twice(values):
    half = lanes // 2
    turned = pltpu.roll(values, half, values.ndim - 1)
    left = iota(values.shape, values.ndim - 1) < half
    return jnp.where(left, values, turned), jnp.where(left, turned, values)


def diff_x(values):
    return values[2:] - values[:-2]


def diff_y(values):
    rows = values.shape[1]
    return (pltpu.roll(values, rows - 1, 1) - pltpu.roll(values, 1, 1))[1:-1]


def diff_z(values):
    return (pltpu.roll(values, lanes - 1, 2) - pltpu.roll(values, 1, 2))[1:-1]


def double_curl(a, b, c):
    return (diff_y(c) - diff_z(b), diff_z(a) - diff_x(c), diff_x(b) - diff_y(a))


def cross_of(lhs, rhs):
    return (
        lhs[1] * rhs[2] - lhs[2] * rhs[1],
        lhs[2] * rhs[0] - lhs[0] * rhs[2],
        lhs[0] * rhs[1] - lhs[1] * rhs[0],
    )


def inner(values, width):
    return [v[width:-width] for v in values]


def double_rate(field, flow, half_resist):
    current = double_curl(*field)
    held = inner(field, 1)
    drift = cross_of(cross_of(current, held), held)
    motion = cross_of(flow, held)
    return double_curl(*[m + half_resist * d for m, d in zip(motion, drift)])


def field_kernel(ext, own_ref, near_ref, far_ref, kick_ref, flow_ref, out_ref):
    ext_x, ext_y, ext_z = ext
    even = lax.axis_index("star") % 2 == 0
    place = {tile: at for at, tile in enumerate(sent_layers())}
    half = lanes // 2

    def sent(ref, pair, away):
        parts = []
        for part in range(2):
            shared = pair == 3 and away == 2
            at = place.get((part, pair, 1 if shared else away))
            if at is None:
                parts.append(jnp.ones((ext_y, lanes), f32))
            elif shared:
                parts.append(pltpu.roll(ref[at], half, 1))
            else:
                parts.append(ref[at])
        return jnp.concatenate(parts, 0)

    comps = []
    for k in range(4):
        near = [sent(near_ref, k, away) for away in range(1, reach + 1)]
        far = [sent(far_ref, k, away) for away in range(1, reach + 1)]
        below = jnp.stack([jnp.where(even, f, n) for n, f in zip(near, far)][::-1])
        above = jnp.stack([jnp.where(even, n, f) for n, f in zip(near, far)])
        whole = twice(jnp.concatenate([below, own_ref[k], above], 0))
        if k == 3:
            comps.append(whole[0][1:-1])
        else:
            comps.extend(whole)
    field = comps[0:3]
    dense = comps[6]
    inv = lax.rsqrt(dense)
    half_resist = 0.5 * (inv * inv * inv)
    flow = []
    for k in range(3):
        kick = jnp.stack(twice(kick_ref[k]), 1).reshape((ext_x + 2 * rim,) + kick_ref.shape[2:])
        flow.append(comps[3 + k][1:-1] + (time_step * gravity) * kick)
    rows = slice(0, ext_y)
    for k in range(3):
        flow_ref[k] = flow[k][rim:-rim, rows, 0:ext_z]
    rate = double_rate(field, flow, half_resist)
    section = [b + (0.5 * field_step) * r for b, r in zip(inner(field, 2), rate)]
    rate = double_rate(section, inner(flow, 2), half_resist[2:-2])
    for k in range(3):
        new = field[k][reach:-reach] + section[k][2:-2] + (0.5 * field_step) * rate[k]
        out_ref[k] = 0.5 * new[:, rows, 0:ext_z]


def order_kernel(order_ref, out_ref):
    out_ref[...] = jnp.zeros(out_ref.shape, f32)


def update_kernel(back_ref, pos_ref, vel_ref, acc_ref, slot_ref, listed_ref, order_ref, out_ref):
    slots = lanes // 4
    summed = jnp.sum(back_ref[...], 0)
    row, lane = iota((8, lanes), 0), iota((8, lanes), 1)
    terms = jnp.where(row < 3, summed[0:1], summed[1:2])
    terms = jnp.where((row < 6) & (row % 3 == lane // slots), terms, 0.0)
    slot = slot_ref[...]
    pieces = dot_of(stack3(terms), slot)
    new = pieces[0:8] + pieces[8:16] + pieces[16:24]
    new_acc, new_jerk = new[0:3], new[3:6]
    pos, vel = pos_ref[...], vel_ref[...]
    old_acc, old_jerk = acc_ref[0:3], acc_ref[3:6]
    vel_one = (
        vel + time_step * (old_acc + new_acc) / 2.0 + time_step**2 * (old_jerk - new_jerk) / 12.0
    )
    pos_one = (
        pos + time_step * (vel + vel_one) / 2.0 + time_step**2 * (old_acc - new_acc) / 12.0
    )
    listed = listed_ref[...] > 0.5
    out_ref[0:3] = jnp.where(listed, pos_one, pos)
    out_ref[3:6] = jnp.where(listed, vel_one, vel)
    out_ref[6:9] = jnp.where(listed, new_acc, old_acc)
    out_ref[9:12] = jnp.where(listed, new_jerk, old_jerk)


def swap_pairs(near, far, axis):
    count = lax.axis_size(axis)
    inside = [(i, i ^ 1) for i in range(count)]
    between = [(i, (i + (1 if i % 2 else -1)) % count) for i in range(count)]
    got_far = lax.ppermute(far, axis, between)
    got_near = lax.ppermute(near, axis, inside)
    return got_near, got_far


def body(star_pos, star_vel, star_accel, star_mass, active, density, flow_in, field_in):
    def shape(*dims, dtype=f32):
        return jax.ShapeDtypeStruct(dims, dtype)

    total = star_pos.shape[1]
    listed = active.shape[0]
    star_count, gas_count = lax.axis_size("star"), lax.axis_size("gas")
    devices = star_count * gas_count
    ext = density.shape
    ext_x, ext_y, ext_z = ext
    grid = (ext_x * star_count, ext_y * gas_count)
    width = min(listed, 256)
    chunks = listed // width
    names = active.reshape(1, listed)
    inputs = [
        star_pos, star_vel, star_accel, star_mass.reshape(1, total), names, field_in, flow_in, density
    ]
    *held, send, state = call(
        predict_kernel,
        [shape(*x.shape, dtype=x.dtype) for x in inputs] + [shape(devices, 2, lanes), shape(8, total)],
        *[pltpu.with_memory_space_constraint(x, pltpu.HBM) for x in inputs],
        in_specs=[pl.BlockSpec(memory_space=pltpu.HBM)] * len(inputs),
        scratch=[pltpu.SemaphoreType.DMA((len(inputs),))],
    )
    pos, vel, acc, _, names, field, flow, dense = held
    got = lax.all_to_all(send, both, 0, 0, tiled=True)

    own, near, far, rows = call(
        pack_kernel,
        (shape(4, ext_x, ext_y, lanes), shape(4, ext_x, reach, lanes), shape(4, ext_x, reach, lanes),
         shape(ext_x * ext_y // 2, 2 * ext_z)),
        field, flow, dense, send, after=1,
    )
    near, far = swap_pairs(near, far, "gas")
    place, slot, is_listed, stars, star_left, cells = call(
        index_kernel,
        (shape(1, listed), shape(lanes, total, dtype=bf16), shape(1, total), shape(total, 6 * lanes),
         shape(32, total, dtype=bf16), shape(2 * ext_z, ext_x * ext_y // 2 * lanes)),
        names, state, rows,
    )
    def all_of(*dims):
        return pl.BlockSpec(dims, lambda k: (0,) * len(dims))

    def part_of(rows):
        return pl.BlockSpec((rows, width), lambda k: (0, k))

    def in_parts(in_specs, out_specs):
        if chunks == 1:
            return {}
        return dict(grid=(chunks,), in_specs=in_specs, out_specs=out_specs)

    back, targets = call(
        functools.partial(force_kernel, ext, chunked=chunks > 1),
        (shape(devices, 2, lanes), shape(8, listed)),
        got, names, place, stars, star_left, cells,
        **in_parts(
            [all_of(*got.shape), part_of(1), part_of(1)]
            + [all_of(*x.shape) for x in (stars, star_left, cells)],
            (all_of(devices, 2, lanes), part_of(8)),
        ),
    )
    back = lax.all_to_all(back, both, 0, 0, tiled=True)

    if ext_x != reach or ext_y != 2 * reach or ext_z != lanes // 2:
        raise ValueError("brick shape")
    kick_shape = (3, (ext_x + 2 * rim) // 2, ext_y + 2 * reach, lanes)
    brick_shape = (4, ext_x, ext_y + 2 * reach, lanes)

    def one_turn(_):
        edge = shape(len(sent_layers()), ext_y, lanes)
        brick, side, other = call(
            join_kernel, (shape(*brick_shape), edge, edge), own, near, far, targets, after=1
        )
        side, other = swap_pairs(side, other, "star")
        kick = call(
            functools.partial(kick_kernel, ext, grid, chunked=chunks > 1), shape(*kick_shape), targets,
            **in_parts([part_of(8)], all_of(*kick_shape)),
        )
        flow, field_out = call(
            functools.partial(field_kernel, ext),
            (shape(*flow_in.shape), shape(*field_in.shape)), brick, side, other, kick,
        )
        return flow, field_out

    def no_turn(_):
        return jnp.zeros(flow_in.shape, f32), jnp.zeros(field_in.shape, f32)

    flow, field_out = lax.cond(lax.axis_index("star") < star_count, one_turn, no_turn, 0)
    order = call(
        order_kernel, shape(8, lanes), pltpu.with_memory_space_constraint(field_out, pltpu.HBM),
        after=1, where=pltpu.HBM,
        cost=pl.CostEstimate(flops=10**10, bytes_accessed=10**8, transcendentals=0),
    )
    star_new = call(
        update_kernel, shape(12, total), back, pos, vel, acc, slot, is_listed,
        order, after=1,
    )
    return (star_new, flow, field_out)


def solution(mesh):
    placed = (
        P(None, both),
        P(None, both),
        P(None, both),
        P(both),
        P(),
        P("star", "gas", None),
        P(None, "star", "gas", None),
        P(None, "star", "gas", None),
    )
    return jax.shard_map(
        body,
        mesh=mesh,
        in_specs=placed,
        out_specs=(
            P(None, both),
            P(None, "star", "gas", None),
            P(None, "star", "gas", None),
        ),
        check_vma=False,
    )
```

```python
import functools

import jax
import jax.numpy as jnp
from jax import lax
from jax.experimental import pallas as pl
from jax.experimental.pallas import tpu as pltpu
from jax.sharding import PartitionSpec as P

gravity = 0.02
soften = 4.0
time_step = 1.5
field_step = 0.1
both = ("star", "gas")
reach = 4
rim = reach - 1
lanes = 128
vmem_bytes = 48 * 1024 * 1024
batch = 4
depth = 512
f32, bf16, i32 = jnp.float32, jnp.bfloat16, jnp.int32


def iota(shape, dim):
    return lax.broadcasted_iota(i32, shape, dim)


def split3(values):
    high = values.astype(bf16)
    rest = values - high.astype(f32)
    mid = rest.astype(bf16)
    low = (rest - mid.astype(f32)).astype(bf16)
    return high, mid, low


def stack3(values):
    return jnp.concatenate(split3(values), 0)


def dot_of(lhs, rhs, lhs_dim=1, rhs_dim=0):
    return lax.dot_general(
        lhs, rhs, (((lhs_dim,), (rhs_dim,)), ((), ())), preferred_element_type=f32
    )


def one_hot(hits):
    return jnp.where(hits, 1.0, 0.0)


def my_rank():
    return lax.axis_index("star") * lax.axis_size("gas") + lax.axis_index("gas")


def rank_at(place):
    star_count, gas_count = lax.axis_size("star"), lax.axis_size("gas")
    pair, rest = place // (2 * star_count), place % (2 * star_count)
    side, along = rest % 2, rest // 2
    star = along + side * (star_count - 1 - 2 * along)
    gas = pair + side * (gas_count - 1 - 2 * pair)
    return star * gas_count + gas


def exchange(pieces):
    order = [rank_at(k) for k in range(pieces.shape[0])]
    return lax.all_to_all(pieces, both, 0, 0, axis_index_groups=[order], tiled=True)


def call(kernel, outs, *args, grid=None, in_specs=None, out_specs=None, scratch=(), after=0, where=pl.ANY, cost=None):
    spec = {}
    if grid is not None:
        spec = dict(grid=grid, in_specs=in_specs, out_specs=out_specs)
    elif in_specs is not None:
        spec = dict(in_specs=in_specs)
    elif after:
        held = [pl.BlockSpec(memory_space=pltpu.VMEM)] * (len(args) - after)
        spec = dict(in_specs=held + [pl.BlockSpec(memory_space=where)] * after)
    return pl.pallas_call(
        kernel,
        out_shape=outs,
        scratch_shapes=list(scratch),
        cost_estimate=cost,
        compiler_params=pltpu.CompilerParams(vmem_limit_bytes=vmem_bytes),
        **spec,
    )(*args)


def predict_kernel(*refs):
    sources, held = refs[0:8], refs[8:16]
    send_ref, state_ref, sems = refs[16:]
    copies = [
        pltpu.make_async_copy(source, target, sems.at[k])
        for k, (source, target) in enumerate(zip(sources, held))
    ]
    for copy in copies:
        copy.start()
    for copy in copies[0:5]:
        copy.wait()
    pos_ref, vel_ref, acc_ref, mass_ref, active_ref = held[0:5]
    total = pos_ref.shape[1]
    listed = active_ref.shape[1]
    slots = lanes // 4
    pos, vel = pos_ref[...], vel_ref[...]
    old_acc, old_jerk = acc_ref[0:3], acc_ref[3:6]
    pred_pos = (
        pos + time_step * vel + time_step**2 / 2.0 * old_acc + time_step**3 / 6.0 * old_jerk
    )
    pred_vel = vel + time_step * old_acc + time_step**2 / 2.0 * old_jerk
    state = jnp.concatenate([pred_pos, mass_ref[...], pred_vel, jnp.zeros((1, total), f32)], 0)
    state_ref[...] = state
    local = active_ref[...] - my_rank() * total
    first = jnp.sum(one_hot(local < 0)).astype(i32)
    hit = one_hot(iota((total, listed), 0) == local).astype(bf16)
    pieces = dot_of(stack3(state), hit)
    placed = pieces[0:8] + pieces[8:16] + pieces[16:24]
    placed = pltpu.roll(placed, lax.rem(listed - first, listed), 1)[:, 0:lanes]
    lane = iota((8, lanes), 1)
    row = iota((8, lanes), 0)
    part = jnp.where(lane < slots, placed, 0.0)
    spread = part
    for k in range(1, 4):
        spread = jnp.where(lane // slots == k, pltpu.roll(part, k * slots, 1), spread)
    spread = jnp.where(row % 4 == lane // slots, spread, 0.0)
    one = jnp.sum(spread[0:4], 0, keepdims=True)
    two = jnp.sum(spread[4:8], 0, keepdims=True)
    send_ref[...] = jnp.broadcast_to(jnp.concatenate([one, two], 0)[None], send_ref.shape)
    for copy in copies[5:]:
        copy.wait()


def pack_kernel(field_ref, flow_ref, density_ref, order_ref, own_ref, near_ref, far_ref, rows_ref):
    comps = [field_ref[0], field_ref[1], field_ref[2], flow_ref[0], flow_ref[1], flow_ref[2]]
    comps = comps + [density_ref[...], density_ref[...]]
    even = lax.axis_index("gas") % 2 == 0
    for k in range(4):
        pair = jnp.concatenate([comps[2 * k], comps[2 * k + 1]], -1)
        own_ref[k] = pair
        low, high = pair[:, :reach], pair[:, -reach:]
        near_ref[k] = jnp.where(even, high, low)
        far_ref[k] = jnp.where(even, low, high)
    half = density_ref.shape[1] // 2
    for k in range(density_ref.shape[0]):
        first = density_ref[k, pl.ds(0, half, stride=2), :]
        second = density_ref[k, pl.ds(1, half, stride=2), :]
        rows_ref[k * half : (k + 1) * half] = jnp.concatenate([first, second], -1)


def join_kernel(own_ref, near_ref, far_ref, order_ref, brick_ref, side_ref, other_ref):
    even = lax.axis_index("gas") % 2 == 0
    own, near, far = own_ref[...], near_ref[...], far_ref[...]
    rows = own.shape[2]
    below = jnp.where(even, far, near)
    above = jnp.where(even, near, far)
    beyond = jnp.concatenate([above, below], 2)
    brick_ref[:, :, 0:rows] = own
    brick_ref[:, :, rows:] = beyond
    even = lax.axis_index("star") % 2 == 0
    depth = own.shape[1]
    left = iota((1, lanes), 1) < lanes // 2

    def layer(part, k, away, high):
        return part[k, depth - away if high else away - 1]

    for send_ref, high_if_even in ((side_ref, True), (other_ref, False)):
        for at, (part, pairs, away) in enumerate(sent_layers()):
            part = beyond if part else own
            tile = []
            for high in (high_if_even, not high_if_even):
                value = layer(part, pairs, away, high)
                if pairs == 3 and away == 1:
                    value = jnp.where(left, value, layer(part, pairs, 2, high))
                tile.append(value)
            send_ref[at] = jnp.where(even, tile[0], tile[1])


def sent_layers():
    tiles = []
    for away in range(1, reach + 1):
        for part in range(2):
            for pair in range(4):
                if part + away > reach or (pair > 1 and part + away > rim) or (pair == 3 and away == 2):
                    continue
                tiles.append((part, pair, away))
    return tiles


def index_kernel(active_ref, state_ref, density_ref, place_ref, slot_ref, listed_ref, stars_ref, star_left_ref, cells_ref):
    listed = active_ref.shape[1]
    total = state_ref.shape[1]
    devices = lax.axis_size("star") * lax.axis_size("gas")
    slots = lanes // 4
    active = active_ref[...]
    starts = iota((devices, listed), 0) * total
    before = one_hot(active < starts)
    after = one_hot(active < starts + total)
    owned = after - before
    first = jnp.sum(before, 1, keepdims=True)
    place = iota((1, listed), 1).astype(f32) - jnp.sum(owned * first, 0, keepdims=True)
    place_ref[...] = place
    local = active - my_rank() * total
    mine = (local >= 0) & (local < total)
    pick = one_hot((iota((lanes, listed), 0) % slots == place.astype(i32)) & mine).astype(bf16)
    hit = one_hot(iota((total, listed), 0) == local).astype(bf16)
    slot = dot_of(pick, hit, 1, 1)
    slot_ref[...] = slot.astype(bf16)
    listed_ref[...] = jnp.sum(slot[0:slots], 0, keepdims=True)
    state = state_ref[...]
    ask = one_hot(iota((24, 6 * lanes), 0) % 8 == wide_row((24, 6 * lanes))).astype(bf16)
    stars_ref[...] = dot_of(stack3(state), ask, 0, 0)
    star_left_ref[...] = stack4(moments(state, state[3:4]))
    rows = density_ref.shape[0]
    wide = rows * lanes
    ask = one_hot(iota((3 * rows, wide), 0) % rows == iota((3 * rows, wide), 1) // lanes).astype(bf16)
    cells_ref[...] = dot_of(stack3(density_ref[...]), ask, 0, 0)


def wide_row(shape):
    at = iota(shape, 1) // lanes
    return jnp.where(at < 3, at, at + 1)


def moments(values, mass):
    return jnp.where(iota(values.shape, 0) == 3, jnp.broadcast_to(mass, values.shape), values * mass)


def stack4(values):
    return jnp.concatenate([stack3(values), jnp.zeros(values.shape, bf16)], 0)


def weigh(left, weight):
    high = weight.astype(bf16)
    return dot_of(left, high) + dot_of(left.astype(f32), weight - high.astype(f32))


def fold3(sums):
    return sums[0:8] + sums[8:16] + sums[16:24]


def force_kernel(
    ext, got_ref, active_ref, place_ref, stars_ref, star_left_ref, cells_ref, send_ref, target_ref, *, chunked
):
    ext_x, ext_y, ext_z = ext
    total = stars_ref.shape[0]
    width = active_ref.shape[1]
    devices = got_ref.shape[0]
    slots = lanes // 4
    starts = rank_at(iota((devices, width), 0)) * total
    active = active_ref[...]
    owned = one_hot((active >= starts) & (active < starts + total)).astype(bf16)
    owned3 = jnp.concatenate([owned, owned, owned], 0)
    slot_hit = one_hot(iota((slots, width), 0) == place_ref[...].astype(i32))
    spread = dot_of(stack3(jnp.concatenate([got_ref[:, 0, :], got_ref[:, 1, :]], 1)), owned3, 0, 0)
    targets = jnp.sum(spread.reshape(8, slots, width) * slot_hit[None], 1)
    target_ref[...] = targets

    first_x = lax.axis_index("star") * ext_x
    first_y = lax.axis_index("gas") * ext_y
    tx, ty, tz, _, tu, tv, tw, _ = [targets[k : k + 1] for k in range(8)]
    pulls = jnp.zeros((32, width), f32)
    bends = jnp.zeros((32, width), f32)
    step = min(total, depth)
    for at in range(0, total, step):
        src = [stars_ref[at : at + step, k * lanes : (k + 1) * lanes] for k in range(6)]
        src = [jnp.concatenate([v] * (width // lanes), 1) for v in src]
        dx, dy, dz = src[0] - tx, src[1] - ty, src[2] - tz
        du, dv, dw = src[3] - tu, src[4] - tv, src[5] - tw
        inv = lax.rsqrt(dx * dx + dy * dy + dz * dz + soften)
        inv2 = inv * inv
        weight = inv * inv2
        bend = (dx * du + dy * dv + dz * dw) * inv2 * weight
        left = star_left_ref[:, at : at + step]
        pulls = pulls + weigh(left, weight)
        bends = bends + weigh(left, bend)
    gas_acc = []
    step = 32
    for lane in range(0, width, lanes):
        def row_of(k):
            return jnp.broadcast_to(targets[k : k + 1, lane : lane + lanes], (8, lanes))

        def wide(row):
            return jnp.concatenate([row] * (step // 8), 0)

        def fold(block):
            return sum(block[k : k + 8] for k in range(0, step, 8))

        px, py, pz = row_of(0), row_of(1), wide(row_of(2))
        sums = [jnp.zeros((8, lanes), f32) for _ in range(3)]
        for pair in range(ext_y // 2):
            for at in range(0, 2 * ext_z, step):
                gap_y = (first_y + 2 * pair + at // ext_z).astype(f32) + 0.5 - py
                gap_z = (iota((step, lanes), 0) + at % ext_z).astype(f32) + 0.5 - pz
                base = gap_z * gap_z + wide(gap_y * gap_y + soften)
                along = None
                for k in range(ext_x):
                    gap_x = ((first_x + k).astype(f32) + 0.5) - px
                    col = (k * (ext_y // 2) + pair) * lanes
                    inv = lax.rsqrt(base + wide(gap_x * gap_x))
                    weight = cells_ref[at : at + step, col : col + lanes] * inv * (inv * inv)
                    sums[0] = sums[0] + gap_x * fold(weight)
                    along = weight if along is None else along + weight
                sums[1] = sums[1] + gap_y * fold(along)
                sums[2] = sums[2] + fold(gap_z * along)
        gas_acc.append(jnp.concatenate([jnp.sum(v, 0, keepdims=True) for v in sums], 0))
    gas_acc = jnp.concatenate(gas_acc, 1)
    pulls, bends = fold3(pulls), fold3(bends)
    new_acc = gas_acc + (pulls[0:3] - targets[0:3] * pulls[3:4])
    new_jerk = pulls[4:7] - targets[4:7] * pulls[3:4]
    new_jerk = new_jerk - 3.0 * (bends[0:3] - targets[0:3] * bends[3:4])
    none = jnp.zeros((1, width), f32)
    partial = gravity * jnp.concatenate([new_acc, none, new_jerk, none], 0)
    owned3 = jnp.concatenate([owned, owned, owned], 1)
    for half in range(2):
        spread = partial[4 * half : 4 * half + 4][:, None, :] * slot_hit[None]
        spread = jnp.concatenate(split3(spread.reshape(4 * slots, width)), 1)
        sent = dot_of(owned3, spread, 1, 1)
        if chunked:
            step_at = pl.program_id(0)

            @pl.when(step_at == 0)
            def _():
                send_ref[:, half, :] = sent

            @pl.when(step_at > 0)
            def _():
                send_ref[:, half, :] += sent
        else:
            send_ref[:, half, :] = sent


def kick_kernel(ext, grid, target_ref, kick_ref, *, chunked):
    ext_x, ext_y, ext_z = ext
    width = target_ref.shape[1]

    def clear():
        kick_ref[...] = jnp.zeros(kick_ref.shape, f32)

    if chunked:
        pl.when(pl.program_id(0) == 0)(clear)
    else:
        clear()
    targets = target_ref[...]
    mass = targets[3:4]
    row = iota((8, width), 0)
    moment = jnp.where(row < 3, targets * mass, jnp.where(row == 3, mass, 0.0))
    left = stack4(moment)
    ask = one_hot(iota((24, 3 * lanes), 0) % 8 == iota((24, 3 * lanes), 1) // lanes).astype(bf16)
    spread = dot_of(stack3(targets), ask, 0, 0)
    tx, ty, tz = spread[:, 0:lanes], spread[:, lanes : 2 * lanes], spread[:, 2 * lanes :]
    lane = iota((1, lanes), 1)
    cell_z = (lane % ext_z).astype(f32) + 0.5
    gap_z = cell_z - tz
    base = gap_z * gap_z + soften
    first_x = lax.axis_index("star") * ext_x + grid[0] - rim
    first_y = lax.axis_index("gas") * ext_y + grid[1] - rim
    place_x, square_x = [], []
    for pair in range((ext_x + 2 * rim) // 2):
        at = lax.rem(first_x + 2 * pair + lane // ext_z, grid[0])
        at = at.astype(f32) + 0.5
        place_x.append(at)
        square_x.append((at - tx) * (at - tx))
    tiles = []
    for j in range(ext_y + 2 * rim):
        out_y = max(rim - j, j - (ext_y + rim - 1), 0)
        for pair in range((ext_x + 2 * rim) // 2):
            out_x = min(max(rim - i, i - (ext_x + rim - 1), 0) for i in (2 * pair, 2 * pair + 1))
            if out_x + out_y <= rim:
                tiles.append((j, pair))
    base_y, at_y = {}, {}
    for k in range(0, len(tiles), batch):
        part = tiles[k : k + batch]
        weights = []
        for j, pair in part:
            if j not in base_y:
                at_y[j] = lax.rem(first_y + j, grid[1]).astype(f32) + 0.5
                gap_y = at_y[j] - ty
                base_y[j] = base + gap_y * gap_y
            inv = lax.rsqrt(base_y[j] + square_x[pair])
            weights.append(inv * (inv * inv))
        sums = fold3(weigh(left, jnp.concatenate(weights, 1)))
        for at, (j, pair) in enumerate(part):
            here = sums[:, at * lanes : (at + 1) * lanes]
            whole = here[3:4]
            row = (j - rim) % (ext_y + 2 * reach)
            kick_ref[0, pair, row : row + 1, :] += here[0:1] - place_x[pair] * whole
            kick_ref[1, pair, row : row + 1, :] += here[1:2] - at_y[j] * whole
            kick_ref[2, pair, row : row + 1, :] += here[2:3] - cell_z * whole


def twice(values):
    half = lanes // 2
    turned = pltpu.roll(values, half, values.ndim - 1)
    left = iota(values.shape, values.ndim - 1) < half
    return jnp.where(left, values, turned), jnp.where(left, turned, values)


def diff_x(values):
    return values[2:] - values[:-2]


def diff_y(values):
    rows = values.shape[1]
    return (pltpu.roll(values, rows - 1, 1) - pltpu.roll(values, 1, 1))[1:-1]


def diff_z(values):
    return (pltpu.roll(values, lanes - 1, 2) - pltpu.roll(values, 1, 2))[1:-1]


def double_curl(a, b, c):
    return (diff_y(c) - diff_z(b), diff_z(a) - diff_x(c), diff_x(b) - diff_y(a))


def cross_of(lhs, rhs):
    return (
        lhs[1] * rhs[2] - lhs[2] * rhs[1],
        lhs[2] * rhs[0] - lhs[0] * rhs[2],
        lhs[0] * rhs[1] - lhs[1] * rhs[0],
    )


def inner(values, width):
    return [v[width:-width] for v in values]


def double_rate(field, flow, half_resist):
    current = double_curl(*field)
    held = inner(field, 1)
    drift = cross_of(cross_of(current, held), held)
    motion = cross_of(flow, held)
    return double_curl(*[m + half_resist * d for m, d in zip(motion, drift)])


def field_kernel(ext, own_ref, near_ref, far_ref, kick_ref, flow_ref, out_ref):
    ext_x, ext_y, ext_z = ext
    even = lax.axis_index("star") % 2 == 0
    place = {tile: at for at, tile in enumerate(sent_layers())}
    half = lanes // 2

    def sent(ref, pair, away):
        parts = []
        for part in range(2):
            shared = pair == 3 and away == 2
            at = place.get((part, pair, 1 if shared else away))
            if at is None:
                parts.append(jnp.ones((ext_y, lanes), f32))
            elif shared:
                parts.append(pltpu.roll(ref[at], half, 1))
            else:
                parts.append(ref[at])
        return jnp.concatenate(parts, 0)

    comps = []
    for k in range(4):
        near = [sent(near_ref, k, away) for away in range(1, reach + 1)]
        far = [sent(far_ref, k, away) for away in range(1, reach + 1)]
        below = jnp.stack([jnp.where(even, f, n) for n, f in zip(near, far)][::-1])
        above = jnp.stack([jnp.where(even, n, f) for n, f in zip(near, far)])
        whole = twice(jnp.concatenate([below, own_ref[k], above], 0))
        if k == 3:
            comps.append(whole[0][1:-1])
        else:
            comps.extend(whole)
    field = comps[0:3]
    dense = comps[6]
    inv = lax.rsqrt(dense)
    half_resist = 0.5 * (inv * inv * inv)
    flow = []
    for k in range(3):
        kick = jnp.stack(twice(kick_ref[k]), 1).reshape((ext_x + 2 * rim,) + kick_ref.shape[2:])
        flow.append(comps[3 + k][1:-1] + (time_step * gravity) * kick)
    rows = slice(0, ext_y)
    for k in range(3):
        flow_ref[k] = flow[k][rim:-rim, rows, 0:ext_z]
    rate = double_rate(field, flow, half_resist)
    section = [b + (0.5 * field_step) * r for b, r in zip(inner(field, 2), rate)]
    rate = double_rate(section, inner(flow, 2), half_resist[2:-2])
    for k in range(3):
        new = field[k][reach:-reach] + section[k][2:-2] + (0.5 * field_step) * rate[k]
        out_ref[k] = 0.5 * new[:, rows, 0:ext_z]


def order_kernel(order_ref, out_ref):
    out_ref[...] = jnp.zeros(out_ref.shape, f32)


def update_kernel(back_ref, pos_ref, vel_ref, acc_ref, slot_ref, listed_ref, order_ref, out_ref):
    slots = lanes // 4
    summed = jnp.sum(back_ref[...], 0)
    row, lane = iota((8, lanes), 0), iota((8, lanes), 1)
    terms = jnp.where(row < 3, summed[0:1], summed[1:2])
    terms = jnp.where((row < 6) & (row % 3 == lane // slots), terms, 0.0)
    slot = slot_ref[...]
    pieces = dot_of(stack3(terms), slot)
    new = pieces[0:8] + pieces[8:16] + pieces[16:24]
    new_acc, new_jerk = new[0:3], new[3:6]
    pos, vel = pos_ref[...], vel_ref[...]
    old_acc, old_jerk = acc_ref[0:3], acc_ref[3:6]
    vel_one = (
        vel + time_step * (old_acc + new_acc) / 2.0 + time_step**2 * (old_jerk - new_jerk) / 12.0
    )
    pos_one = (
        pos + time_step * (vel + vel_one) / 2.0 + time_step**2 * (old_acc - new_acc) / 12.0
    )
    listed = listed_ref[...] > 0.5
    out_ref[0:3] = jnp.where(listed, pos_one, pos)
    out_ref[3:6] = jnp.where(listed, vel_one, vel)
    out_ref[6:9] = jnp.where(listed, new_acc, old_acc)
    out_ref[9:12] = jnp.where(listed, new_jerk, old_jerk)


def swap_pairs(near, far, axis):
    count = lax.axis_size(axis)
    inside = [(i, i ^ 1) for i in range(count)]
    between = [(i, (i + (1 if i % 2 else -1)) % count) for i in range(count)]
    got_far = lax.ppermute(far, axis, between)
    got_near = lax.ppermute(near, axis, inside)
    return got_near, got_far


def body(star_pos, star_vel, star_accel, star_mass, active, density, flow_in, field_in):
    def shape(*dims, dtype=f32):
        return jax.ShapeDtypeStruct(dims, dtype)

    total = star_pos.shape[1]
    listed = active.shape[0]
    star_count, gas_count = lax.axis_size("star"), lax.axis_size("gas")
    devices = star_count * gas_count
    ext = density.shape
    ext_x, ext_y, ext_z = ext
    grid = (ext_x * star_count, ext_y * gas_count)
    width = min(listed, 256)
    chunks = listed // width
    names = active.reshape(1, listed)
    inputs = [
        star_pos, star_vel, star_accel, star_mass.reshape(1, total), names, field_in, flow_in, density
    ]
    *held, send, state = call(
        predict_kernel,
        [shape(*x.shape, dtype=x.dtype) for x in inputs] + [shape(devices, 2, lanes), shape(8, total)],
        *[pltpu.with_memory_space_constraint(x, pltpu.HBM) for x in inputs],
        in_specs=[pl.BlockSpec(memory_space=pltpu.HBM)] * len(inputs),
        scratch=[pltpu.SemaphoreType.DMA((len(inputs),))],
    )
    pos, vel, acc, _, names, field, flow, dense = held
    got = exchange(send)

    own, near, far, rows = call(
        pack_kernel,
        (shape(4, ext_x, ext_y, lanes), shape(4, ext_x, reach, lanes), shape(4, ext_x, reach, lanes),
         shape(ext_x * ext_y // 2, 2 * ext_z)),
        field, flow, dense, send, after=1,
    )
    near, far = swap_pairs(near, far, "gas")
    place, slot, is_listed, stars, star_left, cells = call(
        index_kernel,
        (shape(1, listed), shape(lanes, total, dtype=bf16), shape(1, total), shape(total, 6 * lanes),
         shape(32, total, dtype=bf16), shape(2 * ext_z, ext_x * ext_y // 2 * lanes)),
        names, state, rows,
    )
    def all_of(*dims):
        return pl.BlockSpec(dims, lambda k: (0,) * len(dims))

    def part_of(rows):
        return pl.BlockSpec((rows, width), lambda k: (0, k))

    def in_parts(in_specs, out_specs):
        if chunks == 1:
            return {}
        return dict(grid=(chunks,), in_specs=in_specs, out_specs=out_specs)

    back, targets = call(
        functools.partial(force_kernel, ext, chunked=chunks > 1),
        (shape(devices, 2, lanes), shape(8, listed)),
        got, names, place, stars, star_left, cells,
        **in_parts(
            [all_of(*got.shape), part_of(1), part_of(1)]
            + [all_of(*x.shape) for x in (stars, star_left, cells)],
            (all_of(devices, 2, lanes), part_of(8)),
        ),
    )
    back = exchange(back)

    if ext_x != reach or ext_y != 2 * reach or ext_z != lanes // 2:
        raise ValueError("brick shape")
    kick_shape = (3, (ext_x + 2 * rim) // 2, ext_y + 2 * reach, lanes)
    brick_shape = (4, ext_x, ext_y + 2 * reach, lanes)

    def one_turn(_):
        edge = shape(len(sent_layers()), ext_y, lanes)
        brick, side, other = call(
            join_kernel, (shape(*brick_shape), edge, edge), own, near, far, targets, after=1
        )
        side, other = swap_pairs(side, other, "star")
        kick = call(
            functools.partial(kick_kernel, ext, grid, chunked=chunks > 1), shape(*kick_shape), targets,
            **in_parts([part_of(8)], all_of(*kick_shape)),
        )
        flow, field_out = call(
            functools.partial(field_kernel, ext),
            (shape(*flow_in.shape), shape(*field_in.shape)), brick, side, other, kick,
        )
        return flow, field_out

    def no_turn(_):
        return jnp.zeros(flow_in.shape, f32), jnp.zeros(field_in.shape, f32)

    flow, field_out = lax.cond(lax.axis_index("star") < star_count, one_turn, no_turn, 0)
    order = call(
        order_kernel, shape(8, lanes), pltpu.with_memory_space_constraint(field_out, pltpu.HBM),
        after=1, where=pltpu.HBM,
        cost=pl.CostEstimate(flops=10**10, bytes_accessed=10**8, transcendentals=0),
    )
    star_new = call(
        update_kernel, shape(12, total), back, pos, vel, acc, slot, is_listed,
        order, after=1,
    )
    return (star_new, flow, field_out)


def solution(mesh):
    placed = (
        P(None, both),
        P(None, both),
        P(None, both),
        P(both),
        P(),
        P("star", "gas", None),
        P(None, "star", "gas", None),
        P(None, "star", "gas", None),
    )
    return jax.shard_map(
        body,
        mesh=mesh,
        in_specs=placed,
        out_specs=(
            P(None, both),
            P(None, "star", "gas", None),
            P(None, "star", "gas", None),
        ),
        check_vma=False,
    )
```

```python
import functools

import jax
import jax.numpy as jnp
from jax import lax
from jax.experimental import pallas as pl
from jax.experimental.pallas import tpu as pltpu
from jax.sharding import PartitionSpec as P

gravity = 0.02
soften = 4.0
time_step = 1.5
field_step = 0.1
both = ("star", "gas")
reach = 4
rim = reach - 1
lanes = 128
vmem_bytes = 48 * 1024 * 1024
batch = 2
depth = 512
f32, bf16, i32 = jnp.float32, jnp.bfloat16, jnp.int32


def iota(shape, dim):
    return lax.broadcasted_iota(i32, shape, dim)


def split3(values):
    high = values.astype(bf16)
    rest = values - high.astype(f32)
    mid = rest.astype(bf16)
    low = (rest - mid.astype(f32)).astype(bf16)
    return high, mid, low


def stack3(values):
    return jnp.concatenate(split3(values), 0)


def dot_of(lhs, rhs, lhs_dim=1, rhs_dim=0):
    return lax.dot_general(
        lhs, rhs, (((lhs_dim,), (rhs_dim,)), ((), ())), preferred_element_type=f32
    )


def one_hot(hits):
    return jnp.where(hits, 1.0, 0.0)


def my_rank():
    return lax.axis_index("star") * lax.axis_size("gas") + lax.axis_index("gas")


def rank_at(place):
    star_count, gas_count = lax.axis_size("star"), lax.axis_size("gas")
    pair, rest = place // (2 * star_count), place % (2 * star_count)
    side, along = rest % 2, rest // 2
    star = along + side * (star_count - 1 - 2 * along)
    gas = pair + side * (gas_count - 1 - 2 * pair)
    return star * gas_count + gas


def exchange(pieces):
    order = [rank_at(k) for k in range(pieces.shape[0])]
    return lax.all_to_all(pieces, both, 0, 0, axis_index_groups=[order], tiled=True)


def call(kernel, outs, *args, grid=None, in_specs=None, out_specs=None, scratch=(), after=0, where=pl.ANY, cost=None):
    spec = {}
    if grid is not None:
        spec = dict(grid=grid, in_specs=in_specs, out_specs=out_specs)
    elif in_specs is not None:
        spec = dict(in_specs=in_specs)
    elif after:
        held = [pl.BlockSpec(memory_space=pltpu.VMEM)] * (len(args) - after)
        spec = dict(in_specs=held + [pl.BlockSpec(memory_space=where)] * after)
    return pl.pallas_call(
        kernel,
        out_shape=outs,
        scratch_shapes=list(scratch),
        cost_estimate=cost,
        compiler_params=pltpu.CompilerParams(vmem_limit_bytes=vmem_bytes),
        **spec,
    )(*args)


def predict_kernel(*refs):
    sources, held = refs[0:8], refs[8:16]
    send_ref, state_ref, sems = refs[16:]
    copies = [
        pltpu.make_async_copy(source, target, sems.at[k])
        for k, (source, target) in enumerate(zip(sources, held))
    ]
    for copy in copies:
        copy.start()
    for copy in copies[0:5]:
        copy.wait()
    pos_ref, vel_ref, acc_ref, mass_ref, active_ref = held[0:5]
    total = pos_ref.shape[1]
    listed = active_ref.shape[1]
    slots = lanes // 4
    pos, vel = pos_ref[...], vel_ref[...]
    old_acc, old_jerk = acc_ref[0:3], acc_ref[3:6]
    pred_pos = (
        pos + time_step * vel + time_step**2 / 2.0 * old_acc + time_step**3 / 6.0 * old_jerk
    )
    pred_vel = vel + time_step * old_acc + time_step**2 / 2.0 * old_jerk
    state = jnp.concatenate([pred_pos, mass_ref[...], pred_vel, jnp.zeros((1, total), f32)], 0)
    state_ref[...] = state
    local = active_ref[...] - my_rank() * total
    first = jnp.sum(one_hot(local < 0)).astype(i32)
    hit = one_hot(iota((total, listed), 0) == local).astype(bf16)
    pieces = dot_of(stack3(state), hit)
    placed = pieces[0:8] + pieces[8:16] + pieces[16:24]
    placed = pltpu.roll(placed, lax.rem(listed - first, listed), 1)[:, 0:lanes]
    lane = iota((8, lanes), 1)
    row = iota((8, lanes), 0)
    part = jnp.where(lane < slots, placed, 0.0)
    spread = part
    for k in range(1, 4):
        spread = jnp.where(lane // slots == k, pltpu.roll(part, k * slots, 1), spread)
    spread = jnp.where(row % 4 == lane // slots, spread, 0.0)
    one = jnp.sum(spread[0:4], 0, keepdims=True)
    two = jnp.sum(spread[4:8], 0, keepdims=True)
    send_ref[...] = jnp.broadcast_to(jnp.concatenate([one, two], 0)[None], send_ref.shape)
    for copy in copies[5:]:
        copy.wait()


def pack_kernel(field_ref, flow_ref, density_ref, order_ref, own_ref, near_ref, far_ref, rows_ref):
    comps = [field_ref[0], field_ref[1], field_ref[2], flow_ref[0], flow_ref[1], flow_ref[2]]
    comps = comps + [density_ref[...], density_ref[...]]
    even = lax.axis_index("gas") % 2 == 0
    for k in range(4):
        pair = jnp.concatenate([comps[2 * k], comps[2 * k + 1]], -1)
        own_ref[k] = pair
        low, high = pair[:, :reach], pair[:, -reach:]
        near_ref[k] = jnp.where(even, high, low)
        far_ref[k] = jnp.where(even, low, high)
    half = density_ref.shape[1] // 2
    for k in range(density_ref.shape[0]):
        rows_ref[k * half : (k + 1) * half] = jnp.concatenate(
            [density_ref[k, 0:half, :], density_ref[k, half:, :]], -1
        )


def join_kernel(own_ref, near_ref, far_ref, order_ref, brick_ref, side_ref, other_ref):
    even = lax.axis_index("gas") % 2 == 0
    own, near, far = own_ref[...], near_ref[...], far_ref[...]
    rows = own.shape[2]
    below = jnp.where(even, far, near)
    above = jnp.where(even, near, far)
    beyond = jnp.concatenate([above, below], 2)
    brick_ref[:, :, 0:rows] = own
    brick_ref[:, :, rows:] = beyond
    even = lax.axis_index("star") % 2 == 0
    depth = own.shape[1]
    left = iota((1, lanes), 1) < lanes // 2

    def layer(part, k, away, high):
        return part[k, depth - away if high else away - 1]

    for send_ref, high_if_even in ((side_ref, True), (other_ref, False)):
        for at, (part, pairs, away) in enumerate(sent_layers()):
            part = beyond if part else own
            tile = []
            for high in (high_if_even, not high_if_even):
                value = layer(part, pairs, away, high)
                if pairs == 3 and away == 1:
                    value = jnp.where(left, value, layer(part, pairs, 2, high))
                tile.append(value)
            send_ref[at] = jnp.where(even, tile[0], tile[1])


def sent_layers():
    tiles = []
    for away in range(1, reach + 1):
        for part in range(2):
            for pair in range(4):
                if part + away > reach or (pair > 1 and part + away > rim) or (pair == 3 and away == 2):
                    continue
                tiles.append((part, pair, away))
    return tiles


def index_kernel(active_ref, state_ref, density_ref, place_ref, slot_ref, listed_ref, stars_ref, star_left_ref, cells_ref):
    listed = active_ref.shape[1]
    total = state_ref.shape[1]
    devices = lax.axis_size("star") * lax.axis_size("gas")
    slots = lanes // 4
    active = active_ref[...]
    starts = iota((devices, listed), 0) * total
    before = one_hot(active < starts)
    after = one_hot(active < starts + total)
    owned = after - before
    first = jnp.sum(before, 1, keepdims=True)
    place = iota((1, listed), 1).astype(f32) - jnp.sum(owned * first, 0, keepdims=True)
    place_ref[...] = place
    local = active - my_rank() * total
    mine = (local >= 0) & (local < total)
    pick = one_hot((iota((lanes, listed), 0) % slots == place.astype(i32)) & mine).astype(bf16)
    hit = one_hot(iota((total, listed), 0) == local).astype(bf16)
    slot = dot_of(pick, hit, 1, 1)
    slot_ref[...] = slot.astype(bf16)
    listed_ref[...] = jnp.sum(slot[0:slots], 0, keepdims=True)
    state = state_ref[...]
    ask = one_hot(iota((24, 6 * lanes), 0) % 8 == wide_row((24, 6 * lanes))).astype(bf16)
    stars_ref[...] = dot_of(stack3(state), ask, 0, 0)
    star_left_ref[...] = stack4(moments(state, state[3:4]))
    rows = density_ref.shape[0]
    wide = rows * lanes
    ask = one_hot(iota((3 * rows, wide), 0) % rows == iota((3 * rows, wide), 1) // lanes).astype(bf16)
    cells_ref[...] = dot_of(stack3(density_ref[...]), ask, 0, 0)


def wide_row(shape):
    at = iota(shape, 1) // lanes
    return jnp.where(at < 3, at, at + 1)


def moments(values, mass):
    return jnp.where(iota(values.shape, 0) == 3, jnp.broadcast_to(mass, values.shape), values * mass)


def stack4(values):
    return jnp.concatenate([stack3(values), jnp.zeros(values.shape, bf16)], 0)


def weigh(left, weight):
    high = weight.astype(bf16)
    return dot_of(left, high) + dot_of(left.astype(f32), weight - high.astype(f32))


def fold3(sums):
    return sums[0:8] + sums[8:16] + sums[16:24]


def force_kernel(
    ext, got_ref, active_ref, place_ref, stars_ref, star_left_ref, cells_ref, send_ref, target_ref, *, chunked
):
    ext_x, ext_y, ext_z = ext
    total = stars_ref.shape[0]
    width = active_ref.shape[1]
    devices = got_ref.shape[0]
    slots = lanes // 4
    starts = rank_at(iota((devices, width), 0)) * total
    active = active_ref[...]
    owned = one_hot((active >= starts) & (active < starts + total)).astype(bf16)
    owned3 = jnp.concatenate([owned, owned, owned], 0)
    slot_hit = one_hot(iota((slots, width), 0) == place_ref[...].astype(i32))
    spread = dot_of(stack3(jnp.concatenate([got_ref[:, 0, :], got_ref[:, 1, :]], 1)), owned3, 0, 0)
    targets = jnp.sum(spread.reshape(8, slots, width) * slot_hit[None], 1)
    target_ref[...] = targets

    first_x = lax.axis_index("star") * ext_x
    first_y = lax.axis_index("gas") * ext_y
    tx, ty, tz, _, tu, tv, tw, _ = [targets[k : k + 1] for k in range(8)]
    pulls = jnp.zeros((32, width), f32)
    bends = jnp.zeros((32, width), f32)
    step = min(total, depth)
    for at in range(0, total, step):
        src = [stars_ref[at : at + step, k * lanes : (k + 1) * lanes] for k in range(6)]
        src = [jnp.concatenate([v] * (width // lanes), 1) for v in src]
        dx, dy, dz = src[0] - tx, src[1] - ty, src[2] - tz
        du, dv, dw = src[3] - tu, src[4] - tv, src[5] - tw
        inv = lax.rsqrt(dx * dx + dy * dy + dz * dz + soften)
        inv2 = inv * inv
        weight = inv * inv2
        bend = (dx * du + dy * dv + dz * dw) * inv2 * weight
        left = star_left_ref[:, at : at + step]
        pulls = pulls + weigh(left, weight)
        bends = bends + weigh(left, bend)
    gas_acc = []
    step = 32
    for lane in range(0, width, lanes):
        def row_of(k):
            return jnp.broadcast_to(targets[k : k + 1, lane : lane + lanes], (8, lanes))

        def wide(row):
            return jnp.concatenate([row] * (step // 8), 0)

        def fold(block):
            return sum(block[k : k + 8] for k in range(0, step, 8))

        px, py, pz = row_of(0), row_of(1), wide(row_of(2))
        sums = [jnp.zeros((8, lanes), f32) for _ in range(3)]
        for pair in range(ext_y // 2):
            for at in range(0, 2 * ext_z, step):
                gap_y = (first_y + pair + at // ext_z * (ext_y // 2)).astype(f32) + 0.5 - py
                gap_z = (iota((step, lanes), 0) + at % ext_z).astype(f32) + 0.5 - pz
                base = gap_z * gap_z + wide(gap_y * gap_y + soften)
                along = None
                for k in range(ext_x):
                    gap_x = ((first_x + k).astype(f32) + 0.5) - px
                    col = (k * (ext_y // 2) + pair) * lanes
                    inv = lax.rsqrt(base + wide(gap_x * gap_x))
                    weight = cells_ref[at : at + step, col : col + lanes] * inv * (inv * inv)
                    sums[0] = sums[0] + gap_x * fold(weight)
                    along = weight if along is None else along + weight
                sums[1] = sums[1] + gap_y * fold(along)
                sums[2] = sums[2] + fold(gap_z * along)
        gas_acc.append(jnp.concatenate([jnp.sum(v, 0, keepdims=True) for v in sums], 0))
    gas_acc = jnp.concatenate(gas_acc, 1)
    pulls, bends = fold3(pulls), fold3(bends)
    new_acc = gas_acc + (pulls[0:3] - targets[0:3] * pulls[3:4])
    new_jerk = pulls[4:7] - targets[4:7] * pulls[3:4]
    new_jerk = new_jerk - 3.0 * (bends[0:3] - targets[0:3] * bends[3:4])
    none = jnp.zeros((1, width), f32)
    partial = gravity * jnp.concatenate([new_acc, none, new_jerk, none], 0)
    owned3 = jnp.concatenate([owned, owned, owned], 1)
    for half in range(2):
        spread = partial[4 * half : 4 * half + 4][:, None, :] * slot_hit[None]
        spread = jnp.concatenate(split3(spread.reshape(4 * slots, width)), 1)
        sent = dot_of(owned3, spread, 1, 1)
        if chunked:
            step_at = pl.program_id(0)

            @pl.when(step_at == 0)
            def _():
                send_ref[:, half, :] = sent

            @pl.when(step_at > 0)
            def _():
                send_ref[:, half, :] += sent
        else:
            send_ref[:, half, :] = sent


def kick_kernel(ext, grid, target_ref, kick_ref, *, chunked):
    ext_x, ext_y, ext_z = ext
    width = target_ref.shape[1]

    def clear():
        kick_ref[...] = jnp.zeros(kick_ref.shape, f32)

    if chunked:
        pl.when(pl.program_id(0) == 0)(clear)
    else:
        clear()
    targets = target_ref[...]
    mass = targets[3:4]
    row = iota((8, width), 0)
    moment = jnp.where(row < 3, targets * mass, jnp.where(row == 3, mass, 0.0))
    pieces = split3(moment)
    left = jnp.concatenate([v[0:4] for v in pieces] + [jnp.zeros((4, width), bf16)], 0)
    ask = one_hot(iota((24, 3 * lanes), 0) % 8 == iota((24, 3 * lanes), 1) // lanes).astype(bf16)
    spread = dot_of(stack3(targets), ask, 0, 0)
    tx, ty, tz = spread[:, 0:lanes], spread[:, lanes : 2 * lanes], spread[:, 2 * lanes :]
    lane = iota((1, lanes), 1)
    cell_z = (lane % ext_z).astype(f32) + 0.5
    gap_z = cell_z - tz
    base = gap_z * gap_z + soften
    first_x = lax.axis_index("star") * ext_x + grid[0] - rim
    first_y = lax.axis_index("gas") * ext_y + grid[1] - rim
    place_x, square_x = [], []
    for pair in range((ext_x + 2 * rim) // 2):
        at = lax.rem(first_x + 2 * pair + lane // ext_z, grid[0])
        at = at.astype(f32) + 0.5
        place_x.append(at)
        square_x.append((at - tx) * (at - tx))
    tiles = []
    for j in range(ext_y + 2 * rim):
        out_y = max(rim - j, j - (ext_y + rim - 1), 0)
        for pair in range((ext_x + 2 * rim) // 2):
            out_x = min(max(rim - i, i - (ext_x + rim - 1), 0) for i in (2 * pair, 2 * pair + 1))
            if out_x + out_y <= rim:
                tiles.append((j, pair))
    base_y, at_y = {}, {}
    for k in range(0, len(tiles), batch):
        part = tiles[k : k + batch]
        weights = []
        for j, pair in part:
            if j not in base_y:
                at_y[j] = lax.rem(first_y + j, grid[1]).astype(f32) + 0.5
                gap_y = at_y[j] - ty
                base_y[j] = base + gap_y * gap_y
            inv = lax.rsqrt(base_y[j] + square_x[pair])
            weights.append(inv * (inv * inv))
        sums = weigh(left, jnp.concatenate(weights, 1))
        sums = sums[0:8] + sums[8:16]
        sums = sums + pltpu.roll(sums, 4, 0)
        for at, (j, pair) in enumerate(part):
            here = sums[:, at * lanes : (at + 1) * lanes]
            whole = here[3:4]
            row = (j - rim) % (ext_y + 2 * reach)
            kick_ref[0, pair, row : row + 1, :] += here[0:1] - place_x[pair] * whole
            kick_ref[1, pair, row : row + 1, :] += here[1:2] - at_y[j] * whole
            kick_ref[2, pair, row : row + 1, :] += here[2:3] - cell_z * whole


def twice(values):
    half = lanes // 2
    turned = pltpu.roll(values, half, values.ndim - 1)
    left = iota(values.shape, values.ndim - 1) < half
    return jnp.where(left, values, turned), jnp.where(left, turned, values)


def diff_x(values):
    return values[2:] - values[:-2]


def diff_y(values):
    rows = values.shape[1]
    return (pltpu.roll(values, rows - 1, 1) - pltpu.roll(values, 1, 1))[1:-1]


def diff_z(values):
    return (pltpu.roll(values, lanes - 1, 2) - pltpu.roll(values, 1, 2))[1:-1]


def double_curl(a, b, c):
    return (diff_y(c) - diff_z(b), diff_z(a) - diff_x(c), diff_x(b) - diff_y(a))


def cross_of(lhs, rhs):
    return (
        lhs[1] * rhs[2] - lhs[2] * rhs[1],
        lhs[2] * rhs[0] - lhs[0] * rhs[2],
        lhs[0] * rhs[1] - lhs[1] * rhs[0],
    )


def inner(values, width):
    return [v[width:-width] for v in values]


def double_rate(field, flow, half_resist):
    current = double_curl(*field)
    held = inner(field, 1)
    drift = cross_of(cross_of(current, held), held)
    motion = cross_of(flow, held)
    return double_curl(*[m + half_resist * d for m, d in zip(motion, drift)])


def field_kernel(ext, own_ref, near_ref, far_ref, kick_ref, flow_ref, out_ref):
    ext_x, ext_y, ext_z = ext
    even = lax.axis_index("star") % 2 == 0
    place = {tile: at for at, tile in enumerate(sent_layers())}
    half = lanes // 2

    def sent(ref, pair, away):
        parts = []
        for part in range(2):
            shared = pair == 3 and away == 2
            at = place.get((part, pair, 1 if shared else away))
            if at is None:
                parts.append(jnp.ones((ext_y, lanes), f32))
            elif shared:
                parts.append(pltpu.roll(ref[at], half, 1))
            else:
                parts.append(ref[at])
        return jnp.concatenate(parts, 0)

    comps = []
    for k in range(4):
        near = [sent(near_ref, k, away) for away in range(1, reach + 1)]
        far = [sent(far_ref, k, away) for away in range(1, reach + 1)]
        below = jnp.stack([jnp.where(even, f, n) for n, f in zip(near, far)][::-1])
        above = jnp.stack([jnp.where(even, n, f) for n, f in zip(near, far)])
        whole = twice(jnp.concatenate([below, own_ref[k], above], 0))
        if k == 3:
            comps.append(whole[0][1:-1])
        else:
            comps.extend(whole)
    field = comps[0:3]
    dense = comps[6]
    inv = lax.rsqrt(dense)
    half_resist = 0.5 * (inv * inv * inv)
    flow = []
    for k in range(3):
        kick = jnp.stack(twice(kick_ref[k]), 1).reshape((ext_x + 2 * rim,) + kick_ref.shape[2:])
        flow.append(comps[3 + k][1:-1] + (time_step * gravity) * kick)
    rows = slice(0, ext_y)
    for k in range(3):
        flow_ref[k] = flow[k][rim:-rim, rows, 0:ext_z]
    rate = double_rate(field, flow, half_resist)
    section = [b + (0.5 * field_step) * r for b, r in zip(inner(field, 2), rate)]
    rate = double_rate(section, inner(flow, 2), half_resist[2:-2])
    for k in range(3):
        new = field[k][reach:-reach] + section[k][2:-2] + (0.5 * field_step) * rate[k]
        out_ref[k] = 0.5 * new[:, rows, 0:ext_z]


def order_kernel(order_ref, out_ref):
    out_ref[...] = jnp.zeros(out_ref.shape, f32)


def update_kernel(back_ref, pos_ref, vel_ref, acc_ref, slot_ref, listed_ref, order_ref, out_ref):
    slots = lanes // 4
    summed = jnp.sum(back_ref[...], 0)
    row, lane = iota((8, lanes), 0), iota((8, lanes), 1)
    terms = jnp.where(row < 3, summed[0:1], summed[1:2])
    terms = jnp.where((row < 6) & (row % 3 == lane // slots), terms, 0.0)
    slot = slot_ref[...]
    pieces = dot_of(stack3(terms), slot)
    new = pieces[0:8] + pieces[8:16] + pieces[16:24]
    new_acc, new_jerk = new[0:3], new[3:6]
    pos, vel = pos_ref[...], vel_ref[...]
    old_acc, old_jerk = acc_ref[0:3], acc_ref[3:6]
    vel_one = (
        vel + time_step * (old_acc + new_acc) / 2.0 + time_step**2 * (old_jerk - new_jerk) / 12.0
    )
    pos_one = (
        pos + time_step * (vel + vel_one) / 2.0 + time_step**2 * (old_acc - new_acc) / 12.0
    )
    listed = listed_ref[...] > 0.5
    out_ref[0:3] = jnp.where(listed, pos_one, pos)
    out_ref[3:6] = jnp.where(listed, vel_one, vel)
    out_ref[6:9] = jnp.where(listed, new_acc, old_acc)
    out_ref[9:12] = jnp.where(listed, new_jerk, old_jerk)


def swap_pairs(near, far, axis):
    count = lax.axis_size(axis)
    inside = [(i, i ^ 1) for i in range(count)]
    between = [(i, (i + (1 if i % 2 else -1)) % count) for i in range(count)]
    got_far = lax.ppermute(far, axis, between)
    got_near = lax.ppermute(near, axis, inside)
    return got_near, got_far


def body(star_pos, star_vel, star_accel, star_mass, active, density, flow_in, field_in):
    def shape(*dims, dtype=f32):
        return jax.ShapeDtypeStruct(dims, dtype)

    total = star_pos.shape[1]
    listed = active.shape[0]
    star_count, gas_count = lax.axis_size("star"), lax.axis_size("gas")
    devices = star_count * gas_count
    ext = density.shape
    ext_x, ext_y, ext_z = ext
    grid = (ext_x * star_count, ext_y * gas_count)
    width = min(listed, 256)
    chunks = listed // width
    names = active.reshape(1, listed)
    inputs = [
        star_pos, star_vel, star_accel, star_mass.reshape(1, total), names, field_in, flow_in, density
    ]
    *held, send, state = call(
        predict_kernel,
        [shape(*x.shape, dtype=x.dtype) for x in inputs] + [shape(devices, 2, lanes), shape(8, total)],
        *[pltpu.with_memory_space_constraint(x, pltpu.HBM) for x in inputs],
        in_specs=[pl.BlockSpec(memory_space=pltpu.HBM)] * len(inputs),
        scratch=[pltpu.SemaphoreType.DMA((len(inputs),))],
    )
    pos, vel, acc, _, names, field, flow, dense = held
    got = exchange(send)

    own, near, far, rows = call(
        pack_kernel,
        (shape(4, ext_x, ext_y, lanes), shape(4, ext_x, reach, lanes), shape(4, ext_x, reach, lanes),
         shape(ext_x * ext_y // 2, 2 * ext_z)),
        field, flow, dense, send, after=1,
    )
    near, far = swap_pairs(near, far, "gas")
    place, slot, is_listed, stars, star_left, cells = call(
        index_kernel,
        (shape(1, listed), shape(lanes, total, dtype=bf16), shape(1, total), shape(total, 6 * lanes),
         shape(32, total, dtype=bf16), shape(2 * ext_z, ext_x * ext_y // 2 * lanes)),
        names, state, rows,
    )
    def all_of(*dims):
        return pl.BlockSpec(dims, lambda k: (0,) * len(dims))

    def part_of(rows):
        return pl.BlockSpec((rows, width), lambda k: (0, k))

    def in_parts(in_specs, out_specs):
        if chunks == 1:
            return {}
        return dict(grid=(chunks,), in_specs=in_specs, out_specs=out_specs)

    back, targets = call(
        functools.partial(force_kernel, ext, chunked=chunks > 1),
        (shape(devices, 2, lanes), shape(8, listed)),
        got, names, place, stars, star_left, cells,
        **in_parts(
            [all_of(*got.shape), part_of(1), part_of(1)]
            + [all_of(*x.shape) for x in (stars, star_left, cells)],
            (all_of(devices, 2, lanes), part_of(8)),
        ),
    )
    back = exchange(back)

    if ext_x != reach or ext_y != 2 * reach or ext_z != lanes // 2:
        raise ValueError("brick shape")
    kick_shape = (3, (ext_x + 2 * rim) // 2, ext_y + 2 * reach, lanes)
    brick_shape = (4, ext_x, ext_y + 2 * reach, lanes)

    def one_turn(_):
        edge = shape(len(sent_layers()), ext_y, lanes)
        brick, side, other = call(
            join_kernel, (shape(*brick_shape), edge, edge), own, near, far, targets, after=1
        )
        side, other = swap_pairs(side, other, "star")
        kick = call(
            functools.partial(kick_kernel, ext, grid, chunked=chunks > 1), shape(*kick_shape), targets,
            **in_parts([part_of(8)], all_of(*kick_shape)),
        )
        flow, field_out = call(
            functools.partial(field_kernel, ext),
            (shape(*flow_in.shape), shape(*field_in.shape)), brick, side, other, kick,
        )
        return flow, field_out

    def no_turn(_):
        return jnp.zeros(flow_in.shape, f32), jnp.zeros(field_in.shape, f32)

    flow, field_out = lax.cond(lax.axis_index("star") < star_count, one_turn, no_turn, 0)
    order = call(
        order_kernel, shape(8, lanes), pltpu.with_memory_space_constraint(field_out, pltpu.HBM),
        after=1, where=pltpu.HBM,
        cost=pl.CostEstimate(flops=10**10, bytes_accessed=10**8, transcendentals=0),
    )
    star_new = call(
        update_kernel, shape(12, total), back, pos, vel, acc, slot, is_listed,
        order, after=1,
    )
    return (star_new, flow, field_out)


def solution(mesh):
    placed = (
        P(None, both),
        P(None, both),
        P(None, both),
        P(both),
        P(),
        P("star", "gas", None),
        P(None, "star", "gas", None),
        P(None, "star", "gas", None),
    )
    return jax.shard_map(
        body,
        mesh=mesh,
        in_specs=placed,
        out_specs=(
            P(None, both),
            P(None, "star", "gas", None),
            P(None, "star", "gas", None),
        ),
        check_vma=False,
    )
```

```python
import functools

import jax
import jax.numpy as jnp
from jax import lax
from jax.experimental import pallas as pl
from jax.experimental.pallas import tpu as pltpu
from jax.sharding import PartitionSpec as P

gravity = 0.02
soften = 4.0
time_step = 1.5
field_step = 0.1
both = ("star", "gas")
reach = 4
rim = reach - 1
lanes = 128
vmem_bytes = 48 * 1024 * 1024
batch = 2
depth = 512
f32, bf16, i32 = jnp.float32, jnp.bfloat16, jnp.int32


def iota(shape, dim):
    return lax.broadcasted_iota(i32, shape, dim)


def split3(values):
    high = values.astype(bf16)
    rest = values - high.astype(f32)
    mid = rest.astype(bf16)
    low = (rest - mid.astype(f32)).astype(bf16)
    return high, mid, low


def stack3(values):
    return jnp.concatenate(split3(values), 0)


def dot_of(lhs, rhs, lhs_dim=1, rhs_dim=0):
    return lax.dot_general(
        lhs, rhs, (((lhs_dim,), (rhs_dim,)), ((), ())), preferred_element_type=f32
    )


def one_hot(hits):
    return jnp.where(hits, 1.0, 0.0)


def my_rank():
    return lax.axis_index("star") * lax.axis_size("gas") + lax.axis_index("gas")


def rank_at(place):
    star_count, gas_count = lax.axis_size("star"), lax.axis_size("gas")
    pair, rest = place // (2 * star_count), place % (2 * star_count)
    side, along = rest % 2, rest // 2
    star = along + side * (star_count - 1 - 2 * along)
    gas = pair + side * (gas_count - 1 - 2 * pair)
    return star * gas_count + gas


def exchange(pieces):
    order = [rank_at(k) for k in range(pieces.shape[0])]
    return lax.all_to_all(pieces, both, 0, 0, axis_index_groups=[order], tiled=True)


def call(kernel, outs, *args, grid=None, in_specs=None, out_specs=None, scratch=(), after=0, where=pl.ANY, cost=None):
    spec = {}
    if grid is not None:
        spec = dict(grid=grid, in_specs=in_specs, out_specs=out_specs)
    elif in_specs is not None:
        spec = dict(in_specs=in_specs)
    elif after:
        held = [pl.BlockSpec(memory_space=pltpu.VMEM)] * (len(args) - after)
        spec = dict(in_specs=held + [pl.BlockSpec(memory_space=where)] * after)
    return pl.pallas_call(
        kernel,
        out_shape=outs,
        scratch_shapes=list(scratch),
        cost_estimate=cost,
        compiler_params=pltpu.CompilerParams(vmem_limit_bytes=vmem_bytes),
        **spec,
    )(*args)


def predict_kernel(*refs):
    sources, held = refs[0:8], refs[8:16]
    send_ref, state_ref, sems = refs[16:]
    copies = [
        pltpu.make_async_copy(source, target, sems.at[k])
        for k, (source, target) in enumerate(zip(sources, held))
    ]
    for copy in copies:
        copy.start()
    for copy in copies[0:5]:
        copy.wait()
    pos_ref, vel_ref, acc_ref, mass_ref, active_ref = held[0:5]
    total = pos_ref.shape[1]
    listed = active_ref.shape[1]
    slots = lanes // 4
    pos, vel = pos_ref[...], vel_ref[...]
    old_acc, old_jerk = acc_ref[0:3], acc_ref[3:6]
    pred_pos = (
        pos + time_step * vel + time_step**2 / 2.0 * old_acc + time_step**3 / 6.0 * old_jerk
    )
    pred_vel = vel + time_step * old_acc + time_step**2 / 2.0 * old_jerk
    state = jnp.concatenate([pred_pos, mass_ref[...], pred_vel, jnp.zeros((1, total), f32)], 0)
    state_ref[...] = state
    local = active_ref[...] - my_rank() * total
    hit = one_hot(iota((total, listed), 0) == local).astype(bf16)
    pieces = dot_of(stack3(state), hit)
    placed = pieces[0:8] + pieces[8:16] + pieces[16:24]
    spread = sum(placed[:, k : k + lanes] for k in range(0, listed, lanes))
    for shift in (2 * slots, slots):
        spread = spread + pltpu.roll(spread, shift, 1)
    lane = iota((8, lanes), 1)
    row = iota((8, lanes), 0)
    spread = jnp.where(row % 4 == lane // slots, spread, 0.0)
    one = jnp.sum(spread[0:4], 0, keepdims=True)
    two = jnp.sum(spread[4:8], 0, keepdims=True)
    send_ref[...] = jnp.broadcast_to(jnp.concatenate([one, two], 0)[None], send_ref.shape)
    for copy in copies[5:]:
        copy.wait()


def pack_kernel(field_ref, flow_ref, density_ref, order_ref, own_ref, near_ref, far_ref, rows_ref):
    comps = [field_ref[0], field_ref[1], field_ref[2], flow_ref[0], flow_ref[1], flow_ref[2]]
    comps = comps + [density_ref[...], density_ref[...]]
    even = lax.axis_index("gas") % 2 == 0
    for k in range(4):
        pair = jnp.concatenate([comps[2 * k], comps[2 * k + 1]], -1)
        own_ref[k] = pair
        low, high = pair[:, :reach], pair[:, -reach:]
        near_ref[k] = jnp.where(even, high, low)
        far_ref[k] = jnp.where(even, low, high)
    half = density_ref.shape[1] // 2
    for k in range(density_ref.shape[0]):
        rows_ref[k * half : (k + 1) * half] = jnp.concatenate(
            [density_ref[k, 0:half, :], density_ref[k, half:, :]], -1
        )


def join_kernel(own_ref, near_ref, far_ref, order_ref, brick_ref, side_ref, other_ref):
    even = lax.axis_index("gas") % 2 == 0
    own, near, far = own_ref[...], near_ref[...], far_ref[...]
    rows = own.shape[2]
    below = jnp.where(even, far, near)
    above = jnp.where(even, near, far)
    beyond = jnp.concatenate([above, below], 2)
    brick_ref[:, :, 0:rows] = own
    brick_ref[:, :, rows:] = beyond
    even = lax.axis_index("star") % 2 == 0
    depth = own.shape[1]
    left = iota((1, lanes), 1) < lanes // 2

    def layer(part, k, away, high):
        return part[k, depth - away if high else away - 1]

    for send_ref, high_if_even in ((side_ref, True), (other_ref, False)):
        for at, (part, pairs, away) in enumerate(sent_layers()):
            part = beyond if part else own
            tile = []
            for high in (high_if_even, not high_if_even):
                value = layer(part, pairs, away, high)
                if pairs == 3 and away == 1:
                    value = jnp.where(left, value, layer(part, pairs, 2, high))
                tile.append(value)
            send_ref[at] = jnp.where(even, tile[0], tile[1])


def sent_layers():
    tiles = []
    for away in range(1, reach + 1):
        for part in range(2):
            for pair in range(4):
                if part + away > reach or (pair > 1 and part + away > rim) or (pair == 3 and away == 2):
                    continue
                tiles.append((part, pair, away))
    return tiles


def index_kernel(active_ref, state_ref, density_ref, slot_ref, listed_ref, stars_ref, star_left_ref, cells_ref):
    listed = active_ref.shape[1]
    total = state_ref.shape[1]
    slots = lanes // 4
    active = active_ref[...]
    local = active - my_rank() * total
    mine = (local >= 0) & (local < total)
    pick = one_hot((iota((lanes, listed), 0) % slots == iota((lanes, listed), 1) % slots) & mine).astype(bf16)
    hit = one_hot(iota((total, listed), 0) == local).astype(bf16)
    slot = dot_of(pick, hit, 1, 1)
    slot_ref[...] = slot.astype(bf16)
    listed_ref[...] = jnp.sum(slot[0:slots], 0, keepdims=True)
    state = state_ref[...]
    ask = one_hot(iota((24, 6 * lanes), 0) % 8 == wide_row((24, 6 * lanes))).astype(bf16)
    stars_ref[...] = dot_of(stack3(state), ask, 0, 0)
    star_left_ref[...] = stack4(moments(state, state[3:4]))
    rows = density_ref.shape[0]
    wide = rows * lanes
    ask = one_hot(iota((3 * rows, wide), 0) % rows == iota((3 * rows, wide), 1) // lanes).astype(bf16)
    cells_ref[...] = dot_of(stack3(density_ref[...]), ask, 0, 0)


def wide_row(shape):
    at = iota(shape, 1) // lanes
    return jnp.where(at < 3, at, at + 1)


def moments(values, mass):
    return jnp.where(iota(values.shape, 0) == 3, jnp.broadcast_to(mass, values.shape), values * mass)


def stack4(values):
    return jnp.concatenate([stack3(values), jnp.zeros(values.shape, bf16)], 0)


def weigh(left, weight):
    high = weight.astype(bf16)
    return dot_of(left, high) + dot_of(left.astype(f32), weight - high.astype(f32))


def fold3(sums):
    return sums[0:8] + sums[8:16] + sums[16:24]


def force_kernel(
    ext, got_ref, active_ref, stars_ref, star_left_ref, cells_ref, send_ref, target_ref, *, chunked
):
    ext_x, ext_y, ext_z = ext
    total = stars_ref.shape[0]
    width = active_ref.shape[1]
    devices = got_ref.shape[0]
    slots = lanes // 4
    starts = rank_at(iota((devices, width), 0)) * total
    active = active_ref[...]
    owned = one_hot((active >= starts) & (active < starts + total)).astype(bf16)
    owned3 = jnp.concatenate([owned, owned, owned], 0)
    slot_hit = one_hot(iota((slots, width), 0) == iota((slots, width), 1) % slots)
    spread = dot_of(stack3(jnp.concatenate([got_ref[:, 0, :], got_ref[:, 1, :]], 1)), owned3, 0, 0)
    targets = jnp.sum(spread.reshape(8, slots, width) * slot_hit[None], 1)
    target_ref[...] = targets

    first_x = lax.axis_index("star") * ext_x
    first_y = lax.axis_index("gas") * ext_y
    tx, ty, tz, _, tu, tv, tw, _ = [targets[k : k + 1] for k in range(8)]
    pulls = jnp.zeros((32, width), f32)
    bends = jnp.zeros((32, width), f32)
    step = min(total, depth)
    for at in range(0, total, step):
        src = [stars_ref[at : at + step, k * lanes : (k + 1) * lanes] for k in range(6)]
        src = [jnp.concatenate([v] * (width // lanes), 1) for v in src]
        dx, dy, dz = src[0] - tx, src[1] - ty, src[2] - tz
        du, dv, dw = src[3] - tu, src[4] - tv, src[5] - tw
        inv = lax.rsqrt(dx * dx + dy * dy + dz * dz + soften)
        inv2 = inv * inv
        weight = inv * inv2
        bend = (dx * du + dy * dv + dz * dw) * inv2 * weight
        left = star_left_ref[:, at : at + step]
        pulls = pulls + weigh(left, weight)
        bends = bends + weigh(left, bend)
    gas_acc = []
    step = 32
    for lane in range(0, width, lanes):
        def row_of(k):
            return jnp.broadcast_to(targets[k : k + 1, lane : lane + lanes], (8, lanes))

        def wide(row):
            return jnp.concatenate([row] * (step // 8), 0)

        def fold(block):
            return sum(block[k : k + 8] for k in range(0, step, 8))

        px, py, pz = row_of(0), row_of(1), wide(row_of(2))
        sums = [jnp.zeros((8, lanes), f32) for _ in range(3)]
        for pair in range(ext_y // 2):
            for at in range(0, 2 * ext_z, step):
                gap_y = (first_y + pair + at // ext_z * (ext_y // 2)).astype(f32) + 0.5 - py
                gap_z = (iota((step, lanes), 0) + at % ext_z).astype(f32) + 0.5 - pz
                base = gap_z * gap_z + wide(gap_y * gap_y + soften)
                along = None
                for k in range(ext_x):
                    gap_x = ((first_x + k).astype(f32) + 0.5) - px
                    col = (k * (ext_y // 2) + pair) * lanes
                    inv = lax.rsqrt(base + wide(gap_x * gap_x))
                    weight = cells_ref[at : at + step, col : col + lanes] * inv * (inv * inv)
                    sums[0] = sums[0] + gap_x * fold(weight)
                    along = weight if along is None else along + weight
                sums[1] = sums[1] + gap_y * fold(along)
                sums[2] = sums[2] + fold(gap_z * along)
        gas_acc.append(jnp.concatenate([jnp.sum(v, 0, keepdims=True) for v in sums], 0))
    gas_acc = jnp.concatenate(gas_acc, 1)
    pulls, bends = fold3(pulls), fold3(bends)
    new_acc = gas_acc + (pulls[0:3] - targets[0:3] * pulls[3:4])
    new_jerk = pulls[4:7] - targets[4:7] * pulls[3:4]
    new_jerk = new_jerk - 3.0 * (bends[0:3] - targets[0:3] * bends[3:4])
    none = jnp.zeros((1, width), f32)
    partial = gravity * jnp.concatenate([new_acc, none, new_jerk, none], 0)
    owned3 = jnp.concatenate([owned, owned, owned], 1)
    for half in range(2):
        spread = partial[4 * half : 4 * half + 4][:, None, :] * slot_hit[None]
        spread = jnp.concatenate(split3(spread.reshape(4 * slots, width)), 1)
        sent = dot_of(owned3, spread, 1, 1)
        if chunked:
            step_at = pl.program_id(0)

            @pl.when(step_at == 0)
            def _():
                send_ref[:, half, :] = sent

            @pl.when(step_at > 0)
            def _():
                send_ref[:, half, :] += sent
        else:
            send_ref[:, half, :] = sent


def kick_kernel(ext, grid, target_ref, kick_ref, *, chunked):
    ext_x, ext_y, ext_z = ext
    width = target_ref.shape[1]

    def clear():
        kick_ref[...] = jnp.zeros(kick_ref.shape, f32)

    if chunked:
        pl.when(pl.program_id(0) == 0)(clear)
    else:
        clear()
    targets = target_ref[...]
    mass = targets[3:4]
    row = iota((8, width), 0)
    moment = jnp.where(row < 3, targets * mass, jnp.where(row == 3, mass, 0.0))
    pieces = split3(moment)
    left = jnp.concatenate([v[0:4] for v in pieces] + [jnp.zeros((4, width), bf16)], 0)
    ask = one_hot(iota((24, 3 * lanes), 0) % 8 == iota((24, 3 * lanes), 1) // lanes).astype(bf16)
    spread = dot_of(stack3(targets), ask, 0, 0)
    tx, ty, tz = spread[:, 0:lanes], spread[:, lanes : 2 * lanes], spread[:, 2 * lanes :]
    lane = iota((1, lanes), 1)
    cell_z = (lane % ext_z).astype(f32) + 0.5
    gap_z = cell_z - tz
    base = gap_z * gap_z + soften
    first_x = lax.axis_index("star") * ext_x + grid[0] - rim
    first_y = lax.axis_index("gas") * ext_y + grid[1] - rim
    place_x, square_x = [], []
    for pair in range((ext_x + 2 * rim) // 2):
        at = lax.rem(first_x + 2 * pair + lane // ext_z, grid[0])
        at = at.astype(f32) + 0.5
        place_x.append(at)
        square_x.append((at - tx) * (at - tx))
    tiles = []
    for j in range(ext_y + 2 * rim):
        out_y = max(rim - j, j - (ext_y + rim - 1), 0)
        for pair in range((ext_x + 2 * rim) // 2):
            out_x = min(max(rim - i, i - (ext_x + rim - 1), 0) for i in (2 * pair, 2 * pair + 1))
            if out_x + out_y <= rim:
                tiles.append((j, pair))
    base_y, at_y = {}, {}
    for k in range(0, len(tiles), batch):
        part = tiles[k : k + batch]
        weights = []
        for j, pair in part:
            if j not in base_y:
                at_y[j] = lax.rem(first_y + j, grid[1]).astype(f32) + 0.5
                gap_y = at_y[j] - ty
                base_y[j] = base + gap_y * gap_y
            inv = lax.rsqrt(base_y[j] + square_x[pair])
            weights.append(inv * (inv * inv))
        sums = weigh(left, jnp.concatenate(weights, 1))
        sums = sums[0:8] + sums[8:16]
        sums = sums + pltpu.roll(sums, 4, 0)
        for at, (j, pair) in enumerate(part):
            here = sums[:, at * lanes : (at + 1) * lanes]
            whole = here[3:4]
            row = (j - rim) % (ext_y + 2 * reach)
            kick_ref[0, pair, row : row + 1, :] += here[0:1] - place_x[pair] * whole
            kick_ref[1, pair, row : row + 1, :] += here[1:2] - at_y[j] * whole
            kick_ref[2, pair, row : row + 1, :] += here[2:3] - cell_z * whole


def twice(values):
    half = lanes // 2
    turned = pltpu.roll(values, half, values.ndim - 1)
    left = iota(values.shape, values.ndim - 1) < half
    return jnp.where(left, values, turned), jnp.where(left, turned, values)


def diff_x(values):
    return values[2:] - values[:-2]


def diff_y(values):
    rows = values.shape[1]
    return (pltpu.roll(values, rows - 1, 1) - pltpu.roll(values, 1, 1))[1:-1]


def diff_z(values):
    return (pltpu.roll(values, lanes - 1, 2) - pltpu.roll(values, 1, 2))[1:-1]


def double_curl(a, b, c):
    return (diff_y(c) - diff_z(b), diff_z(a) - diff_x(c), diff_x(b) - diff_y(a))


def cross_of(lhs, rhs):
    return (
        lhs[1] * rhs[2] - lhs[2] * rhs[1],
        lhs[2] * rhs[0] - lhs[0] * rhs[2],
        lhs[0] * rhs[1] - lhs[1] * rhs[0],
    )


def inner(values, width):
    return [v[width:-width] for v in values]


def double_rate(field, flow, half_resist):
    current = double_curl(*field)
    held = inner(field, 1)
    drift = cross_of(cross_of(current, held), held)
    motion = cross_of(flow, held)
    return double_curl(*[m + half_resist * d for m, d in zip(motion, drift)])


def field_kernel(ext, own_ref, near_ref, far_ref, kick_ref, flow_ref, out_ref):
    ext_x, ext_y, ext_z = ext
    even = lax.axis_index("star") % 2 == 0
    place = {tile: at for at, tile in enumerate(sent_layers())}
    half = lanes // 2

    def sent(ref, pair, away):
        parts = []
        for part in range(2):
            shared = pair == 3 and away == 2
            at = place.get((part, pair, 1 if shared else away))
            if at is None:
                parts.append(jnp.ones((ext_y, lanes), f32))
            elif shared:
                parts.append(pltpu.roll(ref[at], half, 1))
            else:
                parts.append(ref[at])
        return jnp.concatenate(parts, 0)

    comps = []
    for k in range(4):
        near = [sent(near_ref, k, away) for away in range(1, reach + 1)]
        far = [sent(far_ref, k, away) for away in range(1, reach + 1)]
        below = jnp.stack([jnp.where(even, f, n) for n, f in zip(near, far)][::-1])
        above = jnp.stack([jnp.where(even, n, f) for n, f in zip(near, far)])
        whole = twice(jnp.concatenate([below, own_ref[k], above], 0))
        if k == 3:
            comps.append(whole[0][1:-1])
        else:
            comps.extend(whole)
    field = comps[0:3]
    dense = comps[6]
    inv = lax.rsqrt(dense)
    half_resist = 0.5 * (inv * inv * inv)
    flow = []
    for k in range(3):
        kick = jnp.stack(twice(kick_ref[k]), 1).reshape((ext_x + 2 * rim,) + kick_ref.shape[2:])
        flow.append(comps[3 + k][1:-1] + (time_step * gravity) * kick)
    rows = slice(0, ext_y)
    for k in range(3):
        flow_ref[k] = flow[k][rim:-rim, rows, 0:ext_z]
    rate = double_rate(field, flow, half_resist)
    section = [b + (0.5 * field_step) * r for b, r in zip(inner(field, 2), rate)]
    rate = double_rate(section, inner(flow, 2), half_resist[2:-2])
    for k in range(3):
        new = field[k][reach:-reach] + section[k][2:-2] + (0.5 * field_step) * rate[k]
        out_ref[k] = 0.5 * new[:, rows, 0:ext_z]


def order_kernel(order_ref, out_ref):
    out_ref[...] = jnp.zeros(out_ref.shape, f32)


def update_kernel(back_ref, pos_ref, vel_ref, acc_ref, slot_ref, listed_ref, order_ref, out_ref):
    slots = lanes // 4
    summed = jnp.sum(back_ref[...], 0)
    row, lane = iota((8, lanes), 0), iota((8, lanes), 1)
    terms = jnp.where(row < 3, summed[0:1], summed[1:2])
    terms = jnp.where((row < 6) & (row % 3 == lane // slots), terms, 0.0)
    slot = slot_ref[...]
    pieces = dot_of(stack3(terms), slot)
    new = pieces[0:8] + pieces[8:16] + pieces[16:24]
    new_acc, new_jerk = new[0:3], new[3:6]
    pos, vel = pos_ref[...], vel_ref[...]
    old_acc, old_jerk = acc_ref[0:3], acc_ref[3:6]
    vel_one = (
        vel + time_step * (old_acc + new_acc) / 2.0 + time_step**2 * (old_jerk - new_jerk) / 12.0
    )
    pos_one = (
        pos + time_step * (vel + vel_one) / 2.0 + time_step**2 * (old_acc - new_acc) / 12.0
    )
    listed = listed_ref[...] > 0.5
    out_ref[0:3] = jnp.where(listed, pos_one, pos)
    out_ref[3:6] = jnp.where(listed, vel_one, vel)
    out_ref[6:9] = jnp.where(listed, new_acc, old_acc)
    out_ref[9:12] = jnp.where(listed, new_jerk, old_jerk)


def swap_pairs(near, far, axis):
    count = lax.axis_size(axis)
    inside = [(i, i ^ 1) for i in range(count)]
    between = [(i, (i + (1 if i % 2 else -1)) % count) for i in range(count)]
    got_far = lax.ppermute(far, axis, between)
    got_near = lax.ppermute(near, axis, inside)
    return got_near, got_far


def body(star_pos, star_vel, star_accel, star_mass, active, density, flow_in, field_in):
    def shape(*dims, dtype=f32):
        return jax.ShapeDtypeStruct(dims, dtype)

    total = star_pos.shape[1]
    listed = active.shape[0]
    star_count, gas_count = lax.axis_size("star"), lax.axis_size("gas")
    devices = star_count * gas_count
    ext = density.shape
    ext_x, ext_y, ext_z = ext
    grid = (ext_x * star_count, ext_y * gas_count)
    width = min(listed, 256)
    chunks = listed // width
    names = active.reshape(1, listed)
    inputs = [
        star_pos, star_vel, star_accel, star_mass.reshape(1, total), names, field_in, flow_in, density
    ]
    *held, send, state = call(
        predict_kernel,
        [shape(*x.shape, dtype=x.dtype) for x in inputs] + [shape(devices, 2, lanes), shape(8, total)],
        *[pltpu.with_memory_space_constraint(x, pltpu.HBM) for x in inputs],
        in_specs=[pl.BlockSpec(memory_space=pltpu.HBM)] * len(inputs),
        scratch=[pltpu.SemaphoreType.DMA((len(inputs),))],
    )
    pos, vel, acc, _, names, field, flow, dense = held
    got = exchange(send)

    own, near, far, rows = call(
        pack_kernel,
        (shape(4, ext_x, ext_y, lanes), shape(4, ext_x, reach, lanes), shape(4, ext_x, reach, lanes),
         shape(ext_x * ext_y // 2, 2 * ext_z)),
        field, flow, dense, send, after=1,
    )
    near, far = swap_pairs(near, far, "gas")
    slot, is_listed, stars, star_left, cells = call(
        index_kernel,
        (shape(lanes, total, dtype=bf16), shape(1, total), shape(total, 6 * lanes),
         shape(32, total, dtype=bf16), shape(2 * ext_z, ext_x * ext_y // 2 * lanes)),
        names, state, rows,
    )
    def all_of(*dims):
        return pl.BlockSpec(dims, lambda k: (0,) * len(dims))

    def part_of(rows):
        return pl.BlockSpec((rows, width), lambda k: (0, k))

    def in_parts(in_specs, out_specs):
        if chunks == 1:
            return {}
        return dict(grid=(chunks,), in_specs=in_specs, out_specs=out_specs)

    back, targets = call(
        functools.partial(force_kernel, ext, chunked=chunks > 1),
        (shape(devices, 2, lanes), shape(8, listed)),
        got, names, stars, star_left, cells,
        **in_parts(
            [all_of(*got.shape), part_of(1)]
            + [all_of(*x.shape) for x in (stars, star_left, cells)],
            (all_of(devices, 2, lanes), part_of(8)),
        ),
    )
    back = exchange(back)

    if ext_x != reach or ext_y != 2 * reach or ext_z != lanes // 2:
        raise ValueError("brick shape")
    kick_shape = (3, (ext_x + 2 * rim) // 2, ext_y + 2 * reach, lanes)
    brick_shape = (4, ext_x, ext_y + 2 * reach, lanes)

    def one_turn(_):
        edge = shape(len(sent_layers()), ext_y, lanes)
        brick, side, other = call(
            join_kernel, (shape(*brick_shape), edge, edge), own, near, far, targets, after=1
        )
        side, other = swap_pairs(side, other, "star")
        kick = call(
            functools.partial(kick_kernel, ext, grid, chunked=chunks > 1), shape(*kick_shape), targets,
            **in_parts([part_of(8)], all_of(*kick_shape)),
        )
        flow, field_out = call(
            functools.partial(field_kernel, ext),
            (shape(*flow_in.shape), shape(*field_in.shape)), brick, side, other, kick,
        )
        return flow, field_out

    def no_turn(_):
        return jnp.zeros(flow_in.shape, f32), jnp.zeros(field_in.shape, f32)

    flow, field_out = lax.cond(lax.axis_index("star") < star_count, one_turn, no_turn, 0)
    order = call(
        order_kernel, shape(8, lanes), pltpu.with_memory_space_constraint(field_out, pltpu.HBM),
        after=1, where=pltpu.HBM,
        cost=pl.CostEstimate(flops=10**10, bytes_accessed=10**8, transcendentals=0),
    )
    star_new = call(
        update_kernel, shape(12, total), back, pos, vel, acc, slot, is_listed,
        order, after=1,
    )
    return (star_new, flow, field_out)


def solution(mesh):
    placed = (
        P(None, both),
        P(None, both),
        P(None, both),
        P(both),
        P(),
        P("star", "gas", None),
        P(None, "star", "gas", None),
        P(None, "star", "gas", None),
    )
    return jax.shard_map(
        body,
        mesh=mesh,
        in_specs=placed,
        out_specs=(
            P(None, both),
            P(None, "star", "gas", None),
            P(None, "star", "gas", None),
        ),
        check_vma=False,
    )
```

```python
import functools

import jax
import jax.numpy as jnp
from jax import lax
from jax.experimental import pallas as pl
from jax.experimental.pallas import tpu as pltpu
from jax.sharding import PartitionSpec as P

gravity = 0.02
soften = 4.0
time_step = 1.5
field_step = 0.1
both = ("star", "gas")
reach = 4
rim = reach - 1
lanes = 128
vmem_bytes = 48 * 1024 * 1024
batch = 2
depth = 512
f32, bf16, i32 = jnp.float32, jnp.bfloat16, jnp.int32


def iota(shape, dim):
    return lax.broadcasted_iota(i32, shape, dim)


def split3(values):
    high = values.astype(bf16)
    rest = values - high.astype(f32)
    mid = rest.astype(bf16)
    low = (rest - mid.astype(f32)).astype(bf16)
    return high, mid, low


def stack3(values):
    return jnp.concatenate(split3(values), 0)


def dot_of(lhs, rhs, lhs_dim=1, rhs_dim=0):
    return lax.dot_general(
        lhs, rhs, (((lhs_dim,), (rhs_dim,)), ((), ())), preferred_element_type=f32
    )


def one_hot(hits):
    return jnp.where(hits, 1.0, 0.0)


def my_rank():
    return lax.axis_index("star") * lax.axis_size("gas") + lax.axis_index("gas")


def rank_at(place):
    star_count, gas_count = lax.axis_size("star"), lax.axis_size("gas")
    pair, rest = place // (2 * star_count), place % (2 * star_count)
    side, along = rest % 2, rest // 2
    star = along + side * (star_count - 1 - 2 * along)
    gas = pair + side * (gas_count - 1 - 2 * pair)
    return star * gas_count + gas


def exchange(pieces):
    order = [rank_at(k) for k in range(pieces.shape[0])]
    return lax.all_to_all(pieces, both, 0, 0, axis_index_groups=[order], tiled=True)


def call(kernel, outs, *args, grid=None, in_specs=None, out_specs=None, scratch=(), after=0, where=pl.ANY, cost=None):
    spec = {}
    if grid is not None:
        spec = dict(grid=grid, in_specs=in_specs, out_specs=out_specs)
    elif in_specs is not None:
        spec = dict(in_specs=in_specs)
    elif after:
        held = [pl.BlockSpec(memory_space=pltpu.VMEM)] * (len(args) - after)
        spec = dict(in_specs=held + [pl.BlockSpec(memory_space=where)] * after)
    return pl.pallas_call(
        kernel,
        out_shape=outs,
        scratch_shapes=list(scratch),
        cost_estimate=cost,
        compiler_params=pltpu.CompilerParams(vmem_limit_bytes=vmem_bytes),
        **spec,
    )(*args)


def predict_kernel(*refs):
    sources, held = refs[0:8], refs[8:16]
    send_ref, state_ref, sems = refs[16:]
    copies = [
        pltpu.make_async_copy(source, target, sems.at[k])
        for k, (source, target) in enumerate(zip(sources, held))
    ]
    for copy in copies:
        copy.start()
    for copy in copies[0:5]:
        copy.wait()
    pos_ref, vel_ref, acc_ref, mass_ref, active_ref = held[0:5]
    total = pos_ref.shape[1]
    listed = active_ref.shape[1]
    slots = lanes // 4
    pos, vel = pos_ref[...], vel_ref[...]
    old_acc, old_jerk = acc_ref[0:3], acc_ref[3:6]
    pred_pos = (
        pos + time_step * vel + time_step**2 / 2.0 * old_acc + time_step**3 / 6.0 * old_jerk
    )
    pred_vel = vel + time_step * old_acc + time_step**2 / 2.0 * old_jerk
    state = jnp.concatenate([pred_pos, mass_ref[...], pred_vel, jnp.zeros((1, total), f32)], 0)
    state_ref[...] = state
    local = active_ref[...] - my_rank() * total
    hit = one_hot(iota((total, listed), 0) == local).astype(bf16)
    pieces = dot_of(stack3(state), hit)
    placed = pieces[0:8] + pieces[8:16] + pieces[16:24]
    spread = sum(placed[:, k : k + lanes] for k in range(0, listed, lanes))
    for shift in (2 * slots, slots):
        spread = spread + pltpu.roll(spread, shift, 1)
    lane = iota((8, lanes), 1)
    row = iota((8, lanes), 0)
    spread = jnp.where(row % 4 == lane // slots, spread, 0.0)
    one = jnp.sum(spread[0:4], 0, keepdims=True)
    two = jnp.sum(spread[4:8], 0, keepdims=True)
    send_ref[...] = jnp.broadcast_to(jnp.concatenate([one, two], 0)[None], send_ref.shape)
    for copy in copies[5:]:
        copy.wait()


def pack_kernel(field_ref, flow_ref, density_ref, order_ref, own_ref, near_ref, far_ref, rows_ref):
    comps = [field_ref[0], field_ref[1], field_ref[2], flow_ref[0], flow_ref[1], flow_ref[2]]
    comps = comps + [density_ref[...], density_ref[...]]
    even = lax.axis_index("gas") % 2 == 0
    for k in range(4):
        pair = jnp.concatenate([comps[2 * k], comps[2 * k + 1]], -1)
        own_ref[k] = pair
        low, high = pair[:, :reach], pair[:, -reach:]
        near_ref[k] = jnp.where(even, high, low)
        far_ref[k] = jnp.where(even, low, high)
    half = density_ref.shape[1] // 2
    for k in range(density_ref.shape[0]):
        rows_ref[k * half : (k + 1) * half] = jnp.concatenate(
            [density_ref[k, 0:half, :], density_ref[k, half:, :]], -1
        )


def join_kernel(own_ref, near_ref, far_ref, order_ref, brick_ref, side_ref, other_ref):
    even = lax.axis_index("gas") % 2 == 0
    own, near, far = own_ref[...], near_ref[...], far_ref[...]
    rows = own.shape[2]
    below = jnp.where(even, far, near)
    above = jnp.where(even, near, far)
    beyond = jnp.concatenate([above, below], 2)
    brick_ref[:, :, 0:rows] = own
    brick_ref[:, :, rows:] = beyond
    even = lax.axis_index("star") % 2 == 0
    depth = own.shape[1]
    left = iota((1, lanes), 1) < lanes // 2

    def layer(part, k, away, high):
        return part[k, depth - away if high else away - 1]

    for send_ref, high_if_even in ((side_ref, True), (other_ref, False)):
        for at, (part, pairs, away) in enumerate(sent_layers()):
            part = beyond if part else own
            tile = []
            for high in (high_if_even, not high_if_even):
                value = layer(part, pairs, away, high)
                if pairs == 3 and away == 1:
                    value = jnp.where(left, value, layer(part, pairs, 2, high))
                tile.append(value)
            send_ref[at] = jnp.where(even, tile[0], tile[1])


def sent_layers():
    tiles = []
    for away in range(1, reach + 1):
        for part in range(2):
            for pair in range(4):
                if part + away > reach or (pair > 1 and part + away > rim) or (pair == 3 and away == 2):
                    continue
                tiles.append((part, pair, away))
    return tiles


def index_kernel(active_ref, state_ref, density_ref, slot_ref, listed_ref, stars_ref, star_left_ref, cells_ref):
    listed = active_ref.shape[1]
    total = state_ref.shape[1]
    slots = lanes // 4
    active = active_ref[...]
    local = active - my_rank() * total
    mine = (local >= 0) & (local < total)
    pick = one_hot((iota((lanes, listed), 0) % slots == iota((lanes, listed), 1) % slots) & mine).astype(bf16)
    hit = one_hot(iota((total, listed), 0) == local).astype(bf16)
    slot = dot_of(pick, hit, 1, 1)
    slot_ref[...] = slot.astype(bf16)
    listed_ref[...] = jnp.sum(slot[0:slots], 0, keepdims=True)
    state = state_ref[...]
    ask = one_hot(iota((24, 6 * lanes), 0) % 8 == wide_row((24, 6 * lanes))).astype(bf16)
    stars_ref[...] = dot_of(stack3(state), ask, 0, 0)
    star_left_ref[...] = stack4(moments(state, state[3:4]))
    rows = density_ref.shape[0]
    wide = rows * lanes
    ask = one_hot(iota((3 * rows, wide), 0) % rows == iota((3 * rows, wide), 1) // lanes).astype(bf16)
    cells_ref[...] = dot_of(stack3(density_ref[...]), ask, 0, 0)


def wide_row(shape):
    at = iota(shape, 1) // lanes
    return jnp.where(at < 3, at, at + 1)


def moments(values, mass):
    return jnp.where(iota(values.shape, 0) == 3, jnp.broadcast_to(mass, values.shape), values * mass)


def stack4(values):
    return jnp.concatenate([stack3(values), jnp.zeros(values.shape, bf16)], 0)


def weigh(left, weight):
    high = weight.astype(bf16)
    return dot_of(left, high) + dot_of(left.astype(f32), weight - high.astype(f32))


def fold3(sums):
    return sums[0:8] + sums[8:16] + sums[16:24]


def force_kernel(
    ext, got_ref, active_ref, stars_ref, star_left_ref, cells_ref, send_ref, target_ref, *, chunked
):
    ext_x, ext_y, ext_z = ext
    total = stars_ref.shape[0]
    width = active_ref.shape[1]
    devices = got_ref.shape[0]
    slots = lanes // 4
    starts = rank_at(iota((devices, width), 0)) * total
    active = active_ref[...]
    owned = one_hot((active >= starts) & (active < starts + total))
    group = iota((devices, lanes), 1) // slots
    rows = []
    for half in range(2):
        raw = got_ref[:, half, :]
        turned = [raw] + [pltpu.roll(raw, k * slots, 1) for k in range(1, 4)]
        for comp in range(4 - half):
            same = turned[(3 - comp) % 4]
            for at in range(3):
                same = jnp.where(group == at, turned[(at - comp) % 4], same)
            picked = jnp.concatenate([same] * (width // lanes), 1) * owned
            rows.append(jnp.sum(picked, 0, keepdims=True))
    targets = jnp.concatenate(rows + [jnp.zeros((1, width), f32)], 0)
    target_ref[...] = targets

    first_x = lax.axis_index("star") * ext_x
    first_y = lax.axis_index("gas") * ext_y
    tx, ty, tz, _, tu, tv, tw, _ = [targets[k : k + 1] for k in range(8)]
    pulls = jnp.zeros((32, width), f32)
    bends = jnp.zeros((32, width), f32)
    step = min(total, depth)
    for at in range(0, total, step):
        src = [stars_ref[at : at + step, k * lanes : (k + 1) * lanes] for k in range(6)]
        src = [jnp.concatenate([v] * (width // lanes), 1) for v in src]
        dx, dy, dz = src[0] - tx, src[1] - ty, src[2] - tz
        du, dv, dw = src[3] - tu, src[4] - tv, src[5] - tw
        inv = lax.rsqrt(dx * dx + dy * dy + dz * dz + soften)
        inv2 = inv * inv
        weight = inv * inv2
        bend = (dx * du + dy * dv + dz * dw) * inv2 * weight
        left = star_left_ref[:, at : at + step]
        pulls = pulls + weigh(left, weight)
        bends = bends + weigh(left, bend)
    gas_acc = []
    step = 32
    for lane in range(0, width, lanes):
        def row_of(k):
            return jnp.broadcast_to(targets[k : k + 1, lane : lane + lanes], (8, lanes))

        def wide(row):
            return jnp.concatenate([row] * (step // 8), 0)

        def fold(block):
            return sum(block[k : k + 8] for k in range(0, step, 8))

        px, py, pz = row_of(0), row_of(1), wide(row_of(2))
        sums = [jnp.zeros((8, lanes), f32) for _ in range(3)]
        for pair in range(ext_y // 2):
            for at in range(0, 2 * ext_z, step):
                gap_y = (first_y + pair + at // ext_z * (ext_y // 2)).astype(f32) + 0.5 - py
                gap_z = (iota((step, lanes), 0) + at % ext_z).astype(f32) + 0.5 - pz
                base = gap_z * gap_z + wide(gap_y * gap_y + soften)
                along = None
                for k in range(ext_x):
                    gap_x = ((first_x + k).astype(f32) + 0.5) - px
                    col = (k * (ext_y // 2) + pair) * lanes
                    inv = lax.rsqrt(base + wide(gap_x * gap_x))
                    weight = cells_ref[at : at + step, col : col + lanes] * inv * (inv * inv)
                    sums[0] = sums[0] + gap_x * fold(weight)
                    along = weight if along is None else along + weight
                sums[1] = sums[1] + gap_y * fold(along)
                sums[2] = sums[2] + fold(gap_z * along)
        gas_acc.append(jnp.concatenate([jnp.sum(v, 0, keepdims=True) for v in sums], 0))
    gas_acc = jnp.concatenate(gas_acc, 1)
    pulls, bends = fold3(pulls), fold3(bends)
    new_acc = gas_acc + (pulls[0:3] - targets[0:3] * pulls[3:4])
    new_jerk = pulls[4:7] - targets[4:7] * pulls[3:4]
    new_jerk = new_jerk - 3.0 * (bends[0:3] - targets[0:3] * bends[3:4])
    for half, terms in enumerate((new_acc, new_jerk)):
        parts = []
        for comp in range(3):
            held = owned * (gravity * terms[comp : comp + 1])
            parts.append(sum(held[:, k : k + lanes] for k in range(0, width, lanes)))
        parts.append(jnp.zeros((devices, lanes), f32))
        sent = None
        for k in range(4):
            mixed = parts[(3 + k) % 4]
            for at in range(3):
                mixed = jnp.where(group == at, parts[(at + k) % 4], mixed)
            mixed = pltpu.roll(mixed, k * slots, 1) if k else mixed
            sent = mixed if sent is None else sent + mixed
        if chunked:
            step_at = pl.program_id(0)

            @pl.when(step_at == 0)
            def _():
                send_ref[:, half, :] = sent

            @pl.when(step_at > 0)
            def _():
                send_ref[:, half, :] += sent
        else:
            send_ref[:, half, :] = sent


def kick_kernel(ext, grid, target_ref, kick_ref, *, chunked):
    ext_x, ext_y, ext_z = ext
    width = target_ref.shape[1]

    def clear():
        kick_ref[...] = jnp.zeros(kick_ref.shape, f32)

    if chunked:
        pl.when(pl.program_id(0) == 0)(clear)
    else:
        clear()
    targets = target_ref[...]
    mass = targets[3:4]
    row = iota((8, width), 0)
    moment = jnp.where(row < 3, targets * mass, jnp.where(row == 3, mass, 0.0))
    pieces = split3(moment)
    left = jnp.concatenate([v[0:4] for v in pieces] + [jnp.zeros((4, width), bf16)], 0)
    ask = one_hot(iota((24, 3 * lanes), 0) % 8 == iota((24, 3 * lanes), 1) // lanes).astype(bf16)
    spread = dot_of(stack3(targets), ask, 0, 0)
    tx, ty, tz = spread[:, 0:lanes], spread[:, lanes : 2 * lanes], spread[:, 2 * lanes :]
    lane = iota((1, lanes), 1)
    cell_z = (lane % ext_z).astype(f32) + 0.5
    gap_z = cell_z - tz
    base = gap_z * gap_z + soften
    first_x = lax.axis_index("star") * ext_x + grid[0] - rim
    first_y = lax.axis_index("gas") * ext_y + grid[1] - rim
    place_x, square_x = [], []
    for pair in range((ext_x + 2 * rim) // 2):
        at = lax.rem(first_x + 2 * pair + lane // ext_z, grid[0])
        at = at.astype(f32) + 0.5
        place_x.append(at)
        square_x.append((at - tx) * (at - tx))
    tiles = []
    for j in range(ext_y + 2 * rim):
        out_y = max(rim - j, j - (ext_y + rim - 1), 0)
        for pair in range((ext_x + 2 * rim) // 2):
            out_x = min(max(rim - i, i - (ext_x + rim - 1), 0) for i in (2 * pair, 2 * pair + 1))
            if out_x + out_y <= rim:
                tiles.append((j, pair))
    base_y, at_y = {}, {}
    for k in range(0, len(tiles), batch):
        part = tiles[k : k + batch]
        weights = []
        for j, pair in part:
            if j not in base_y:
                at_y[j] = lax.rem(first_y + j, grid[1]).astype(f32) + 0.5
                gap_y = at_y[j] - ty
                base_y[j] = base + gap_y * gap_y
            inv = lax.rsqrt(base_y[j] + square_x[pair])
            weights.append(inv * (inv * inv))
        sums = weigh(left, jnp.concatenate(weights, 1))
        sums = sums[0:8] + sums[8:16]
        sums = sums + pltpu.roll(sums, 4, 0)
        for at, (j, pair) in enumerate(part):
            here = sums[:, at * lanes : (at + 1) * lanes]
            whole = here[3:4]
            row = (j - rim) % (ext_y + 2 * reach)
            kick_ref[0, pair, row : row + 1, :] += here[0:1] - place_x[pair] * whole
            kick_ref[1, pair, row : row + 1, :] += here[1:2] - at_y[j] * whole
            kick_ref[2, pair, row : row + 1, :] += here[2:3] - cell_z * whole


def twice(values):
    half = lanes // 2
    turned = pltpu.roll(values, half, values.ndim - 1)
    left = iota(values.shape, values.ndim - 1) < half
    return jnp.where(left, values, turned), jnp.where(left, turned, values)


def diff_x(values):
    return values[2:] - values[:-2]


def diff_y(values):
    rows = values.shape[1]
    return (pltpu.roll(values, rows - 1, 1) - pltpu.roll(values, 1, 1))[1:-1]


def diff_z(values):
    return (pltpu.roll(values, lanes - 1, 2) - pltpu.roll(values, 1, 2))[1:-1]


def double_curl(a, b, c):
    return (diff_y(c) - diff_z(b), diff_z(a) - diff_x(c), diff_x(b) - diff_y(a))


def cross_of(lhs, rhs):
    return (
        lhs[1] * rhs[2] - lhs[2] * rhs[1],
        lhs[2] * rhs[0] - lhs[0] * rhs[2],
        lhs[0] * rhs[1] - lhs[1] * rhs[0],
    )


def inner(values, width):
    return [v[width:-width] for v in values]


def double_rate(field, flow, half_resist):
    current = double_curl(*field)
    held = inner(field, 1)
    drift = cross_of(cross_of(current, held), held)
    motion = cross_of(flow, held)
    return double_curl(*[m + half_resist * d for m, d in zip(motion, drift)])


def field_kernel(ext, own_ref, near_ref, far_ref, kick_ref, flow_ref, out_ref):
    ext_x, ext_y, ext_z = ext
    even = lax.axis_index("star") % 2 == 0
    place = {tile: at for at, tile in enumerate(sent_layers())}
    half = lanes // 2

    def sent(ref, pair, away):
        parts = []
        for part in range(2):
            shared = pair == 3 and away == 2
            at = place.get((part, pair, 1 if shared else away))
            if at is None:
                parts.append(jnp.ones((ext_y, lanes), f32))
            elif shared:
                parts.append(pltpu.roll(ref[at], half, 1))
            else:
                parts.append(ref[at])
        return jnp.concatenate(parts, 0)

    comps = []
    for k in range(4):
        near = [sent(near_ref, k, away) for away in range(1, reach + 1)]
        far = [sent(far_ref, k, away) for away in range(1, reach + 1)]
        below = jnp.stack([jnp.where(even, f, n) for n, f in zip(near, far)][::-1])
        above = jnp.stack([jnp.where(even, n, f) for n, f in zip(near, far)])
        whole = twice(jnp.concatenate([below, own_ref[k], above], 0))
        if k == 3:
            comps.append(whole[0][1:-1])
        else:
            comps.extend(whole)
    field = comps[0:3]
    dense = comps[6]
    inv = lax.rsqrt(dense)
    half_resist = 0.5 * (inv * inv * inv)
    flow = []
    for k in range(3):
        kick = jnp.stack(twice(kick_ref[k]), 1).reshape((ext_x + 2 * rim,) + kick_ref.shape[2:])
        flow.append(comps[3 + k][1:-1] + (time_step * gravity) * kick)
    rows = slice(0, ext_y)
    for k in range(3):
        flow_ref[k] = flow[k][rim:-rim, rows, 0:ext_z]
    rate = double_rate(field, flow, half_resist)
    section = [b + (0.5 * field_step) * r for b, r in zip(inner(field, 2), rate)]
    rate = double_rate(section, inner(flow, 2), half_resist[2:-2])
    for k in range(3):
        new = field[k][reach:-reach] + section[k][2:-2] + (0.5 * field_step) * rate[k]
        out_ref[k] = 0.5 * new[:, rows, 0:ext_z]


def order_kernel(order_ref, out_ref):
    out_ref[...] = jnp.zeros(out_ref.shape, f32)


def update_kernel(back_ref, pos_ref, vel_ref, acc_ref, slot_ref, listed_ref, order_ref, out_ref):
    slots = lanes // 4
    summed = jnp.sum(back_ref[...], 0)
    row, lane = iota((8, lanes), 0), iota((8, lanes), 1)
    terms = jnp.where(row < 3, summed[0:1], summed[1:2])
    terms = jnp.where((row < 6) & (row % 3 == lane // slots), terms, 0.0)
    slot = slot_ref[...]
    pieces = dot_of(stack3(terms), slot)
    new = pieces[0:8] + pieces[8:16] + pieces[16:24]
    new_acc, new_jerk = new[0:3], new[3:6]
    pos, vel = pos_ref[...], vel_ref[...]
    old_acc, old_jerk = acc_ref[0:3], acc_ref[3:6]
    vel_one = (
        vel + time_step * (old_acc + new_acc) / 2.0 + time_step**2 * (old_jerk - new_jerk) / 12.0
    )
    pos_one = (
        pos + time_step * (vel + vel_one) / 2.0 + time_step**2 * (old_acc - new_acc) / 12.0
    )
    listed = listed_ref[...] > 0.5
    out_ref[0:3] = jnp.where(listed, pos_one, pos)
    out_ref[3:6] = jnp.where(listed, vel_one, vel)
    out_ref[6:9] = jnp.where(listed, new_acc, old_acc)
    out_ref[9:12] = jnp.where(listed, new_jerk, old_jerk)


def swap_pairs(near, far, axis):
    count = lax.axis_size(axis)
    inside = [(i, i ^ 1) for i in range(count)]
    between = [(i, (i + (1 if i % 2 else -1)) % count) for i in range(count)]
    got_far = lax.ppermute(far, axis, between)
    got_near = lax.ppermute(near, axis, inside)
    return got_near, got_far


def body(star_pos, star_vel, star_accel, star_mass, active, density, flow_in, field_in):
    def shape(*dims, dtype=f32):
        return jax.ShapeDtypeStruct(dims, dtype)

    total = star_pos.shape[1]
    listed = active.shape[0]
    star_count, gas_count = lax.axis_size("star"), lax.axis_size("gas")
    devices = star_count * gas_count
    ext = density.shape
    ext_x, ext_y, ext_z = ext
    grid = (ext_x * star_count, ext_y * gas_count)
    width = min(listed, 256)
    chunks = listed // width
    names = active.reshape(1, listed)
    inputs = [
        star_pos, star_vel, star_accel, star_mass.reshape(1, total), names, field_in, flow_in, density
    ]
    *held, send, state = call(
        predict_kernel,
        [shape(*x.shape, dtype=x.dtype) for x in inputs] + [shape(devices, 2, lanes), shape(8, total)],
        *[pltpu.with_memory_space_constraint(x, pltpu.HBM) for x in inputs],
        in_specs=[pl.BlockSpec(memory_space=pltpu.HBM)] * len(inputs),
        scratch=[pltpu.SemaphoreType.DMA((len(inputs),))],
    )
    pos, vel, acc, _, names, field, flow, dense = held
    got = exchange(send)

    own, near, far, rows = call(
        pack_kernel,
        (shape(4, ext_x, ext_y, lanes), shape(4, ext_x, reach, lanes), shape(4, ext_x, reach, lanes),
         shape(ext_x * ext_y // 2, 2 * ext_z)),
        field, flow, dense, send, after=1,
    )
    near, far = swap_pairs(near, far, "gas")
    slot, is_listed, stars, star_left, cells = call(
        index_kernel,
        (shape(lanes, total, dtype=bf16), shape(1, total), shape(total, 6 * lanes),
         shape(32, total, dtype=bf16), shape(2 * ext_z, ext_x * ext_y // 2 * lanes)),
        names, state, rows,
    )
    def all_of(*dims):
        return pl.BlockSpec(dims, lambda k: (0,) * len(dims))

    def part_of(rows):
        return pl.BlockSpec((rows, width), lambda k: (0, k))

    def in_parts(in_specs, out_specs):
        if chunks == 1:
            return {}
        return dict(grid=(chunks,), in_specs=in_specs, out_specs=out_specs)

    back, targets = call(
        functools.partial(force_kernel, ext, chunked=chunks > 1),
        (shape(devices, 2, lanes), shape(8, listed)),
        got, names, stars, star_left, cells,
        **in_parts(
            [all_of(*got.shape), part_of(1)]
            + [all_of(*x.shape) for x in (stars, star_left, cells)],
            (all_of(devices, 2, lanes), part_of(8)),
        ),
    )
    back = exchange(back)

    if ext_x != reach or ext_y != 2 * reach or ext_z != lanes // 2:
        raise ValueError("brick shape")
    kick_shape = (3, (ext_x + 2 * rim) // 2, ext_y + 2 * reach, lanes)
    brick_shape = (4, ext_x, ext_y + 2 * reach, lanes)

    def one_turn(_):
        edge = shape(len(sent_layers()), ext_y, lanes)
        brick, side, other = call(
            join_kernel, (shape(*brick_shape), edge, edge), own, near, far, targets, after=1
        )
        side, other = swap_pairs(side, other, "star")
        kick = call(
            functools.partial(kick_kernel, ext, grid, chunked=chunks > 1), shape(*kick_shape), targets,
            **in_parts([part_of(8)], all_of(*kick_shape)),
        )
        flow, field_out = call(
            functools.partial(field_kernel, ext),
            (shape(*flow_in.shape), shape(*field_in.shape)), brick, side, other, kick,
        )
        return flow, field_out

    def no_turn(_):
        return jnp.zeros(flow_in.shape, f32), jnp.zeros(field_in.shape, f32)

    flow, field_out = lax.cond(lax.axis_index("star") < star_count, one_turn, no_turn, 0)
    order = call(
        order_kernel, shape(8, lanes), pltpu.with_memory_space_constraint(field_out, pltpu.HBM),
        after=1, where=pltpu.HBM,
        cost=pl.CostEstimate(flops=10**10, bytes_accessed=10**8, transcendentals=0),
    )
    star_new = call(
        update_kernel, shape(12, total), back, pos, vel, acc, slot, is_listed,
        order, after=1,
    )
    return (star_new, flow, field_out)


def solution(mesh):
    placed = (
        P(None, both),
        P(None, both),
        P(None, both),
        P(both),
        P(),
        P("star", "gas", None),
        P(None, "star", "gas", None),
        P(None, "star", "gas", None),
    )
    return jax.shard_map(
        body,
        mesh=mesh,
        in_specs=placed,
        out_specs=(
            P(None, both),
            P(None, "star", "gas", None),
            P(None, "star", "gas", None),
        ),
        check_vma=False,
    )
```

```python
import functools

import jax
import jax.numpy as jnp
from jax import lax
from jax.experimental import pallas as pl
from jax.experimental.pallas import tpu as pltpu
from jax.sharding import PartitionSpec as P

gravity = 0.02
soften = 4.0
time_step = 1.5
field_step = 0.1
both = ("star", "gas")
reach = 4
rim = reach - 1
lanes = 128
vmem_bytes = 48 * 1024 * 1024
batch = 2
depth = 512
f32, bf16, i32 = jnp.float32, jnp.bfloat16, jnp.int32


def iota(shape, dim):
    return lax.broadcasted_iota(i32, shape, dim)


def split3(values):
    high = values.astype(bf16)
    rest = values - high.astype(f32)
    mid = rest.astype(bf16)
    low = (rest - mid.astype(f32)).astype(bf16)
    return high, mid, low


def stack3(values):
    return jnp.concatenate(split3(values), 0)


def dot_of(lhs, rhs, lhs_dim=1, rhs_dim=0):
    return lax.dot_general(
        lhs, rhs, (((lhs_dim,), (rhs_dim,)), ((), ())), preferred_element_type=f32
    )


def one_hot(hits):
    return jnp.where(hits, 1.0, 0.0)


def my_rank():
    return lax.axis_index("star") * lax.axis_size("gas") + lax.axis_index("gas")


def rank_at(place):
    star_count, gas_count = lax.axis_size("star"), lax.axis_size("gas")
    pair, rest = place // (2 * star_count), place % (2 * star_count)
    side, along = rest % 2, rest // 2
    star = along + side * (star_count - 1 - 2 * along)
    gas = pair + side * (gas_count - 1 - 2 * pair)
    return star * gas_count + gas


def exchange(pieces):
    order = [rank_at(k) for k in range(pieces.shape[0])]
    return lax.all_to_all(pieces, both, 0, 0, axis_index_groups=[order], tiled=True)


def call(kernel, outs, *args, grid=None, in_specs=None, out_specs=None, scratch=(), after=0, where=pl.ANY, cost=None):
    spec = {}
    if grid is not None:
        spec = dict(grid=grid, in_specs=in_specs, out_specs=out_specs)
    elif in_specs is not None:
        spec = dict(in_specs=in_specs)
    elif after:
        held = [pl.BlockSpec(memory_space=pltpu.VMEM)] * (len(args) - after)
        spec = dict(in_specs=held + [pl.BlockSpec(memory_space=where)] * after)
    return pl.pallas_call(
        kernel,
        out_shape=outs,
        scratch_shapes=list(scratch),
        cost_estimate=cost,
        compiler_params=pltpu.CompilerParams(vmem_limit_bytes=vmem_bytes),
        **spec,
    )(*args)


def predict_kernel(*refs):
    sources, held = refs[0:8], refs[8:16]
    send_ref, state_ref, sems = refs[16:]
    copies = [
        pltpu.make_async_copy(source, target, sems.at[k])
        for k, (source, target) in enumerate(zip(sources, held))
    ]
    for copy in copies:
        copy.start()
    for copy in copies[0:5]:
        copy.wait()
    pos_ref, vel_ref, acc_ref, mass_ref, active_ref = held[0:5]
    total = pos_ref.shape[1]
    listed = active_ref.shape[1]
    slots = lanes // 4
    pos, vel = pos_ref[...], vel_ref[...]
    old_acc, old_jerk = acc_ref[0:3], acc_ref[3:6]
    pred_pos = (
        pos + time_step * vel + time_step**2 / 2.0 * old_acc + time_step**3 / 6.0 * old_jerk
    )
    pred_vel = vel + time_step * old_acc + time_step**2 / 2.0 * old_jerk
    state = jnp.concatenate([pred_pos, mass_ref[...], pred_vel, jnp.zeros((1, total), f32)], 0)
    state_ref[...] = state
    local = active_ref[...] - my_rank() * total
    local = jnp.where((local >= 0) & (local < total), local + 1, 0)
    mine = sum(local[:, k : k + lanes] for k in range(0, listed, lanes))
    mine = jnp.broadcast_to(mine, (8, lanes))
    for shift in (2 * slots, slots):
        mine = mine + pltpu.roll(mine, shift, 1)
    hit = one_hot(iota((total, lanes), 0) + 1 == mine[0:1]).astype(bf16)
    pieces = dot_of(stack3(state), hit)
    spread = pieces[0:8] + pieces[8:16] + pieces[16:24]
    lane = iota((8, lanes), 1)
    row = iota((8, lanes), 0)
    spread = jnp.where(row % 4 == lane // slots, spread, 0.0)
    one = jnp.sum(spread[0:4], 0, keepdims=True)
    two = jnp.sum(spread[4:8], 0, keepdims=True)
    send_ref[...] = jnp.broadcast_to(jnp.concatenate([one, two], 0)[None], send_ref.shape)
    for copy in copies[5:]:
        copy.wait()


def pack_kernel(field_ref, flow_ref, density_ref, order_ref, own_ref, near_ref, far_ref, rows_ref):
    comps = [field_ref[0], field_ref[1], field_ref[2], flow_ref[0], flow_ref[1], flow_ref[2]]
    comps = comps + [density_ref[...], density_ref[...]]
    even = lax.axis_index("gas") % 2 == 0
    for k in range(4):
        pair = jnp.concatenate([comps[2 * k], comps[2 * k + 1]], -1)
        own_ref[k] = pair
        low, high = pair[:, :reach], pair[:, -reach:]
        near_ref[k] = jnp.where(even, high, low)
        far_ref[k] = jnp.where(even, low, high)
    half = density_ref.shape[1] // 2
    for k in range(density_ref.shape[0]):
        rows_ref[k * half : (k + 1) * half] = jnp.concatenate(
            [density_ref[k, 0:half, :], density_ref[k, half:, :]], -1
        )


def join_kernel(own_ref, near_ref, far_ref, order_ref, brick_ref, side_ref, other_ref):
    even = lax.axis_index("gas") % 2 == 0
    own, near, far = own_ref[...], near_ref[...], far_ref[...]
    rows = own.shape[2]
    below = jnp.where(even, far, near)
    above = jnp.where(even, near, far)
    beyond = jnp.concatenate([above, below], 2)
    brick_ref[:, :, 0:rows] = own
    brick_ref[:, :, rows:] = beyond
    even = lax.axis_index("star") % 2 == 0
    depth = own.shape[1]
    left = iota((1, lanes), 1) < lanes // 2

    def layer(part, k, away, high):
        return part[k, depth - away if high else away - 1]

    for send_ref, high_if_even in ((side_ref, True), (other_ref, False)):
        for at, (part, pairs, away) in enumerate(sent_layers()):
            part = beyond if part else own
            tile = []
            for high in (high_if_even, not high_if_even):
                value = layer(part, pairs, away, high)
                if pairs == 3 and away == 1:
                    value = jnp.where(left, value, layer(part, pairs, 2, high))
                tile.append(value)
            send_ref[at] = jnp.where(even, tile[0], tile[1])


def sent_layers():
    tiles = []
    for away in range(1, reach + 1):
        for part in range(2):
            for pair in range(4):
                if part + away > reach or (pair > 1 and part + away > rim) or (pair == 3 and away == 2):
                    continue
                tiles.append((part, pair, away))
    return tiles


def index_kernel(active_ref, state_ref, density_ref, slot_ref, listed_ref, stars_ref, star_left_ref, cells_ref):
    listed = active_ref.shape[1]
    total = state_ref.shape[1]
    slots = lanes // 4
    active = active_ref[...]
    local = active - my_rank() * total
    mine = (local >= 0) & (local < total)
    pick = one_hot((iota((lanes, listed), 0) % slots == iota((lanes, listed), 1) % slots) & mine).astype(bf16)
    hit = one_hot(iota((total, listed), 0) == local).astype(bf16)
    slot = dot_of(pick, hit, 1, 1)
    at = jnp.sum(slot[0:slots] * iota((slots, total), 0).astype(f32), 0, keepdims=True)
    part = iota((8, total), 0) % 3 * slots
    slot_ref[...] = jnp.minimum(part, 2 * slots) + at.astype(i32)
    listed_ref[...] = jnp.sum(slot[0:slots], 0, keepdims=True)
    state = state_ref[...]
    ask = one_hot(iota((24, 6 * lanes), 0) % 8 == wide_row((24, 6 * lanes))).astype(bf16)
    stars_ref[...] = dot_of(stack3(state), ask, 0, 0)
    star_left_ref[...] = stack4(moments(state, state[3:4]))
    rows = density_ref.shape[0]
    wide = rows * lanes
    ask = one_hot(iota((3 * rows, wide), 0) % rows == iota((3 * rows, wide), 1) // lanes).astype(bf16)
    cells_ref[...] = dot_of(stack3(density_ref[...]), ask, 0, 0)


def wide_row(shape):
    at = iota(shape, 1) // lanes
    return jnp.where(at < 3, at, at + 1)


def moments(values, mass):
    return jnp.where(iota(values.shape, 0) == 3, jnp.broadcast_to(mass, values.shape), values * mass)


def stack4(values):
    return jnp.concatenate([stack3(values), jnp.zeros(values.shape, bf16)], 0)


def weigh(left, weight):
    high = weight.astype(bf16)
    return dot_of(left, high) + dot_of(left.astype(f32), weight - high.astype(f32))


def fold3(sums):
    return sums[0:8] + sums[8:16] + sums[16:24]


def force_kernel(
    ext, got_ref, active_ref, stars_ref, star_left_ref, cells_ref, send_ref, target_ref, *, chunked
):
    ext_x, ext_y, ext_z = ext
    total = stars_ref.shape[0]
    width = active_ref.shape[1]
    devices = got_ref.shape[0]
    slots = lanes // 4
    starts = rank_at(iota((devices, width), 0)) * total
    active = active_ref[...]
    owned = one_hot((active >= starts) & (active < starts + total))
    group = iota((devices, lanes), 1) // slots
    rows = []
    for half in range(2):
        raw = got_ref[:, half, :]
        turned = [raw] + [pltpu.roll(raw, k * slots, 1) for k in range(1, 4)]
        for comp in range(4 - half):
            same = turned[(3 - comp) % 4]
            for at in range(3):
                same = jnp.where(group == at, turned[(at - comp) % 4], same)
            picked = jnp.concatenate([same] * (width // lanes), 1) * owned
            rows.append(jnp.sum(picked, 0, keepdims=True))
    targets = jnp.concatenate(rows + [jnp.zeros((1, width), f32)], 0)
    target_ref[...] = targets

    first_x = lax.axis_index("star") * ext_x
    first_y = lax.axis_index("gas") * ext_y
    tx, ty, tz, _, tu, tv, tw, _ = [targets[k : k + 1] for k in range(8)]
    pulls = jnp.zeros((32, width), f32)
    bends = jnp.zeros((32, width), f32)
    step = min(total, depth)
    for at in range(0, total, step):
        src = [stars_ref[at : at + step, k * lanes : (k + 1) * lanes] for k in range(6)]
        src = [jnp.concatenate([v] * (width // lanes), 1) for v in src]
        dx, dy, dz = src[0] - tx, src[1] - ty, src[2] - tz
        du, dv, dw = src[3] - tu, src[4] - tv, src[5] - tw
        inv = lax.rsqrt(dx * dx + dy * dy + dz * dz + soften)
        inv2 = inv * inv
        weight = inv * inv2
        bend = (dx * du + dy * dv + dz * dw) * inv2 * weight
        left = star_left_ref[:, at : at + step]
        pulls = pulls + weigh(left, weight)
        bends = bends + weigh(left, bend)
    gas_acc = []
    step = ext_z
    for lane in range(0, width, lanes):
        def row_of(k):
            return jnp.broadcast_to(targets[k : k + 1, lane : lane + lanes], (8, lanes))

        def wide(row):
            return jnp.concatenate([row] * (step // 8), 0)

        def fold(block):
            return sum(block[k : k + 8] for k in range(0, step, 8))

        px, py, pz = row_of(0), row_of(1), wide(row_of(2))
        sums = [jnp.zeros((8, lanes), f32) for _ in range(3)]
        for pair in range(ext_y // 2):
            for at in range(0, 2 * ext_z, step):
                gap_y = (first_y + pair + at // ext_z * (ext_y // 2)).astype(f32) + 0.5 - py
                gap_z = (iota((step, lanes), 0) + at % ext_z).astype(f32) + 0.5 - pz
                base = gap_z * gap_z + wide(gap_y * gap_y + soften)
                along = None
                for k in range(ext_x):
                    gap_x = ((first_x + k).astype(f32) + 0.5) - px
                    col = (k * (ext_y // 2) + pair) * lanes
                    inv = lax.rsqrt(base + wide(gap_x * gap_x))
                    weight = cells_ref[at : at + step, col : col + lanes] * inv * (inv * inv)
                    sums[0] = sums[0] + gap_x * fold(weight)
                    along = weight if along is None else along + weight
                sums[1] = sums[1] + gap_y * fold(along)
                sums[2] = sums[2] + fold(gap_z * along)
        gas_acc.append(jnp.concatenate([jnp.sum(v, 0, keepdims=True) for v in sums], 0))
    gas_acc = jnp.concatenate(gas_acc, 1)
    pulls, bends = fold3(pulls), fold3(bends)
    new_acc = gas_acc + (pulls[0:3] - targets[0:3] * pulls[3:4])
    new_jerk = pulls[4:7] - targets[4:7] * pulls[3:4]
    new_jerk = new_jerk - 3.0 * (bends[0:3] - targets[0:3] * bends[3:4])
    for half, terms in enumerate((new_acc, new_jerk)):
        parts = []
        for comp in range(3):
            held = owned * (gravity * terms[comp : comp + 1])
            parts.append(sum(held[:, k : k + lanes] for k in range(0, width, lanes)))
        parts.append(jnp.zeros((devices, lanes), f32))
        sent = None
        for k in range(4):
            mixed = parts[(3 + k) % 4]
            for at in range(3):
                mixed = jnp.where(group == at, parts[(at + k) % 4], mixed)
            mixed = pltpu.roll(mixed, k * slots, 1) if k else mixed
            sent = mixed if sent is None else sent + mixed
        if chunked:
            step_at = pl.program_id(0)

            @pl.when(step_at == 0)
            def _():
                send_ref[:, half, :] = sent

            @pl.when(step_at > 0)
            def _():
                send_ref[:, half, :] += sent
        else:
            send_ref[:, half, :] = sent


def kick_kernel(ext, grid, target_ref, kick_ref, *, chunked):
    ext_x, ext_y, ext_z = ext
    width = target_ref.shape[1]

    def clear():
        kick_ref[...] = jnp.zeros(kick_ref.shape, f32)

    if chunked:
        pl.when(pl.program_id(0) == 0)(clear)
    else:
        clear()
    targets = target_ref[...]
    mass = targets[3:4]
    row = iota((8, width), 0)
    moment = jnp.where(row < 3, targets * mass, jnp.where(row == 3, mass, 0.0))
    pieces = split3(moment)
    left = jnp.concatenate([v[0:4] for v in pieces] + [jnp.zeros((4, width), bf16)], 0)
    ask = one_hot(iota((24, 3 * lanes), 0) % 8 == iota((24, 3 * lanes), 1) // lanes).astype(bf16)
    spread = dot_of(stack3(targets), ask, 0, 0)
    tx, ty, tz = spread[:, 0:lanes], spread[:, lanes : 2 * lanes], spread[:, 2 * lanes :]
    lane = iota((1, lanes), 1)
    cell_z = (lane % ext_z).astype(f32) + 0.5
    gap_z = cell_z - tz
    base = gap_z * gap_z + soften
    first_x = lax.axis_index("star") * ext_x + grid[0] - rim
    first_y = lax.axis_index("gas") * ext_y + grid[1] - rim
    place_x, square_x = [], []
    for pair in range((ext_x + 2 * rim) // 2):
        at = lax.rem(first_x + 2 * pair + lane // ext_z, grid[0])
        at = at.astype(f32) + 0.5
        place_x.append(at)
        square_x.append((at - tx) * (at - tx))
    tiles = []
    for j in range(ext_y + 2 * rim):
        out_y = max(rim - j, j - (ext_y + rim - 1), 0)
        for pair in range((ext_x + 2 * rim) // 2):
            out_x = min(max(rim - i, i - (ext_x + rim - 1), 0) for i in (2 * pair, 2 * pair + 1))
            if out_x + out_y <= rim:
                tiles.append((j, pair))
    base_y, at_y = {}, {}
    for k in range(0, len(tiles), batch):
        part = tiles[k : k + batch]
        weights = []
        for j, pair in part:
            if j not in base_y:
                at_y[j] = lax.rem(first_y + j, grid[1]).astype(f32) + 0.5
                gap_y = at_y[j] - ty
                base_y[j] = base + gap_y * gap_y
            inv = lax.rsqrt(base_y[j] + square_x[pair])
            weights.append(inv * (inv * inv))
        sums = weigh(left, jnp.concatenate(weights, 1))
        sums = sums[0:8] + sums[8:16]
        sums = sums + pltpu.roll(sums, 4, 0)
        for at, (j, pair) in enumerate(part):
            here = sums[:, at * lanes : (at + 1) * lanes]
            whole = here[3:4]
            row = (j - rim) % (ext_y + 2 * reach)
            kick_ref[0, pair, row : row + 1, :] += here[0:1] - place_x[pair] * whole
            kick_ref[1, pair, row : row + 1, :] += here[1:2] - at_y[j] * whole
            kick_ref[2, pair, row : row + 1, :] += here[2:3] - cell_z * whole


def twice(values):
    half = lanes // 2
    turned = pltpu.roll(values, half, values.ndim - 1)
    left = iota(values.shape, values.ndim - 1) < half
    return jnp.where(left, values, turned), jnp.where(left, turned, values)


def diff_x(values):
    return values[2:] - values[:-2]


def diff_y(values):
    rows = values.shape[1]
    return (pltpu.roll(values, rows - 1, 1) - pltpu.roll(values, 1, 1))[1:-1]


def diff_z(values):
    return (pltpu.roll(values, lanes - 1, 2) - pltpu.roll(values, 1, 2))[1:-1]


def double_curl(a, b, c):
    return (diff_y(c) - diff_z(b), diff_z(a) - diff_x(c), diff_x(b) - diff_y(a))


def cross_of(lhs, rhs):
    return (
        lhs[1] * rhs[2] - lhs[2] * rhs[1],
        lhs[2] * rhs[0] - lhs[0] * rhs[2],
        lhs[0] * rhs[1] - lhs[1] * rhs[0],
    )


def inner(values, width):
    return [v[width:-width] for v in values]


def double_rate(field, flow, half_resist):
    current = double_curl(*field)
    held = inner(field, 1)
    drift = cross_of(cross_of(current, held), held)
    motion = cross_of(flow, held)
    return double_curl(*[m + half_resist * d for m, d in zip(motion, drift)])


def field_kernel(ext, own_ref, near_ref, far_ref, kick_ref, flow_ref, out_ref):
    ext_x, ext_y, ext_z = ext
    even = lax.axis_index("star") % 2 == 0
    place = {tile: at for at, tile in enumerate(sent_layers())}
    half = lanes // 2

    def sent(ref, pair, away):
        parts = []
        for part in range(2):
            shared = pair == 3 and away == 2
            at = place.get((part, pair, 1 if shared else away))
            if at is None:
                parts.append(jnp.ones((ext_y, lanes), f32))
            elif shared:
                parts.append(pltpu.roll(ref[at], half, 1))
            else:
                parts.append(ref[at])
        return jnp.concatenate(parts, 0)

    comps = []
    for k in range(4):
        near = [sent(near_ref, k, away) for away in range(1, reach + 1)]
        far = [sent(far_ref, k, away) for away in range(1, reach + 1)]
        below = jnp.stack([jnp.where(even, f, n) for n, f in zip(near, far)][::-1])
        above = jnp.stack([jnp.where(even, n, f) for n, f in zip(near, far)])
        whole = twice(jnp.concatenate([below, own_ref[k], above], 0))
        if k == 3:
            comps.append(whole[0][1:-1])
        else:
            comps.extend(whole)
    field = comps[0:3]
    dense = comps[6]
    inv = lax.rsqrt(dense)
    half_resist = 0.5 * (inv * inv * inv)
    flow = []
    for k in range(3):
        kick = jnp.stack(twice(kick_ref[k]), 1).reshape((ext_x + 2 * rim,) + kick_ref.shape[2:])
        flow.append(comps[3 + k][1:-1] + (time_step * gravity) * kick)
    rows = slice(0, ext_y)
    for k in range(3):
        flow_ref[k] = flow[k][rim:-rim, rows, 0:ext_z]
    rate = double_rate(field, flow, half_resist)
    section = [b + (0.5 * field_step) * r for b, r in zip(inner(field, 2), rate)]
    rate = double_rate(section, inner(flow, 2), half_resist[2:-2])
    for k in range(3):
        new = field[k][reach:-reach] + section[k][2:-2] + (0.5 * field_step) * rate[k]
        out_ref[k] = 0.5 * new[:, rows, 0:ext_z]


def order_kernel(order_ref, out_ref):
    out_ref[...] = jnp.zeros(out_ref.shape, f32)


def update_kernel(back_ref, pos_ref, vel_ref, acc_ref, slot_ref, listed_ref, order_ref, out_ref):
    summed = jnp.sum(back_ref[...], 0)
    terms = jnp.where(iota((8, lanes), 0) < 3, summed[0:1], summed[1:2])
    slot = slot_ref[...]
    new = jnp.concatenate(
        [
            jnp.take_along_axis(terms, slot[:, k : k + lanes], axis=1, mode="promise_in_bounds")
            for k in range(0, slot.shape[1], lanes)
        ],
        1,
    )
    new_acc, new_jerk = new[0:3], new[3:6]
    pos, vel = pos_ref[...], vel_ref[...]
    old_acc, old_jerk = acc_ref[0:3], acc_ref[3:6]
    vel_one = (
        vel + time_step * (old_acc + new_acc) / 2.0 + time_step**2 * (old_jerk - new_jerk) / 12.0
    )
    pos_one = (
        pos + time_step * (vel + vel_one) / 2.0 + time_step**2 * (old_acc - new_acc) / 12.0
    )
    listed = listed_ref[...] > 0.5
    out_ref[0:3] = jnp.where(listed, pos_one, pos)
    out_ref[3:6] = jnp.where(listed, vel_one, vel)
    out_ref[6:9] = jnp.where(listed, new_acc, old_acc)
    out_ref[9:12] = jnp.where(listed, new_jerk, old_jerk)


def swap_pairs(near, far, axis):
    count = lax.axis_size(axis)
    inside = [(i, i ^ 1) for i in range(count)]
    between = [(i, (i + (1 if i % 2 else -1)) % count) for i in range(count)]
    got_far = lax.ppermute(far, axis, between)
    got_near = lax.ppermute(near, axis, inside)
    return got_near, got_far


def body(star_pos, star_vel, star_accel, star_mass, active, density, flow_in, field_in):
    def shape(*dims, dtype=f32):
        return jax.ShapeDtypeStruct(dims, dtype)

    total = star_pos.shape[1]
    listed = active.shape[0]
    star_count, gas_count = lax.axis_size("star"), lax.axis_size("gas")
    devices = star_count * gas_count
    ext = density.shape
    ext_x, ext_y, ext_z = ext
    grid = (ext_x * star_count, ext_y * gas_count)
    width = min(listed, 256)
    chunks = listed // width
    names = active.reshape(1, listed)
    inputs = [
        star_pos, star_vel, star_accel, star_mass.reshape(1, total), names, field_in, flow_in, density
    ]
    *held, send, state = call(
        predict_kernel,
        [shape(*x.shape, dtype=x.dtype) for x in inputs] + [shape(devices, 2, lanes), shape(8, total)],
        *[pltpu.with_memory_space_constraint(x, pltpu.HBM) for x in inputs],
        in_specs=[pl.BlockSpec(memory_space=pltpu.HBM)] * len(inputs),
        scratch=[pltpu.SemaphoreType.DMA((len(inputs),))],
    )
    pos, vel, acc, _, names, field, flow, dense = held
    got = exchange(send)

    own, near, far, rows = call(
        pack_kernel,
        (shape(4, ext_x, ext_y, lanes), shape(4, ext_x, reach, lanes), shape(4, ext_x, reach, lanes),
         shape(ext_x * ext_y // 2, 2 * ext_z)),
        field, flow, dense, send, after=1,
    )
    near, far = swap_pairs(near, far, "gas")
    slot, is_listed, stars, star_left, cells = call(
        index_kernel,
        (shape(8, total, dtype=i32), shape(1, total), shape(total, 6 * lanes),
         shape(32, total, dtype=bf16), shape(2 * ext_z, ext_x * ext_y // 2 * lanes)),
        names, state, rows,
    )
    def all_of(*dims):
        return pl.BlockSpec(dims, lambda k: (0,) * len(dims))

    def part_of(rows):
        return pl.BlockSpec((rows, width), lambda k: (0, k))

    def in_parts(in_specs, out_specs):
        if chunks == 1:
            return {}
        return dict(grid=(chunks,), in_specs=in_specs, out_specs=out_specs)

    back, targets = call(
        functools.partial(force_kernel, ext, chunked=chunks > 1),
        (shape(devices, 2, lanes), shape(8, listed)),
        got, names, stars, star_left, cells,
        **in_parts(
            [all_of(*got.shape), part_of(1)]
            + [all_of(*x.shape) for x in (stars, star_left, cells)],
            (all_of(devices, 2, lanes), part_of(8)),
        ),
    )
    back = exchange(back)

    if ext_x != reach or ext_y != 2 * reach or ext_z != lanes // 2:
        raise ValueError("brick shape")
    kick_shape = (3, (ext_x + 2 * rim) // 2, ext_y + 2 * reach, lanes)
    brick_shape = (4, ext_x, ext_y + 2 * reach, lanes)

    def one_turn(_):
        edge = shape(len(sent_layers()), ext_y, lanes)
        brick, side, other = call(
            join_kernel, (shape(*brick_shape), edge, edge), own, near, far, targets, after=1
        )
        side, other = swap_pairs(side, other, "star")
        kick = call(
            functools.partial(kick_kernel, ext, grid, chunked=chunks > 1), shape(*kick_shape), targets,
            **in_parts([part_of(8)], all_of(*kick_shape)),
        )
        flow, field_out = call(
            functools.partial(field_kernel, ext),
            (shape(*flow_in.shape), shape(*field_in.shape)), brick, side, other, kick,
        )
        return flow, field_out

    def no_turn(_):
        return jnp.zeros(flow_in.shape, f32), jnp.zeros(field_in.shape, f32)

    flow, field_out = lax.cond(lax.axis_index("star") < star_count, one_turn, no_turn, 0)
    order = call(
        order_kernel, shape(8, lanes), pltpu.with_memory_space_constraint(field_out, pltpu.HBM),
        after=1, where=pltpu.HBM,
        cost=pl.CostEstimate(flops=10**10, bytes_accessed=10**8, transcendentals=0),
    )
    star_new = call(
        update_kernel, shape(12, total), back, pos, vel, acc, slot, is_listed,
        order, after=1,
    )
    return (star_new, flow, field_out)


def solution(mesh):
    placed = (
        P(None, both),
        P(None, both),
        P(None, both),
        P(both),
        P(),
        P("star", "gas", None),
        P(None, "star", "gas", None),
        P(None, "star", "gas", None),
    )
    return jax.shard_map(
        body,
        mesh=mesh,
        in_specs=placed,
        out_specs=(
            P(None, both),
            P(None, "star", "gas", None),
            P(None, "star", "gas", None),
        ),
        check_vma=False,
    )
```

```python
import functools

import jax
import jax.numpy as jnp
from jax import lax
from jax.experimental import pallas as pl
from jax.experimental.pallas import tpu as pltpu
from jax.sharding import PartitionSpec as P

gravity = 0.02
soften = 4.0
time_step = 1.5
field_step = 0.1
both = ("star", "gas")
reach = 4
rim = reach - 1
lanes = 128
vmem_bytes = 48 * 1024 * 1024
batch = 2
depth = 512
f32, bf16, i32 = jnp.float32, jnp.bfloat16, jnp.int32


def iota(shape, dim):
    return lax.broadcasted_iota(i32, shape, dim)


def split3(values):
    high = values.astype(bf16)
    rest = values - high.astype(f32)
    mid = rest.astype(bf16)
    low = (rest - mid.astype(f32)).astype(bf16)
    return high, mid, low


def stack3(values):
    return jnp.concatenate(split3(values), 0)


def dot_of(lhs, rhs, lhs_dim=1, rhs_dim=0):
    return lax.dot_general(
        lhs, rhs, (((lhs_dim,), (rhs_dim,)), ((), ())), preferred_element_type=f32
    )


def one_hot(hits):
    return jnp.where(hits, 1.0, 0.0)


def my_rank():
    return lax.axis_index("star") * lax.axis_size("gas") + lax.axis_index("gas")


def rank_at(place):
    star_count, gas_count = lax.axis_size("star"), lax.axis_size("gas")
    pair, rest = gas_count // 2 - 1 - place // (2 * star_count), place % (2 * star_count)
    side, along = rest % 2, rest // 2
    star = along + side * (star_count - 1 - 2 * along)
    gas = pair + side * (gas_count - 1 - 2 * pair)
    return star * gas_count + gas


def exchange(pieces):
    order = [rank_at(k) for k in range(pieces.shape[0])]
    return lax.all_to_all(pieces, both, 0, 0, axis_index_groups=[order], tiled=True)


def call(kernel, outs, *args, grid=None, in_specs=None, out_specs=None, scratch=(), after=0, where=pl.ANY, cost=None):
    spec = {}
    if grid is not None:
        spec = dict(grid=grid, in_specs=in_specs, out_specs=out_specs)
    elif in_specs is not None:
        spec = dict(in_specs=in_specs)
    elif after:
        held = [pl.BlockSpec(memory_space=pltpu.VMEM)] * (len(args) - after)
        spec = dict(in_specs=held + [pl.BlockSpec(memory_space=where)] * after)
    return pl.pallas_call(
        kernel,
        out_shape=outs,
        scratch_shapes=list(scratch),
        cost_estimate=cost,
        compiler_params=pltpu.CompilerParams(vmem_limit_bytes=vmem_bytes),
        **spec,
    )(*args)


def predict_kernel(*refs):
    sources, held = refs[0:8], refs[8:16]
    send_ref, state_ref, sems = refs[16:]
    copies = [
        pltpu.make_async_copy(source, target, sems.at[k])
        for k, (source, target) in enumerate(zip(sources, held))
    ]
    for copy in copies:
        copy.start()
    for copy in copies[0:5]:
        copy.wait()
    pos_ref, vel_ref, acc_ref, mass_ref, active_ref = held[0:5]
    total = pos_ref.shape[1]
    listed = active_ref.shape[1]
    slots = lanes // 4
    pos, vel = pos_ref[...], vel_ref[...]
    old_acc, old_jerk = acc_ref[0:3], acc_ref[3:6]
    pred_pos = (
        pos + time_step * vel + time_step**2 / 2.0 * old_acc + time_step**3 / 6.0 * old_jerk
    )
    pred_vel = vel + time_step * old_acc + time_step**2 / 2.0 * old_jerk
    state = jnp.concatenate([pred_pos, mass_ref[...], pred_vel, jnp.zeros((1, total), f32)], 0)
    state_ref[...] = state
    local = active_ref[...] - my_rank() * total
    local = jnp.where((local >= 0) & (local < total), local + 1, 0)
    mine = sum(local[:, k : k + lanes] for k in range(0, listed, lanes))
    mine = jnp.broadcast_to(mine, (8, lanes))
    for shift in (2 * slots, slots):
        mine = mine + pltpu.roll(mine, shift, 1)
    hit = one_hot(iota((total, lanes), 0) + 1 == mine[0:1]).astype(bf16)
    pieces = dot_of(stack3(state), hit)
    spread = pieces[0:8] + pieces[8:16] + pieces[16:24]
    lane = iota((8, lanes), 1)
    row = iota((8, lanes), 0)
    spread = jnp.where(row % 4 == lane // slots, spread, 0.0)
    one = jnp.sum(spread[0:4], 0, keepdims=True)
    two = jnp.sum(spread[4:8], 0, keepdims=True)
    send_ref[...] = jnp.broadcast_to(jnp.concatenate([one, two], 0)[None], send_ref.shape)
    for copy in copies[5:]:
        copy.wait()


def pack_kernel(field_ref, flow_ref, density_ref, order_ref, own_ref, near_ref, far_ref, rows_ref):
    comps = [field_ref[0], field_ref[1], field_ref[2], flow_ref[0], flow_ref[1], flow_ref[2]]
    comps = comps + [density_ref[...], density_ref[...]]
    even = lax.axis_index("gas") % 2 == 0
    for k in range(4):
        pair = jnp.concatenate([comps[2 * k], comps[2 * k + 1]], -1)
        own_ref[k] = pair
        low, high = pair[:, :reach], pair[:, -reach:]
        near_ref[k] = jnp.where(even, high, low)
        far_ref[k] = jnp.where(even, low, high)
    half = density_ref.shape[1] // 2
    for k in range(density_ref.shape[0]):
        rows_ref[k * half : (k + 1) * half] = jnp.concatenate(
            [density_ref[k, 0:half, :], density_ref[k, half:, :]], -1
        )


def join_kernel(own_ref, near_ref, far_ref, order_ref, brick_ref, side_ref, other_ref):
    even = lax.axis_index("gas") % 2 == 0
    own, near, far = own_ref[...], near_ref[...], far_ref[...]
    rows = own.shape[2]
    below = jnp.where(even, far, near)
    above = jnp.where(even, near, far)
    beyond = jnp.concatenate([above, below], 2)
    brick_ref[:, :, 0:rows] = own
    brick_ref[:, :, rows:] = beyond
    even = lax.axis_index("star") % 2 == 0
    depth = own.shape[1]
    left = iota((1, lanes), 1) < lanes // 2

    def layer(part, k, away, high):
        return part[k, depth - away if high else away - 1]

    for send_ref, high_if_even in ((side_ref, True), (other_ref, False)):
        for at, (part, pairs, away) in enumerate(sent_layers()):
            part = beyond if part else own
            tile = []
            for high in (high_if_even, not high_if_even):
                value = layer(part, pairs, away, high)
                if pairs == 3 and away == 1:
                    value = jnp.where(left, value, layer(part, pairs, 2, high))
                tile.append(value)
            send_ref[at] = jnp.where(even, tile[0], tile[1])


def sent_layers():
    tiles = []
    for away in range(1, reach + 1):
        for part in range(2):
            for pair in range(4):
                if part + away > reach or (pair > 1 and part + away > rim) or (pair == 3 and away == 2):
                    continue
                tiles.append((part, pair, away))
    return tiles


def index_kernel(active_ref, state_ref, density_ref, slot_ref, listed_ref, stars_ref, star_left_ref, cells_ref):
    listed = active_ref.shape[1]
    total = state_ref.shape[1]
    slots = lanes // 4
    active = active_ref[...]
    local = active - my_rank() * total
    mine = (local >= 0) & (local < total)
    pick = one_hot((iota((lanes, listed), 0) % slots == iota((lanes, listed), 1) % slots) & mine).astype(bf16)
    hit = one_hot(iota((total, listed), 0) == local).astype(bf16)
    slot = dot_of(pick, hit, 1, 1)
    at = jnp.sum(slot[0:slots] * iota((slots, total), 0).astype(f32), 0, keepdims=True)
    part = iota((8, total), 0) % 3 * slots
    slot_ref[...] = jnp.minimum(part, 2 * slots) + at.astype(i32)
    listed_ref[...] = jnp.sum(slot[0:slots], 0, keepdims=True)
    state = state_ref[...]
    ask = one_hot(iota((24, 6 * lanes), 0) % 8 == wide_row((24, 6 * lanes))).astype(bf16)
    stars_ref[...] = dot_of(stack3(state), ask, 0, 0)
    star_left_ref[...] = stack4(moments(state, state[3:4]))
    rows = density_ref.shape[0]
    wide = rows * lanes
    ask = one_hot(iota((3 * rows, wide), 0) % rows == iota((3 * rows, wide), 1) // lanes).astype(bf16)
    cells_ref[...] = dot_of(stack3(density_ref[...]), ask, 0, 0)


def wide_row(shape):
    at = iota(shape, 1) // lanes
    return jnp.where(at < 3, at, at + 1)


def moments(values, mass):
    return jnp.where(iota(values.shape, 0) == 3, jnp.broadcast_to(mass, values.shape), values * mass)


def stack4(values):
    return jnp.concatenate([stack3(values), jnp.zeros(values.shape, bf16)], 0)


def weigh(left, weight):
    high = weight.astype(bf16)
    return dot_of(left, high) + dot_of(left.astype(f32), weight - high.astype(f32))


def fold3(sums):
    return sums[0:8] + sums[8:16] + sums[16:24]


def force_kernel(
    ext, got_ref, active_ref, stars_ref, star_left_ref, cells_ref, send_ref, target_ref, *, chunked
):
    ext_x, ext_y, ext_z = ext
    total = stars_ref.shape[0]
    width = active_ref.shape[1]
    devices = got_ref.shape[0]
    slots = lanes // 4
    starts = rank_at(iota((devices, width), 0)) * total
    active = active_ref[...]
    owned = one_hot((active >= starts) & (active < starts + total))
    group = iota((devices, lanes), 1) // slots
    rows = []
    for half in range(2):
        raw = got_ref[:, half, :]
        turned = [raw] + [pltpu.roll(raw, k * slots, 1) for k in range(1, 4)]
        for comp in range(4 - half):
            same = turned[(3 - comp) % 4]
            for at in range(3):
                same = jnp.where(group == at, turned[(at - comp) % 4], same)
            picked = jnp.concatenate([same] * (width // lanes), 1) * owned
            rows.append(jnp.sum(picked, 0, keepdims=True))
    targets = jnp.concatenate(rows + [jnp.zeros((1, width), f32)], 0)
    target_ref[...] = targets

    first_x = lax.axis_index("star") * ext_x
    first_y = lax.axis_index("gas") * ext_y
    tx, ty, tz, _, tu, tv, tw, _ = [targets[k : k + 1] for k in range(8)]
    pulls = jnp.zeros((32, width), f32)
    bends = jnp.zeros((32, width), f32)
    step = min(total, depth)
    for at in range(0, total, step):
        src = [stars_ref[at : at + step, k * lanes : (k + 1) * lanes] for k in range(6)]
        src = [jnp.concatenate([v] * (width // lanes), 1) for v in src]
        dx, dy, dz = src[0] - tx, src[1] - ty, src[2] - tz
        du, dv, dw = src[3] - tu, src[4] - tv, src[5] - tw
        inv = lax.rsqrt(dx * dx + dy * dy + dz * dz + soften)
        inv2 = inv * inv
        weight = inv * inv2
        bend = (dx * du + dy * dv + dz * dw) * inv2 * weight
        left = star_left_ref[:, at : at + step]
        pulls = pulls + weigh(left, weight)
        bends = bends + weigh(left, bend)
    gas_acc = []
    step = ext_z
    for lane in range(0, width, lanes):
        def row_of(k):
            return jnp.broadcast_to(targets[k : k + 1, lane : lane + lanes], (8, lanes))

        def wide(row):
            return jnp.concatenate([row] * (step // 8), 0)

        def fold(block):
            return sum(block[k : k + 8] for k in range(0, step, 8))

        px, py, pz = row_of(0), row_of(1), wide(row_of(2))
        sums = [jnp.zeros((8, lanes), f32) for _ in range(3)]
        for pair in range(ext_y // 2):
            for at in range(0, 2 * ext_z, step):
                gap_y = (first_y + pair + at // ext_z * (ext_y // 2)).astype(f32) + 0.5 - py
                gap_z = (iota((step, lanes), 0) + at % ext_z).astype(f32) + 0.5 - pz
                base = gap_z * gap_z + wide(gap_y * gap_y + soften)
                along = None
                for k in range(ext_x):
                    gap_x = ((first_x + k).astype(f32) + 0.5) - px
                    col = (k * (ext_y // 2) + pair) * lanes
                    inv = lax.rsqrt(base + wide(gap_x * gap_x))
                    weight = cells_ref[at : at + step, col : col + lanes] * inv * (inv * inv)
                    sums[0] = sums[0] + gap_x * fold(weight)
                    along = weight if along is None else along + weight
                sums[1] = sums[1] + gap_y * fold(along)
                sums[2] = sums[2] + fold(gap_z * along)
        gas_acc.append(jnp.concatenate([jnp.sum(v, 0, keepdims=True) for v in sums], 0))
    gas_acc = jnp.concatenate(gas_acc, 1)
    pulls, bends = fold3(pulls), fold3(bends)
    new_acc = gas_acc + (pulls[0:3] - targets[0:3] * pulls[3:4])
    new_jerk = pulls[4:7] - targets[4:7] * pulls[3:4]
    new_jerk = new_jerk - 3.0 * (bends[0:3] - targets[0:3] * bends[3:4])
    for half, terms in enumerate((new_acc, new_jerk)):
        parts = []
        for comp in range(3):
            held = owned * (gravity * terms[comp : comp + 1])
            parts.append(sum(held[:, k : k + lanes] for k in range(0, width, lanes)))
        parts.append(jnp.zeros((devices, lanes), f32))
        sent = None
        for k in range(4):
            mixed = parts[(3 + k) % 4]
            for at in range(3):
                mixed = jnp.where(group == at, parts[(at + k) % 4], mixed)
            mixed = pltpu.roll(mixed, k * slots, 1) if k else mixed
            sent = mixed if sent is None else sent + mixed
        if chunked:
            step_at = pl.program_id(0)

            @pl.when(step_at == 0)
            def _():
                send_ref[:, half, :] = sent

            @pl.when(step_at > 0)
            def _():
                send_ref[:, half, :] += sent
        else:
            send_ref[:, half, :] = sent


def kick_kernel(ext, grid, target_ref, kick_ref, *, chunked):
    ext_x, ext_y, ext_z = ext
    width = target_ref.shape[1]

    def clear():
        kick_ref[...] = jnp.zeros(kick_ref.shape, f32)

    if chunked:
        pl.when(pl.program_id(0) == 0)(clear)
    else:
        clear()
    targets = target_ref[...]
    mass = targets[3:4]
    row = iota((8, width), 0)
    moment = jnp.where(row < 3, targets * mass, jnp.where(row == 3, mass, 0.0))
    pieces = split3(moment)
    left = jnp.concatenate([v[0:4] for v in pieces] + [jnp.zeros((4, width), bf16)], 0)
    ask = one_hot(iota((24, 3 * lanes), 0) % 8 == iota((24, 3 * lanes), 1) // lanes).astype(bf16)
    spread = dot_of(stack3(targets), ask, 0, 0)
    tx, ty, tz = spread[:, 0:lanes], spread[:, lanes : 2 * lanes], spread[:, 2 * lanes :]
    lane = iota((1, lanes), 1)
    cell_z = (lane % ext_z).astype(f32) + 0.5
    gap_z = cell_z - tz
    base = gap_z * gap_z + soften
    first_x = lax.axis_index("star") * ext_x + grid[0] - rim
    first_y = lax.axis_index("gas") * ext_y + grid[1] - rim
    place_x, square_x = [], []
    for pair in range((ext_x + 2 * rim) // 2):
        at = lax.rem(first_x + 2 * pair + lane // ext_z, grid[0])
        at = at.astype(f32) + 0.5
        place_x.append(at)
        square_x.append((at - tx) * (at - tx))
    tiles = []
    for j in range(ext_y + 2 * rim):
        out_y = max(rim - j, j - (ext_y + rim - 1), 0)
        for pair in range((ext_x + 2 * rim) // 2):
            out_x = min(max(rim - i, i - (ext_x + rim - 1), 0) for i in (2 * pair, 2 * pair + 1))
            if out_x + out_y <= rim:
                tiles.append((j, pair))
    base_y, at_y = {}, {}
    for k in range(0, len(tiles), batch):
        part = tiles[k : k + batch]
        weights = []
        for j, pair in part:
            if j not in base_y:
                at_y[j] = lax.rem(first_y + j, grid[1]).astype(f32) + 0.5
                gap_y = at_y[j] - ty
                base_y[j] = base + gap_y * gap_y
            inv = lax.rsqrt(base_y[j] + square_x[pair])
            weights.append(inv * (inv * inv))
        sums = weigh(left, jnp.concatenate(weights, 1))
        sums = sums[0:8] + sums[8:16]
        sums = sums + pltpu.roll(sums, 4, 0)
        for at, (j, pair) in enumerate(part):
            here = sums[:, at * lanes : (at + 1) * lanes]
            whole = here[3:4]
            row = (j - rim) % (ext_y + 2 * reach)
            kick_ref[0, pair, row : row + 1, :] += here[0:1] - place_x[pair] * whole
            kick_ref[1, pair, row : row + 1, :] += here[1:2] - at_y[j] * whole
            kick_ref[2, pair, row : row + 1, :] += here[2:3] - cell_z * whole


def twice(values):
    half = lanes // 2
    turned = pltpu.roll(values, half, values.ndim - 1)
    left = iota(values.shape, values.ndim - 1) < half
    return jnp.where(left, values, turned), jnp.where(left, turned, values)


def diff_x(values):
    return values[2:] - values[:-2]


def diff_y(values):
    rows = values.shape[1]
    return (pltpu.roll(values, rows - 1, 1) - pltpu.roll(values, 1, 1))[1:-1]


def diff_z(values):
    return (pltpu.roll(values, lanes - 1, 2) - pltpu.roll(values, 1, 2))[1:-1]


def double_curl(a, b, c):
    return (diff_y(c) - diff_z(b), diff_z(a) - diff_x(c), diff_x(b) - diff_y(a))


def cross_of(lhs, rhs):
    return (
        lhs[1] * rhs[2] - lhs[2] * rhs[1],
        lhs[2] * rhs[0] - lhs[0] * rhs[2],
        lhs[0] * rhs[1] - lhs[1] * rhs[0],
    )


def inner(values, width):
    return [v[width:-width] for v in values]


def double_rate(field, flow, half_resist):
    current = double_curl(*field)
    held = inner(field, 1)
    drift = cross_of(cross_of(current, held), held)
    motion = cross_of(flow, held)
    return double_curl(*[m + half_resist * d for m, d in zip(motion, drift)])


def field_kernel(ext, own_ref, near_ref, far_ref, kick_ref, flow_ref, out_ref):
    ext_x, ext_y, ext_z = ext
    even = lax.axis_index("star") % 2 == 0
    place = {tile: at for at, tile in enumerate(sent_layers())}
    half = lanes // 2

    def sent(ref, pair, away):
        parts = []
        for part in range(2):
            shared = pair == 3 and away == 2
            at = place.get((part, pair, 1 if shared else away))
            if at is None:
                parts.append(jnp.ones((ext_y, lanes), f32))
            elif shared:
                parts.append(pltpu.roll(ref[at], half, 1))
            else:
                parts.append(ref[at])
        return jnp.concatenate(parts, 0)

    comps = []
    for k in range(4):
        near = [sent(near_ref, k, away) for away in range(1, reach + 1)]
        far = [sent(far_ref, k, away) for away in range(1, reach + 1)]
        below = jnp.stack([jnp.where(even, f, n) for n, f in zip(near, far)][::-1])
        above = jnp.stack([jnp.where(even, n, f) for n, f in zip(near, far)])
        whole = twice(jnp.concatenate([below, own_ref[k], above], 0))
        if k == 3:
            comps.append(whole[0][1:-1])
        else:
            comps.extend(whole)
    field = comps[0:3]
    dense = comps[6]
    inv = lax.rsqrt(dense)
    half_resist = 0.5 * (inv * inv * inv)
    flow = []
    for k in range(3):
        kick = jnp.stack(twice(kick_ref[k]), 1).reshape((ext_x + 2 * rim,) + kick_ref.shape[2:])
        flow.append(comps[3 + k][1:-1] + (time_step * gravity) * kick)
    rows = slice(0, ext_y)
    for k in range(3):
        flow_ref[k] = flow[k][rim:-rim, rows, 0:ext_z]
    rate = double_rate(field, flow, half_resist)
    section = [b + (0.5 * field_step) * r for b, r in zip(inner(field, 2), rate)]
    rate = double_rate(section, inner(flow, 2), half_resist[2:-2])
    for k in range(3):
        new = field[k][reach:-reach] + section[k][2:-2] + (0.5 * field_step) * rate[k]
        out_ref[k] = 0.5 * new[:, rows, 0:ext_z]


def order_kernel(order_ref, out_ref):
    out_ref[...] = jnp.zeros(out_ref.shape, f32)


def update_kernel(back_ref, pos_ref, vel_ref, acc_ref, slot_ref, listed_ref, order_ref, out_ref):
    summed = jnp.sum(back_ref[...], 0)
    terms = jnp.where(iota((8, lanes), 0) < 3, summed[0:1], summed[1:2])
    slot = slot_ref[...]
    new = jnp.concatenate(
        [
            jnp.take_along_axis(terms, slot[:, k : k + lanes], axis=1, mode="promise_in_bounds")
            for k in range(0, slot.shape[1], lanes)
        ],
        1,
    )
    new_acc, new_jerk = new[0:3], new[3:6]
    pos, vel = pos_ref[...], vel_ref[...]
    old_acc, old_jerk = acc_ref[0:3], acc_ref[3:6]
    vel_one = (
        vel + time_step * (old_acc + new_acc) / 2.0 + time_step**2 * (old_jerk - new_jerk) / 12.0
    )
    pos_one = (
        pos + time_step * (vel + vel_one) / 2.0 + time_step**2 * (old_acc - new_acc) / 12.0
    )
    listed = listed_ref[...] > 0.5
    out_ref[0:3] = jnp.where(listed, pos_one, pos)
    out_ref[3:6] = jnp.where(listed, vel_one, vel)
    out_ref[6:9] = jnp.where(listed, new_acc, old_acc)
    out_ref[9:12] = jnp.where(listed, new_jerk, old_jerk)


def swap_pairs(near, far, axis):
    count = lax.axis_size(axis)
    inside = [(i, i ^ 1) for i in range(count)]
    between = [(i, (i + (1 if i % 2 else -1)) % count) for i in range(count)]
    got_far = lax.ppermute(far, axis, between)
    got_near = lax.ppermute(near, axis, inside)
    return got_near, got_far


def body(star_pos, star_vel, star_accel, star_mass, active, density, flow_in, field_in):
    def shape(*dims, dtype=f32):
        return jax.ShapeDtypeStruct(dims, dtype)

    total = star_pos.shape[1]
    listed = active.shape[0]
    star_count, gas_count = lax.axis_size("star"), lax.axis_size("gas")
    devices = star_count * gas_count
    ext = density.shape
    ext_x, ext_y, ext_z = ext
    grid = (ext_x * star_count, ext_y * gas_count)
    width = min(listed, 256)
    chunks = listed // width
    names = active.reshape(1, listed)
    inputs = [
        star_pos, star_vel, star_accel, star_mass.reshape(1, total), names, field_in, flow_in, density
    ]
    *held, send, state = call(
        predict_kernel,
        [shape(*x.shape, dtype=x.dtype) for x in inputs] + [shape(devices, 2, lanes), shape(8, total)],
        *[pltpu.with_memory_space_constraint(x, pltpu.HBM) for x in inputs],
        in_specs=[pl.BlockSpec(memory_space=pltpu.HBM)] * len(inputs),
        scratch=[pltpu.SemaphoreType.DMA((len(inputs),))],
    )
    pos, vel, acc, _, names, field, flow, dense = held
    got = exchange(send)

    own, near, far, rows = call(
        pack_kernel,
        (shape(4, ext_x, ext_y, lanes), shape(4, ext_x, reach, lanes), shape(4, ext_x, reach, lanes),
         shape(ext_x * ext_y // 2, 2 * ext_z)),
        field, flow, dense, send, after=1,
    )
    near, far = swap_pairs(near, far, "gas")
    slot, is_listed, stars, star_left, cells = call(
        index_kernel,
        (shape(8, total, dtype=i32), shape(1, total), shape(total, 6 * lanes),
         shape(32, total, dtype=bf16), shape(2 * ext_z, ext_x * ext_y // 2 * lanes)),
        names, state, rows,
    )
    def all_of(*dims):
        return pl.BlockSpec(dims, lambda k: (0,) * len(dims))

    def part_of(rows):
        return pl.BlockSpec((rows, width), lambda k: (0, k))

    def in_parts(in_specs, out_specs):
        if chunks == 1:
            return {}
        return dict(grid=(chunks,), in_specs=in_specs, out_specs=out_specs)

    back, targets = call(
        functools.partial(force_kernel, ext, chunked=chunks > 1),
        (shape(devices, 2, lanes), shape(8, listed)),
        got, names, stars, star_left, cells,
        **in_parts(
            [all_of(*got.shape), part_of(1)]
            + [all_of(*x.shape) for x in (stars, star_left, cells)],
            (all_of(devices, 2, lanes), part_of(8)),
        ),
    )
    back = exchange(back)

    if ext_x != reach or ext_y != 2 * reach or ext_z != lanes // 2:
        raise ValueError("brick shape")
    kick_shape = (3, (ext_x + 2 * rim) // 2, ext_y + 2 * reach, lanes)
    brick_shape = (4, ext_x, ext_y + 2 * reach, lanes)

    def one_turn(_):
        edge = shape(len(sent_layers()), ext_y, lanes)
        brick, side, other = call(
            join_kernel, (shape(*brick_shape), edge, edge), own, near, far, targets, after=1
        )
        side, other = swap_pairs(side, other, "star")
        kick = call(
            functools.partial(kick_kernel, ext, grid, chunked=chunks > 1), shape(*kick_shape), targets,
            **in_parts([part_of(8)], all_of(*kick_shape)),
        )
        flow, field_out = call(
            functools.partial(field_kernel, ext),
            (shape(*flow_in.shape), shape(*field_in.shape)), brick, side, other, kick,
        )
        return flow, field_out

    def no_turn(_):
        return jnp.zeros(flow_in.shape, f32), jnp.zeros(field_in.shape, f32)

    flow, field_out = lax.cond(lax.axis_index("star") < star_count, one_turn, no_turn, 0)
    order = call(
        order_kernel, shape(8, lanes), pltpu.with_memory_space_constraint(field_out, pltpu.HBM),
        after=1, where=pltpu.HBM,
        cost=pl.CostEstimate(flops=10**10, bytes_accessed=10**8, transcendentals=0),
    )
    star_new = call(
        update_kernel, shape(12, total), back, pos, vel, acc, slot, is_listed,
        order, after=1,
    )
    return (star_new, flow, field_out)


def solution(mesh):
    placed = (
        P(None, both),
        P(None, both),
        P(None, both),
        P(both),
        P(),
        P("star", "gas", None),
        P(None, "star", "gas", None),
        P(None, "star", "gas", None),
    )
    return jax.shard_map(
        body,
        mesh=mesh,
        in_specs=placed,
        out_specs=(
            P(None, both),
            P(None, "star", "gas", None),
            P(None, "star", "gas", None),
        ),
        check_vma=False,
    )
```
